128 devices in a mesh: replica: 16 (over x_hi, z, core), shard: 8 (over x_lo, y).
Axes of the slice: x: 4 (x_hi: 2, x_lo: 2; x = x_hi * 2 + x_lo), y: 4, z: 4, core: 2. Of those that a mesh axis runs over, the one named last changes fastest.
Arguments:
- tokens: bfloat16 [16384, 896], P(('replica', 'shard')), may hold values from -6 to 6
- segments: int32 [16384], P(('replica', 'shard')), may hold values from 0 to 2, as said below
- attn_gain: bfloat16 [896], P('shard'), may hold values from 0.25 to 1.75
- w_query: bfloat16 [896, 896], P('shard'), may hold values from -0.1875 to 0.1875
- w_key: bfloat16 [896, 128], P('shard'), may hold values from -0.1875 to 0.1875
- w_value: bfloat16 [896, 128], P('shard'), may hold values from -0.1875 to 0.1875
- w_out: bfloat16 [896, 896], P('shard'), may hold values from -2 to 2
- ffn_gain: bfloat16 [896], P('shard'), may hold values from 0.25 to 1.75
- w_gate: bfloat16 [896, 4864], P('shard'), may hold values from -0.1875 to 0.1875
- w_up: bfloat16 [896, 4864], P('shard'), may hold values from -0.1875 to 0.1875
- w_down: bfloat16 [4864, 896], P('shard'), may hold values from -0.078125 to 0.078125
- cotangent: bfloat16 [16384, 896], P(('replica', 'shard')), may hold values from -6 to 6
Outputs:
- output: bfloat16 [16384, 896], P(('replica', 'shard'))
- grad_tokens: float32 [16384, 896], P(('replica', 'shard'))
- grad_attn_gain: float32 [896], P('shard')
- grad_query: float32 [896, 896], P('shard')
- grad_key: float32 [896, 128], P('shard')
- grad_value: float32 [896, 128], P('shard')
- grad_out: float32 [896, 896], P('shard')
- grad_ffn_gain: float32 [896], P('shard')
- grad_gate: float32 [896, 4864], P('shard')
- grad_up: float32 [896, 4864], P('shard')
- grad_down: float32 [4864, 896], P('shard')
The draws below stay inside these ranges and needn't reach their ends.
Inputs may be any that keep to these rules, and one draw needn't show every extreme that they name: `segments`: in each sequence of 1024 tokens the segment numbers start at 0, never fall and take exactly the values 0, 1 and 2; segment 1 starts within the first 128 tokens of the sequence and ends within its last 128.
All inputs are finite; a program needn't handle non-finite values.
Results may differ from the reference program's by a relative error of at most 0.02.
Values may be sent and summed in bfloat16 or wider, within the bound.
A program may use at most 192 MiB of HBM per device.

```python
import math
import jax
import jax.numpy as jnp
from jax import lax

D = 896
H = 14
HD = 64
KVH = 2
FF = 4864
LENGTH = 1024
ROWS = 128
TOKENS = 16384


def draw_segments(key, part):
    key = jax.random.fold_in(key, 11)
    count = TOKENS // LENGTH
    first_key, second_key = jax.random.split(key)
    head = jax.random.randint(first_key, (count, 1), 1, ROWS, dtype=jnp.int32)
    tail = jax.random.randint(second_key, (count, 1), 1, ROWS, dtype=jnp.int32)
    place = jnp.arange(LENGTH, dtype=jnp.int32)[None, :]
    number = (place >= head).astype(jnp.int32) + (place >= LENGTH - tail).astype(jnp.int32)
    return number.reshape(TOKENS)


def steps_of(key, dims, cuts, smallest, largest):
    def one(axis_at, parts):
        steps = jax.random.uniform(jax.random.fold_in(jax.random.fold_in(key, 6), axis_at), (parts,), jnp.float32, smallest / len(cuts), largest / len(cuts))
        return jnp.repeat(jnp.exp(steps), dims[axis_at] // parts).reshape((-1,) + (1,) * (len(dims) - axis_at - 1))

    level = one(*cuts[0])
    for cut in cuts[1:]:
        level = level * one(*cut)
    return level


def normal_values(stream_key, extent, scale, bound, cuts=(), held_as=jnp.bfloat16):
    values = scale * jax.random.normal(stream_key, extent, jnp.float32)
    if cuts:
        values = values * steps_of(stream_key, extent, cuts, -0.22, 0.18)
    return jnp.clip(values, -bound, bound).astype(held_as)


def setup_inputs(seed: int = 0) -> dict:
    key_list = jax.random.split(jax.random.key(seed), 13)
    return {
        "tokens": normal_values(key_list[0], (TOKENS, D), 1.0, 6.0, ((0, 128),)),
        "segments": draw_segments(jax.random.fold_in(key_list[12], 71), 0),
        "attn_gain": jnp.clip(1.0 + 0.15 * jax.random.normal(key_list[2], (D,), jnp.float32), 0.25, 1.75).astype(jnp.bfloat16),
        "w_query": normal_values(key_list[3], (D, D), D ** -0.5, 0.1875, ((0, 8),)),
        "w_key": normal_values(key_list[4], (D, KVH * HD), D ** -0.5, 0.1875, ((0, 8),)),
        "w_value": normal_values(key_list[5], (D, KVH * HD), D ** -0.5, 0.1875, ((0, 8),)),
        "w_out": normal_values(key_list[6], (D, D), (D // 128) ** -0.5, 2.0, ((0, 8),)),
        "ffn_gain": jnp.clip(1.0 + 0.15 * jax.random.normal(key_list[7], (D,), jnp.float32), 0.25, 1.75).astype(jnp.bfloat16),
        "w_gate": normal_values(key_list[8], (D, FF), D ** -0.5, 0.1875, ((0, 8),)),
        "w_up": normal_values(key_list[9], (D, FF), D ** -0.5, 0.1875, ((0, 8),)),
        "w_down": normal_values(key_list[10], (FF, D), FF ** -0.5, 0.078125, ((0, 8),)),
        "cotangent": normal_values(key_list[11], (TOKENS, D), 1.0, 6.0, ((0, 128),)),
    }


EPS = 1e-05
THETA = 10000.0

@jax.custom_vjp
def low(v):
    return lax.optimization_barrier(v.astype(jnp.bfloat16)).astype(jnp.float32)

@jax.custom_vjp
def low_back(v):
    return v

def low_keep(v):
    return (low(v), None)

def low_pass(kept, grad):
    return (grad,)

def back_keep(v):
    return (v, None)

def back_low(kept, grad):
    return (low(grad),)
low.defvjp(low_keep, low_pass)
low_back.defvjp(back_keep, back_low)

def product(left, right):
    return jnp.dot(left, right, precision=lax.Precision.HIGHEST, preferred_element_type=jnp.float32)

def norm_rows(values, gain):
    return values * lax.rsqrt(lax.optimization_barrier(jnp.mean(values * values, axis=-1, keepdims=True)) + EPS) * gain

def positions(seq_ids):
    place = jnp.arange(seq_ids.shape[0], dtype=jnp.int32)
    earlier = lax.optimization_barrier(jnp.sum((seq_ids[None, :] < seq_ids[:, None]).astype(jnp.int32), axis=1))
    return (place - earlier).astype(jnp.int32)

def tables(position):
    half = HD // 2
    frequency = THETA ** (-(jnp.arange(half, dtype=jnp.float32) * 2.0 / HD))
    angle = position.astype(jnp.float32)[:, None] * frequency[None, :]
    return (jnp.cos(angle)[:, None, :], jnp.sin(angle)[:, None, :])

def rotate(values, cosine, sine):
    half = values.shape[-1] // 2
    first = values[..., :half]
    second = values[..., half:]
    return jnp.concatenate([first * cosine - second * sine, second * cosine + first * sine], axis=-1)

def attend(query, key_rot, value, seq_ids):
    group = H // KVH
    scale = 1.0 / math.sqrt(HD)
    grouped = query.reshape(LENGTH, KVH, group, HD)
    scores = jnp.einsum('qcgd,kcd->cgqk', grouped, key_rot, precision=lax.Precision.HIGHEST) * scale
    scores = low_back(scores)
    place = jnp.arange(LENGTH, dtype=jnp.int32)
    allowed = (seq_ids[:, None] == seq_ids[None, :]) & (place[:, None] >= place[None, :])
    scores = jnp.where(allowed[None, None], scores, -1e+30)
    highest = lax.optimization_barrier(jnp.max(scores, axis=-1, keepdims=True))
    weights = jnp.exp(scores - highest)
    probs = low(weights / lax.optimization_barrier(jnp.sum(weights, axis=-1, keepdims=True)))
    mixed = jnp.einsum('cgqk,kcd->qcgd', probs, value, precision=lax.Precision.HIGHEST)
    return mixed.reshape(LENGTH, H * HD)

def layer(tokens, attn_gain, w_query, w_key, w_value, w_out, ffn_gain, w_gate, w_up, w_down, seq_rows, cosine, sine):
    count = TOKENS // LENGTH
    normed_one = low(norm_rows(tokens, attn_gain))
    query = low_back(product(normed_one, w_query)).reshape(TOKENS, H, HD)
    key_raw = low_back(product(normed_one, w_key)).reshape(TOKENS, KVH, HD)
    value = low(low_back(product(normed_one, w_value))).reshape(count, LENGTH, KVH, HD)
    query = low(rotate(query, cosine, sine)).reshape(count, LENGTH, H, HD)
    key_rot = low(rotate(key_raw, cosine, sine)).reshape(count, LENGTH, KVH, HD)
    saved = jax.checkpoint(attend)
    mixed = lax.map(lambda item: saved(item[0], item[1], item[2], item[3]), (query, key_rot, value, seq_rows))
    mixed = low_back(low(mixed.reshape(TOKENS, H * HD)))
    branch = low_back(product(mixed, w_out))
    middle = tokens + branch
    normed_two = low(norm_rows(middle, ffn_gain))
    gate = low_back(product(normed_two, w_gate))
    up_proj = low_back(product(normed_two, w_up))
    hidden = low(jax.nn.silu(gate) * up_proj)
    return middle + product(hidden, w_down)

def reference(tokens, segments, attn_gain, w_query, w_key, w_value, w_out, ffn_gain, w_gate, w_up, w_down, cotangent):
    seq_rows = segments.reshape(TOKENS // LENGTH, LENGTH)
    position = lax.map(positions, seq_rows).reshape(TOKENS)
    cosine, sine = tables(position)
    floats = tuple((item.astype(jnp.float32) for item in (tokens, attn_gain, w_query, w_key, w_value, w_out, ffn_gain, w_gate, w_up, w_down)))

    def forward(*values):
        return layer(*values, seq_rows, cosine, sine)
    result, pullback = jax.vjp(forward, *floats)
    grads = pullback(cotangent.astype(jnp.float32))
    return (result.astype(jnp.bfloat16), grads[0], grads[1], grads[2], grads[3], grads[4], grads[5], grads[6], grads[7], grads[8], grads[9])
```

```python
import jax
import jax.numpy as jnp
from jax import lax
from jax.experimental import pallas as pl
from jax.experimental.pallas import tpu as pltpu
from jax.sharding import PartitionSpec as P

D = 896
H = 14
HD = 64
KVH = 2
GROUP = H // KVH
FF = 4864
FC = FF // 8
FH = FC // 2
ROWS = 128
LENGTH = 1024
WR = D // 8
EPS = 1e-05
THETA = 10000.0
SCALE = 0.125

F32 = jnp.float32
BF16 = jnp.bfloat16
MESH = pl.DeviceIdType.MESH


def coords():
    replica = lax.axis_index("replica")
    shard = lax.axis_index("shard")
    x = lax.div(replica, 8) * 2 + lax.div(shard, 4)
    return x, lax.rem(shard, 4), lax.rem(lax.div(replica, 2), 4), lax.rem(replica, 2)


def place(x, y, z, core):
    return (lax.div(x, 2) * 8 + z * 2 + core, lax.rem(x, 2) * 4 + y)


def wrap(value):
    return lax.rem(value + 8, 4)


def part_of(index, size, unit):
    return pl.ds(pl.multiple_of(index * size, unit), size)


def remote(src, dst, send, recv, device):
    return pltpu.make_async_remote_copy(
        src_ref=src, dst_ref=dst, send_sem=send, recv_sem=recv, device_id=device, device_id_type=MESH
    )


class Net:
    def __init__(self, ssem, rsem, peer):
        self.ssem, self.rsem, self.peer = ssem, rsem, peer
        self.ns = self.nr = 0
        self.open = []

    def sends(self, count):
        base = self.ns
        self.ns += count
        assert self.ns <= self.ssem.shape[0]
        return lambda index: self.ssem.at[base + index]

    def recvs(self, count):
        base = self.nr
        self.nr += count
        assert self.nr <= self.rsem.shape[0]
        return lambda index: self.rsem.at[base + index]

    def pair(self, count):
        return self.sends(count), self.recvs(count)

    def go(self, src, dst, send, recv, device, when=None):
        copy = remote(src, dst, send, recv, device)
        if when is None:
            copy.start()
        else:
            pl.when(when)(copy.start)
        self.open.append((copy, when))

    def landed(self, ref, recv, when=None):
        copy = remote(ref, ref, self.ssem.at[0], recv, self.peer)
        if when is None:
            copy.wait_recv()
        else:
            pl.when(when)(copy.wait_recv)

    def drain(self):
        done, self.open = self.open, []
        for copy, when in done:
            if when is None:
                copy.wait_send()
            else:
                pl.when(when)(copy.wait_send)


def signal(barrier, device):
    pl.semaphore_signal(barrier, inc=1, device_id=device, device_id_type=MESH)


def dot(left, right):
    return jnp.dot(left, right, preferred_element_type=F32)


def dot_nt(left, right):
    return lax.dot_general(left, right, (((1,), (1,)), ((), ())), preferred_element_type=F32)


SENDS = 192
RECVS = 192
LOCALS = 16


def layer_kernel(
    tokens, seg, gain_one, gain_two, freq,
    cot, wq, wk, wv, wo, wg, wu, wd,
    output, gtok, gain_o,
    attn_o, wide_o, d_o,
    misc, wqk, wvo, wvd, st, wgu, wdv, acts, da, kv, kc, vc, kt, vt, qs, mask, mixt, mid, gains, trig, lse,
    gua, own, pa, fr, dgu, dwd,
    gmt, dkv, rkv, gqk,
    rz, sz, rx, sgu, agu, wide, rxd, sdx, rzd, agd,
    xa, sa, rya, ta, rzb, sb, rza, ryb, tile, rh, aout,
    gvec, gx, gsum, gy, gz, gh,
    ssem, rsem, lsem,
):
    x, y, z, c = coords()
    xl, xh = lax.rem(x, 2), lax.div(x, 2)
    s = xl * 4 + y
    t = 2 * y + c
    core_peer = place(x, y, z, 1 - c)
    net = Net(ssem, rsem, core_peer)

    def of_sequence(k):
        other = lax.rem(s + k, 8)
        return other, place(xh * 2 + lax.div(other, 4), lax.rem(other, 4), z, c)

    def along_z(k):
        return place(x, y, wrap(z + k), c)

    def along_x(k):
        return place(wrap(x + k), y, z, c)

    rows = part_of(s, WR, 16)
    own_rows = part_of(s, ROWS, 16)
    own_tokens = part_of(t, ROWS, 16)
    core_half = part_of(c, 512, 128)

    kv[...] = jnp.zeros_like(kv)
    rkv[...] = jnp.zeros_like(rkv)

    barrier = pltpu.get_barrier_semaphore()
    for k in range(1, 4):
        signal(barrier, place(x, wrap(y + k), z, c))
        signal(barrier, along_z(k))
    for d in (1, 3):
        for k in range(4):
            signal(barrier, place(wrap(x + d), wrap(y + k), z, c))
        signal(barrier, place(wrap(x + d), y, z, 1 - c))
    signal(barrier, along_x(2))
    signal(barrier, core_peer)
    for k in range(4):

        @pl.when((k != y) | (z != y))
        def _():
            signal(barrier, place(x, k, y, c))

    local = [
        pltpu.make_async_copy(wq, wqk.at[rows, pl.ds(0, D)], lsem.at[2]),
        pltpu.make_async_copy(wk, wqk.at[rows, pl.ds(D, 128)], lsem.at[3]),
        pltpu.make_async_copy(wv, wvd.at[rows], lsem.at[4]),
        pltpu.make_async_copy(cot, acts.at[1, own_tokens], lsem.at[5]),
    ]
    own_index = 4 * c + z
    own_lanes = part_of(own_index, 128, 128)
    own_v = pltpu.make_async_copy(wv, wvo.at[rows, own_lanes], lsem.at[0])
    own_o = pltpu.make_async_copy(
        wo.at[:, part_of(jnp.maximum(own_index - 1, 0), 128, 128)], wvo.at[rows, own_lanes], lsem.at[0]
    )
    pl.when(own_index == 0)(own_v.start)
    pl.when(own_index != 0)(own_o.start)
    for copy in local:
        copy.start()
    sender = xl == lax.div(z, 2)
    own_gate = pltpu.make_async_copy(wg, wide.at[0], lsem.at[6])
    own_up = pltpu.make_async_copy(wu, wide.at[0], lsem.at[6])
    pl.when(sender & (lax.rem(z, 2) == 0))(own_gate.start)
    pl.when(sender & (lax.rem(z, 2) == 1))(own_up.start)
    own_down = pltpu.make_async_copy(wd, wdv, lsem.at[7])
    pl.when(c == xl)(own_down.start)

    misc[s] = jnp.zeros((8, 128), F32)
    misc[s, 0:1, 0:WR] = gain_one[...].astype(F32)
    misc[s, 1:2, 0:WR] = gain_two[...].astype(F32)
    misc[s, 2:3, :] = seg[...].astype(F32)

    pl.semaphore_wait(barrier, 22 - jnp.where(z == y, 1, 0))

    ms, mr = net.pair(7)
    for k in range(1, 8):
        net.go(misc.at[s], misc.at[s], ms(k - 1), mr(k - 1), of_sequence(k)[1])

    pl.when(own_index == 0)(own_v.wait)
    pl.when(own_index != 0)(own_o.wait)
    os_, or_ = net.pair(7)
    for k in range(1, 8):
        part = wvo.at[rows, own_lanes]
        net.go(part, part, os_(k - 1), or_(k - 1), of_sequence(k)[1])

    local[0].wait()
    local[1].wait()
    qs_s, qs_r = net.pair(11)
    for k in range(1, 4):
        part = wqk.at[rows, core_half]
        net.go(part, part, qs_s(k - 1), qs_r(k - 1), place(x, wrap(y + k), z, c))
    for k in range(4):
        for d in range(2):
            part = wqk.at[rows, part_of(2 * c + d, 256, 128)]
            i = 3 + 2 * k + d
            net.go(part, part, qs_s(i), qs_r(i), place(wrap(x + 1 - 2 * d), wrap(y + k), z, c))
    local[2].wait()
    vs_s, vs_r = net.pair(7)
    for k in range(1, 8):
        net.go(wvd.at[rows], wvd.at[rows], vs_s(k - 1), vs_r(k - 1), of_sequence(k)[1])

    pl.when(sender & (lax.rem(z, 2) == 0))(own_gate.wait)
    pl.when(sender & (lax.rem(z, 2) == 1))(own_up.wait)

    @pl.when(sender)
    def _():
        for k in range(8):
            st[k] = wide[0, :, FC * k : FC * (k + 1)]

    matrix = lax.rem(z, 2)
    gs, gr = net.pair(8)
    for d in range(2):
        for k in range(4):
            if d == 0 and k == 0:
                continue
            target = place(xh * 2 + lax.rem(xl + d, 2), wrap(y + k), z, c)
            block = st.at[4 * c + wrap(y + k)]
            net.go(block, wgu.at[matrix, rows], gs(4 * d + k), gr(4 * d + k), target, when=sender)

    @pl.when(sender)
    def _():
        wgu[matrix, rows] = st[4 * c + y]

    tok = tokens[...].astype(F32)
    unit = tok * lax.rsqrt(jnp.mean(tok * tok, axis=-1, keepdims=True) + EPS)

    for k in range(1, 8):
        net.landed(misc.at[0], mr(k - 1))
    for k in range(8):
        gains[0:8, WR * k : WR * (k + 1)] = misc[k, 0:8, 0:WR]
    numbers = misc[:, 2, :]
    zeros = jnp.sum(jnp.where(numbers < 0.5, 1.0, 0.0), keepdims=True)
    ones = jnp.sum(jnp.where((numbers > 0.5) & (numbers < 1.5), 1.0, 0.0), keepdims=True)
    own_numbers = misc[s, 2:3, :]
    begin = jnp.where(own_numbers < 0.5, 0.0, jnp.where(own_numbers < 1.5, zeros, zeros + ones))
    lane = lax.broadcasted_iota(jnp.int32, (1, ROWS), 1) + s * ROWS
    angle = freq[...] * (lane.astype(F32) - begin)
    trig[0] = jnp.cos(angle)
    trig[1] = jnp.sin(angle)
    key_place = lax.broadcasted_iota(jnp.int32, (LENGTH, ROWS), 0)
    allowed = (key_place >= begin.astype(jnp.int32)) & (key_place <= lane)
    mask[...] = jnp.where(allowed, 0.0, -1e30)
    normed = (unit * gains[0:1, :]).astype(BF16)
    normed_t = jnp.transpose(normed)

    for k in range(1, 8):
        net.landed(wvo.at[rows, own_lanes], or_(k - 1))
    oz_s, oz_r = net.pair(3)
    for k in range(1, 4):
        part = wvo.at[:, own_lanes]
        net.go(part, part, oz_s(k - 1), oz_r(k - 1), along_z(k))

    qf_s, qf_r = net.pair(11)
    for i in range(11):
        if i < 3:
            part = wqk.at[part_of(xl * 4 + wrap(y - (i + 1)), WR, 16), core_half]
        else:
            k, d = divmod(i - 3, 2)
            part = wqk.at[part_of((1 - xl) * 4 + wrap(y - k), WR, 16), part_of(2 * c + d, 256, 128)]
        net.landed(part, qs_r(i))
        net.go(part, part, qf_s(i), qf_r(i), core_peer)
    for i in range(11):
        part = wqk.at[rows, pl.ds(0, 512 if i < 3 else 256)]
        net.landed(part, qf_r(i))
    raw = jnp.transpose(dot(normed, wqk[...]))
    cosine, sine = trig[0], trig[1]

    def rotated(head):
        first = raw[HD * head : HD * head + 32]
        second = raw[HD * head + 32 : HD * head + 64]
        return first * cosine - second * sine, second * cosine + first * sine

    keys = jnp.concatenate([*rotated(H), *rotated(H + 1)], axis=0)
    kv[own_rows, 0:128] = jnp.transpose(keys).astype(BF16)
    for k in range(1, 8):
        net.landed(wvd.at[rows], vs_r(k - 1))
    kv[own_rows, 128:256] = dot(normed, wvd[...]).astype(BF16)

    ks, kr = net.pair(7)
    for k in range(1, 8):
        net.go(kv.at[own_rows], kv.at[own_rows], ks(k - 1), kr(k - 1), of_sequence(k)[1], when=s + k < 8)

    ds_, dr = net.sends(1), net.recvs(2)
    half = part_of(c, FH, 16)
    net.go(wd.at[half], wdv.at[half], ds_(0), dr(c), place(wrap(x + 1 - 2 * c), y, z, xl))

    def gather_tokens(which):
        ts, tr = net.pair(3)
        part = acts.at[which, own_tokens]
        for k in range(1, 4):
            net.go(part, part, ts(k - 1), tr(k - 1), place(x, wrap(y + k), z, c))
        return tr

    local[3].wait()
    cot_r = gather_tokens(1)

    for head in range(H):
        kv_head, j = divmod(head, GROUP)
        first, second = rotated(head)
        qs[kv_head, 0:32, ROWS * j : ROWS * (j + 1)] = (first * SCALE).astype(BF16)
        qs[kv_head, 32:64, ROWS * j : ROWS * (j + 1)] = (second * SCALE).astype(BF16)

    is_far = jnp.where(sender, 0, 1)
    for k in range(4):
        if k == 0:
            net.landed(wgu.at[0, rows], gr(4), when=jnp.logical_not(sender))
        else:
            net.landed(wgu.at[0, rows], gr(4 * is_far + k))
    gz_s, gz_r = net.pair(3)
    for k in range(1, 4):
        part = wgu.at[matrix, part_of(lax.div(z, 2), 4 * WR, 16)]
        net.go(part, part, gz_s(k - 1), gz_r(k - 1), along_z(k))

    for k in range(1, 8):
        net.landed(kv.at[own_rows], kr(k - 1), when=s - k >= 0)
    for head in range(KVH):
        keys = kv[:, HD * head : HD * (head + 1)]
        values = kv[:, 128 + HD * head : 128 + HD * (head + 1)]
        kc[head] = keys
        vc[head] = values
        kt[head] = jnp.transpose(keys)
        vt[head] = jnp.transpose(values)

    @pl.loop(0, GROUP)
    def _(j):
        lanes = part_of(j, ROWS, 128)
        for head in range(KVH):
            scores = dot(kc[head], qs[head, :, lanes]) + mask[...]
            highest = jnp.max(scores, axis=0, keepdims=True)
            weights = jnp.exp(scores - highest)
            total = jnp.sum(weights, axis=0, keepdims=True)
            probs = (weights * (1.0 / total)).astype(BF16)
            lse[GROUP * head + j] = jnp.broadcast_to(highest + jnp.log(total), (8, ROWS))
            mixt[part_of(GROUP * head + j, HD, HD)] = dot(vt[head], probs)

    of_s, of_r = net.pair(4)
    for k in range(4):
        part = wvo.at[:, part_of(4 * c + wrap(z - k), 128, 128)]
        if k:
            net.landed(part, oz_r(k - 1))
        net.go(part, part, of_s(k), of_r(k), core_peer)
    for k in range(4):
        net.landed(wvo.at[:, own_lanes], of_r(k))

    attended_t = mixt[...].astype(BF16)
    attended = jnp.transpose(mixt[...]).astype(BF16)
    middle = tokens[...].astype(F32) + dot(attended, wvo[:, 128:1024])
    mid[...] = middle
    factor = lax.rsqrt(jnp.mean(middle * middle, axis=-1, keepdims=True) + EPS)
    acts[0, own_tokens] = (middle * factor * gains[1:2, :]).astype(BF16)

    n2_r = gather_tokens(0)

    def forward_tokens(which, recv):
        fs, fr_ = net.pair(4)
        for k in range(4):
            part = acts.at[which, part_of(2 * wrap(y - k) + c, ROWS, 16)]
            if k:
                net.landed(part, recv(k - 1))
            net.go(part, part, fs(k), fr_(k), core_peer)
        return fr_

    cot_f = forward_tokens(1, cot_r)
    pl.when(c == xl)(own_down.wait)
    for i in range(2):
        net.landed(wdv.at[pl.ds(FH * i, FH)], dr(i), when=c != xl)
    n2_f = forward_tokens(0, n2_r)
    for k in range(4):
        net.landed(acts.at[1, own_tokens], cot_f(k))
        net.landed(acts.at[0, own_tokens], n2_f(k))
    for k in range(1, 4):
        net.landed(wgu.at[0, pl.ds(0, 4 * WR)], gz_r(k - 1))

    xsend, xrecv = net.pair(4)
    psend, precv = net.sends(8), net.recvs(8)

    def offset(k):
        return 2 - k + 3 * lax.div(k, 2) - 2 * lax.div(k, 3)

    def exchange(off):
        block = part_of(off, 256, 256)
        return remote(pa.at[0, block], pa.at[1, block], xsend(off), xrecv(off), core_peer)

    def part_copy(off, core):
        return remote(
            pa.at[0, part_of(2 * off + core, ROWS, ROWS)], fr.at[c, off], psend(2 * off + core), precv(4 * c + off),
            place(x, wrap(y - off), z, core),
        )

    def add_cores(off):
        exchange(off).wait()
        block = part_of(off, 256, 256)
        pa[0, block] = (own[lax.rem(off, 2)] + pa[1, block].astype(F32)).astype(BF16)

    def feed_forward(k):
        off = offset(k)
        block = part_of(wrap(y - off), 256, 256)
        normed_two = acts[0, block]
        cotangent = acts[1, block]
        gate = dot(normed_two, wgu[0])
        up = dot(normed_two, wgu[1])
        grad_hidden = dot_nt(cotangent, wdv[...])
        opening = 1.0 / (1.0 + jnp.exp(-gate))
        act = gate * opening
        hidden = (act * up).astype(BF16)
        grad_gate = (grad_hidden * up * opening * (1.0 + gate * (1.0 - opening))).astype(BF16)
        grad_up = (grad_hidden * act).astype(BF16)
        gua[0, block] = grad_gate
        gua[1, block] = grad_up
        da[1, 0:FC, block] = jnp.transpose(hidden)
        da[0, :, block] = jnp.transpose(normed_two)
        out_part = dot(hidden, wdv[...])
        grad_part = dot_nt(grad_gate, wgu[0]) + dot_nt(grad_up, wgu[1])
        return off, out_part, grad_part

    @pl.loop(0, 4)
    def _(k):
        off, out_part, grad_part = feed_forward(k)

        @pl.when(k >= 1)
        def _():
            before = offset(k - 1)
            add_cores(before)
            for core in range(2):
                part_copy(before, core).start()

        own[lax.rem(off, 2)] = jnp.where(c == 0, out_part, grad_part)
        pa[0, part_of(off, 256, 256)] = jnp.where(c == 0, grad_part, out_part).astype(BF16)
        exchange(off).start()

    net.drain()

    for matrix_ in range(2):

        @pl.loop(0, 8)
        def _(i):
            block = dot(da[0, part_of(i, WR, 16)], gua[matrix_]).astype(BF16)
            dgu[2 * matrix_ + lax.div(i, 4), lax.rem(i, 4)] = block

    add_cores(0)
    for core in range(2):

        @pl.when(c == core)
        def _():
            fr[core, 0] = pa[0, ROWS * core : ROWS * (core + 1)]

        pl.when(c != core)(part_copy(0, core).start)

    zs, zr = net.pair(3)
    for k in range(1, 4):
        net.go(dgu.at[:, wrap(z + k)], rz.at[k - 1], zs(k - 1), zr(k - 1), along_z(k))

    for h in range(2):
        tall = dot(da[1, FH * h : FH * (h + 1)], acts[1]).astype(BF16)
        for i in range(7):
            q = 7 * h + i
            dwd[q // 4, q % 4] = tall[:, 128 * i : 128 * (i + 1)]
    for q in (14, 15):
        dwd[q // 4, q % 4] = jnp.zeros((FH, 128), BF16)
    xds, xdr = net.pair(3)
    for k in range(1, 4):
        net.go(dwd.at[wrap(x + k)], rxd.at[k - 1], xds(k - 1), xdr(k - 1), along_x(k))

    for kind in range(2):
        for off in range(4):
            net.landed(fr.at[kind, off], precv(4 * kind + off), when=None if off else c != kind)
    middle = mid[...]
    total = fr[0, 0].astype(F32)
    grad_normed = fr[1, 0].astype(F32)
    for off in range(1, 4):
        total = total + fr[0, off].astype(F32)
        grad_normed = grad_normed + fr[1, off].astype(F32)
    output[...] = (middle + total).astype(BF16)
    factor = lax.rsqrt(jnp.mean(middle * middle, axis=-1, keepdims=True) + EPS)
    unit_two = middle * factor
    scaled = grad_normed * gains[1:2, :]
    gvec[...] = jnp.broadcast_to(jnp.sum(grad_normed * unit_two, axis=0, keepdims=True), (8, D))
    grad_middle = acts[1, own_tokens].astype(F32) + factor * (
        scaled - unit_two * jnp.mean(scaled * unit_two, axis=-1, keepdims=True)
    )
    mid[...] = grad_middle

    branch = grad_middle.astype(BF16)
    grad_mixed = jnp.transpose(dot_nt(branch, wvo[:, 128:1024]))
    for head in range(H):
        kv_head, j = divmod(head, GROUP)
        gmt[kv_head, :, ROWS * j : ROWS * (j + 1)] = grad_mixed[HD * head : HD * (head + 1)].astype(BF16)
    da[1, :, 128:1024] = dot(attended_t, branch).astype(BF16)

    for off in range(4):
        for core in range(2):
            if off:
                part_copy(off, core).wait_send()
            else:
                pl.when(c != core)(part_copy(off, core).wait_send)
    @pl.loop(0, GROUP)
    def _(j):
        lanes = part_of(j, ROWS, 128)
        for head in range(KVH):
            row = GROUP * head + j
            scores = dot(kc[head], qs[head, :, lanes]) + mask[...]
            probs = jnp.exp(scores - lse[row, 0:1, :])
            grad_probs = dot(vc[head], gmt[head, :, lanes])
            delta = jnp.sum(grad_probs * probs, axis=0, keepdims=True)
            grad_scores = (probs * (grad_probs - delta)).astype(BF16)
            acts[head, :, lanes] = grad_scores
            pa[head, :, lanes] = probs.astype(BF16)
            rot = dot(kt[head], grad_scores) * SCALE
            cosine, sine = trig[0], trig[1]
            mixt[pl.ds(pl.multiple_of(HD * row, 32), 32)] = rot[0:32] * cosine + rot[32:64] * sine
            mixt[pl.ds(pl.multiple_of(HD * row + 32, 32), 32)] = rot[32:64] * cosine - rot[0:32] * sine

    for head in range(KVH):
        dkv[:, HD * head : HD * (head + 1)] = dot_nt(acts[head], qs[head]).astype(BF16)
        dkv[:, 128 + HD * head : 128 + HD * (head + 1)] = dot_nt(pa[head], gmt[head]).astype(BF16)

    kvs, kvr = net.pair(7)
    for k in range(1, 8):
        other, target = of_sequence(k)
        net.go(dkv.at[part_of(other, ROWS, 16)], rkv.at[k - 1], kvs(k - 1), kvr(k - 1), target, when=s + k >= 8)
    gqk[:, 0:D] = jnp.transpose(mixt[...]).astype(BF16)

    for k in range(1, 4):
        net.landed(rxd.at[k - 1], xdr(k - 1))
    sdx[...] = (
        dwd[x].astype(F32) + rxd[0].astype(F32) + rxd[1].astype(F32) + rxd[2].astype(F32)
    ).astype(BF16)
    zds, zdr = net.pair(3)
    for k in range(1, 4):
        net.go(sdx.at[wrap(z + k)], rzd.at[k - 1], zds(k - 1), zdr(k - 1), along_z(k))

    total = dkv[own_rows].astype(F32)
    for k in range(1, 8):
        net.landed(rkv.at[k - 1], kvr(k - 1), when=k > s)
        total = total + rkv[k - 1].astype(F32)
    keys = jnp.transpose(total[:, 0:128])
    cosine, sine = trig[0], trig[1]
    back = []
    for head in range(KVH):
        first = keys[HD * head : HD * head + 32]
        second = keys[HD * head + 32 : HD * head + 64]
        back += [first * cosine + second * sine, second * cosine - first * sine]
    gqk[:, D:1024] = jnp.transpose(jnp.concatenate(back, axis=0)).astype(BF16)
    grad_value = total[:, 128:256].astype(BF16)

    da[0] = dot(normed_t, gqk[...]).astype(BF16)
    da[1, :, 0:128] = dot(normed_t, grad_value).astype(BF16)
    xas, xar = net.pair(3)
    for i in range(2):
        net.go(da.at[i, :, part_of(1 - c, 512, 128)], xa.at[i], xas(i), xar(i), core_peer)

    grad_normed = dot_nt(gqk[...], wqk[...]) + dot_nt(grad_value, wvd[...])
    tok = tokens[...].astype(F32)
    factor = lax.rsqrt(jnp.mean(tok * tok, axis=-1, keepdims=True) + EPS)
    unit = tok * factor
    scaled = grad_normed * gains[0:1, :]
    gtok[...] = mid[...] + factor * (scaled - unit * jnp.mean(scaled * unit, axis=-1, keepdims=True))
    gvec[0:1, :] = jnp.sum(grad_normed * unit, axis=0, keepdims=True)
    net.go(gvec, gx, xas(2), xar(2), core_peer)

    net.landed(xa.at[0], xar(0))
    sa[0] = (da[0, :, core_half].astype(F32) + xa[0].astype(F32)).astype(BF16)
    yas, yar = net.pair(11)
    for k in range(1, 4):
        other = xl * 4 + wrap(y + k)
        net.go(
            sa.at[0, part_of(other, WR, 16)], rya.at[0, k - 1], yas(k - 1), yar(k - 1), place(x, wrap(y + k), z, c)
        )
    for k in range(4):
        for d in range(2):
            other = (1 - xl) * 4 + wrap(y + k)
            lanes = pl.ds(256 * d, 256)
            net.go(
                sa.at[0, part_of(other, WR, 16), lanes], rya.at[1, k, :, lanes], yas(3 + 2 * k + d), yar(3 + 2 * k + d),
                place(wrap(x + 1 - 2 * d), wrap(y + k), z, c),
            )
    net.landed(xa.at[1], xar(1))
    sa[1] = (da[1, :, core_half].astype(F32) + xa[1].astype(F32)).astype(BF16)
    zbs, zbr = net.pair(3)
    for k in range(1, 4):
        net.go(sa.at[1, :, part_of(wrap(z + k), 128, 128)], rzb.at[k - 1], zbs(k - 1), zbr(k - 1), along_z(k))
    net.landed(gx, xar(2))
    gsum[...] = gvec[...] + gx[...]
    gys, gyr = net.pair(7)
    for k in range(1, 8):
        net.go(gsum, gy.at[k - 1], gys(k - 1), gyr(k - 1), of_sequence(k)[1])

    for k in range(1, 4):
        net.landed(rz.at[k - 1], zr(k - 1))
    for i in range(4):
        sz[lax.div(i, 2), lax.rem(i, 2)] = (
            dgu[i, z].astype(F32) + rz[0, i].astype(F32) + rz[1, i].astype(F32) + rz[2, i].astype(F32)
        ).astype(BF16)
    xs_s, xs_r = net.pair(3)
    for k in range(1, 4):
        net.go(sz.at[:, lax.rem(xl + k, 2)], rx.at[k - 1], xs_s(k - 1), xs_r(k - 1), along_x(k))

    for k in range(1, 4):
        net.landed(rzd.at[k - 1], zdr(k - 1))
    agd[x, z] = (
        sdx[z].astype(F32) + rzd[0].astype(F32) + rzd[1].astype(F32) + rzd[2].astype(F32)
    ).astype(BF16)
    zas, zar = net.pair(3)
    for k in range(1, 4):
        net.go(agd.at[x, z], agd.at[x, z], zas(k - 1), zar(k - 1), along_z(k))

    for k in range(1, 4):
        net.landed(rya.at[0, k - 1], yar(k - 1))
    for k in range(4):
        for d in range(2):
            net.landed(rya.at[1, k, :, pl.ds(256 * d, 256)], yar(3 + 2 * k + d))
    total = sa[0, rows].astype(F32)
    for k in range(3):
        total = total + rya[0, k].astype(F32)
    for k in range(4):
        total = total + rya[1, k].astype(F32)
    ta[...] = total.astype(BF16)
    zas2, zar2 = net.pair(3)
    for k in range(1, 4):
        net.go(ta.at[:, part_of(wrap(z + k), 128, 128)], rza.at[k - 1], zas2(k - 1), zar2(k - 1), along_z(k))

    for k in range(1, 4):
        net.landed(rzb.at[k - 1], zbr(k - 1))
    sb[...] = (
        sa[1, :, part_of(z, 128, 128)].astype(F32)
        + rzb[0].astype(F32) + rzb[1].astype(F32) + rzb[2].astype(F32)
    ).astype(BF16)
    ybs, ybr = net.pair(7)
    for k in range(1, 8):
        other, target = of_sequence(k)
        net.go(sb.at[part_of(other, WR, 16)], ryb.at[k - 1], ybs(k - 1), ybr(k - 1), target)
    total = gsum[...]
    for k in range(1, 8):
        net.landed(gy.at[k - 1], gyr(k - 1))
        total = total + gy[k - 1]
    gz[3] = total
    gzs, gzr = net.pair(3)
    for k in range(1, 4):
        net.go(gz.at[3], gz.at[k - 1], gzs(k - 1), gzr(k - 1), along_z(k))

    for k in range(1, 4):
        net.landed(rza.at[k - 1], zar2(k - 1))
    tile[0] = (
        ta[:, part_of(z, 128, 128)].astype(F32)
        + rza[0].astype(F32) + rza[1].astype(F32) + rza[2].astype(F32)
    ).astype(BF16)
    total = sb[rows].astype(F32)
    for k in range(1, 8):
        net.landed(ryb.at[k - 1], ybr(k - 1))
        total = total + ryb[k - 1].astype(F32)
    tile[1] = total.astype(BF16)
    total = gz[3]
    for k in range(1, 4):
        net.landed(gz.at[k - 1], gzr(k - 1))
        total = total + gz[k - 1]
    gh[1] = total
    hs, hr = net.pair(2)
    net.go(tile, rh, hs(0), hr(0), along_x(2))
    net.go(gh.at[1], gh.at[0], hs(1), hr(1), along_x(2))

    for k in range(1, 4):
        net.landed(rx.at[k - 1], xs_r(k - 1))
    own_block = 4 * c + y
    sgu[...] = (
        sz[:, xl].astype(F32) + rx[0].astype(F32) + rx[1].astype(F32) + rx[2].astype(F32)
    ).astype(BF16)

    net.landed(rh, hr(0))
    own_tile = aout.at[:, :, own_lanes]
    aout[:, :, own_lanes] = (tile[...].astype(F32) + rh[...].astype(F32)).astype(BF16)
    lasts, lastr = net.pair(3)
    for k in range(1, 4):
        net.go(own_tile, own_tile, lasts(k - 1), lastr(k - 1), along_z(k))

    ags, agr = net.sends(4), net.recvs(4)
    for k in range(4):
        net.go(
            sgu, agu.at[own_block], ags(k), agr(y), place(x, z, wrap(z + k), c), when=None if k else z != y
        )

    @pl.when(z == y)
    def _():
        agu[own_block] = sgu[...]

    for k in range(1, 4):
        net.landed(agd.at[x, z], zar(k - 1))
    dxs, dxr = net.pair(3)
    for k in range(1, 4):
        net.go(
            agd.at[x], agd.at[x], dxs(k - 1), dxr(k - 1), along_x(k), when=lax.rem(xl + k, 2) == c
        )
    for k in range(1, 4):
        net.landed(agd.at[x], dxr(k - 1), when=xl == c)
    dfs, dfr = net.pair(1)
    net.go(agd, d_o, dfs(0), dfr(0), core_peer, when=xl == c)
    own_sums = pltpu.make_async_copy(agd, d_o, lsem.at[8])
    pl.when(xl == c)(own_sums.start)

    net.landed(gh.at[0], hr(1))
    gain_o[...] = gh[0] + gh[1]

    for k in range(1, 4):
        net.landed(own_tile, lastr(k - 1))
    fs, fr_ = net.pair(2)
    part = aout.at[:, :, core_half]
    net.go(part, part, fs(0), fr_(0), core_peer)

    for k in range(4):
        net.landed(agu.at[0], agr(k), when=(z != y) | (y != k))
    part = agu.at[pl.ds(4 * c, 4)]
    net.go(part, part, fs(1), fr_(1), core_peer)

    net.landed(d_o, dfr(0), when=xl != c)
    outs = [
        pltpu.make_async_copy(aout, attn_o, lsem.at[9]),
        pltpu.make_async_copy(wide, wide_o, lsem.at[10]),
    ]
    net.landed(aout.at[:, :, pl.ds(0, 512)], fr_(0))
    outs[0].start()
    net.landed(agu.at[pl.ds(0, 4)], fr_(1))
    for k in range(8):
        for matrix_ in range(2):
            wide[matrix_, :, FC * k : FC * (k + 1)] = agu[k, matrix_]
    outs[1].start()

    net.drain()
    for copy in outs:
        copy.wait()
    pl.when(xl == c)(own_sums.wait)


def finish_kernel(out_in, tok_in, gain_in, attn, wide, down, out, tok, gain, gq, gk, gv, go, gate, up, gdown):
    out[...] = out_in[...]
    tok[...] = tok_in[...]
    gain[...] = gain_in[...]
    gq[...] = attn[0, :, 0:D].astype(F32)
    gk[...] = attn[0, :, D:1024].astype(F32)
    gv[...] = attn[1, :, 0:128].astype(F32)
    go[...] = attn[1, :, 128:1024].astype(F32)
    gate[...] = wide[0].astype(F32)
    up[...] = wide[1].astype(F32)
    for q in range(14):
        h, i = divmod(q, 7)
        gdown[FH * h : FH * (h + 1), 128 * i : 128 * (i + 1)] = down[q // 4, q % 4].astype(F32)


def vmem():
    return pl.BlockSpec(memory_space=pltpu.VMEM)


def anywhere():
    return pl.BlockSpec(memory_space=pl.ANY)


def shape(dims, dtype):
    return jax.ShapeDtypeStruct(dims, dtype)


def body(
    tokens, segments, attn_gain, w_query, w_key, w_value, w_out, ffn_gain, w_gate, w_up, w_down, cotangent
):
    half = HD // 2
    frequency = THETA ** (-(jnp.arange(half, dtype=F32) * 2.0 / HD))
    freq = jnp.broadcast_to(frequency[:, None], (half, ROWS))
    layer = pl.pallas_call(
        layer_kernel,
        name="layer",
        out_shape=[
            shape((ROWS, D), BF16),
            shape((ROWS, D), F32),
            shape((8, D), F32),
            shape((2, WR, 1024), BF16),
            shape((2, WR, FF), BF16),
            shape((4, 4, FH, 128), BF16),
        ],
        in_specs=[vmem()] * 5 + [anywhere()] * 8,
        out_specs=[vmem()] * 3 + [anywhere()] * 3,
        scratch_shapes=[
            pltpu.VMEM((8, 8, 128), F32),
            pltpu.VMEM((D, 1024), BF16),
            pltpu.VMEM((D, 1024), BF16),
            pltpu.VMEM((D, 128), BF16),
            pltpu.VMEM((8, WR, FC), BF16),
            pltpu.VMEM((2, D, FC), BF16),
            pltpu.VMEM((FC, D), BF16),
            pltpu.VMEM((2, LENGTH, D), BF16),
            pltpu.VMEM((2, D, LENGTH), BF16),
            pltpu.VMEM((LENGTH, 256), BF16),
            pltpu.VMEM((KVH, LENGTH, HD), BF16),
            pltpu.VMEM((KVH, LENGTH, HD), BF16),
            pltpu.VMEM((KVH, HD, LENGTH), BF16),
            pltpu.VMEM((KVH, HD, LENGTH), BF16),
            pltpu.VMEM((KVH, HD, D), BF16),
            pltpu.VMEM((LENGTH, ROWS), F32),
            pltpu.VMEM((D, ROWS), F32),
            pltpu.VMEM((ROWS, D), F32),
            pltpu.VMEM((8, D), F32),
            pltpu.VMEM((2, half, ROWS), F32),
            pltpu.VMEM((H, 8, ROWS), F32),
            pltpu.VMEM((2, LENGTH, FC), BF16),
            pltpu.VMEM((2, 256, D), F32),
            pltpu.VMEM((2, LENGTH, D), BF16),
            pltpu.VMEM((2, 4, ROWS, D), BF16),
            pltpu.VMEM((4, 4, WR, FC), BF16),
            pltpu.VMEM((4, 4, FH, 128), BF16),
            pltpu.VMEM((KVH, HD, D), BF16),
            pltpu.VMEM((LENGTH, 256), BF16),
            pltpu.VMEM((7, ROWS, 256), BF16),
            pltpu.VMEM((ROWS, 1024), BF16),
            pltpu.VMEM((3, 4, WR, FC), BF16),
            pltpu.VMEM((2, 2, WR, FC), BF16),
            pltpu.VMEM((3, 2, WR, FC), BF16),
            pltpu.VMEM((2, WR, FC), BF16),
            pltpu.VMEM((8, 2, WR, FC), BF16),
            pltpu.VMEM((2, WR, FF), BF16),
            pltpu.VMEM((3, 4, FH, 128), BF16),
            pltpu.VMEM((4, FH, 128), BF16),
            pltpu.VMEM((3, FH, 128), BF16),
            pltpu.VMEM((4, 4, FH, 128), BF16),
            pltpu.VMEM((2, D, 512), BF16),
            pltpu.VMEM((2, D, 512), BF16),
            pltpu.VMEM((2, 4, WR, 512), BF16),
            pltpu.VMEM((WR, 512), BF16),
            pltpu.VMEM((3, D, 128), BF16),
            pltpu.VMEM((D, 128), BF16),
            pltpu.VMEM((3, WR, 128), BF16),
            pltpu.VMEM((7, WR, 128), BF16),
            pltpu.VMEM((2, WR, 128), BF16),
            pltpu.VMEM((2, WR, 128), BF16),
            pltpu.VMEM((2, WR, 1024), BF16),
            pltpu.VMEM((8, D), F32),
            pltpu.VMEM((8, D), F32),
            pltpu.VMEM((8, D), F32),
            pltpu.VMEM((7, 8, D), F32),
            pltpu.VMEM((4, 8, D), F32),
            pltpu.VMEM((2, 8, D), F32),
            pltpu.SemaphoreType.DMA((SENDS,)),
            pltpu.SemaphoreType.DMA((RECVS,)),
            pltpu.SemaphoreType.DMA((LOCALS,)),
        ],
        compiler_params=pltpu.CompilerParams(
            collective_id=0, has_side_effects=True, vmem_limit_bytes=60 << 20
        ),
    )
    results = layer(
        tokens,
        segments.reshape(1, ROWS),
        attn_gain.reshape(1, WR),
        ffn_gain.reshape(1, WR),
        freq,
        cotangent,
        w_query,
        w_key,
        w_value,
        w_out,
        w_gate,
        w_up,
        w_down,
    )
    finish = pl.pallas_call(
        finish_kernel,
        name="finish",
        out_shape=[
            shape((ROWS, D), BF16),
            shape((ROWS, D), F32),
            shape((8, D), F32),
            shape((WR, D), F32),
            shape((WR, 128), F32),
            shape((WR, 128), F32),
            shape((WR, D), F32),
            shape((WR, FF), F32),
            shape((WR, FF), F32),
            shape((FC, D), F32),
        ],
        in_specs=[vmem()] * 6,
        out_specs=[vmem()] * 10,
        compiler_params=pltpu.CompilerParams(vmem_limit_bytes=48 << 20),
    )
    out, tok, gain, gq, gk, gv, go, gate, up, down = finish(*results)
    own = lax.axis_index("shard") * WR
    both = lax.dynamic_slice(gain, (0, own), (2, WR))
    return out, tok, both[0], gq, gk, gv, go, both[1], gate, up, down


def solution(mesh):
    tokens = P(("replica", "shard"), None)
    weight = P("shard", None)
    return jax.shard_map(
        body,
        mesh=mesh,
        in_specs=(
            tokens, P(("replica", "shard")), P("shard"), weight, weight, weight, weight,
            P("shard"), weight, weight, weight, tokens,
        ),
        out_specs=(
            tokens, tokens, P("shard"), weight, weight, weight, weight, P("shard"), weight, weight, weight,
        ),
        check_vma=False,
    )
```

```python
import jax
import jax.numpy as jnp
from jax import lax
from jax.experimental import pallas as pl
from jax.experimental.pallas import tpu as pltpu
from jax.sharding import PartitionSpec as P

D = 896
H = 14
HD = 64
KVH = 2
GROUP = H // KVH
FF = 4864
FC = FF // 8
FH = FC // 2
ROWS = 128
LENGTH = 1024
WR = D // 8
EPS = 1e-05
THETA = 10000.0
SCALE = 0.125

F32 = jnp.float32
BF16 = jnp.bfloat16
MESH = pl.DeviceIdType.MESH


def coords():
    replica = lax.axis_index("replica")
    shard = lax.axis_index("shard")
    x = lax.div(replica, 8) * 2 + lax.div(shard, 4)
    return x, lax.rem(shard, 4), lax.rem(lax.div(replica, 2), 4), lax.rem(replica, 2)


def place(x, y, z, core):
    return (lax.div(x, 2) * 8 + z * 2 + core, lax.rem(x, 2) * 4 + y)


def wrap(value):
    return lax.rem(value + 8, 4)


def part_of(index, size, unit):
    return pl.ds(pl.multiple_of(index * size, unit), size)


def remote(src, dst, send, recv, device):
    return pltpu.make_async_remote_copy(
        src_ref=src, dst_ref=dst, send_sem=send, recv_sem=recv, device_id=device, device_id_type=MESH
    )


class Net:
    def __init__(self, ssem, rsem, peer):
        self.ssem, self.rsem, self.peer = ssem, rsem, peer
        self.ns = self.nr = 0
        self.open = []

    def sends(self, count):
        base = self.ns
        self.ns += count
        assert self.ns <= self.ssem.shape[0]
        return lambda index: self.ssem.at[base + index]

    def recvs(self, count):
        base = self.nr
        self.nr += count
        assert self.nr <= self.rsem.shape[0]
        return lambda index: self.rsem.at[base + index]

    def pair(self, count):
        return self.sends(count), self.recvs(count)

    def go(self, src, dst, send, recv, device, when=None):
        copy = remote(src, dst, send, recv, device)
        if when is None:
            copy.start()
        else:
            pl.when(when)(copy.start)
        self.open.append((copy, when))

    def landed(self, ref, recv, when=None):
        copy = remote(ref, ref, self.ssem.at[0], recv, self.peer)
        if when is None:
            copy.wait_recv()
        else:
            pl.when(when)(copy.wait_recv)

    def drain(self):
        done, self.open = self.open, []
        for copy, when in done:
            if when is None:
                copy.wait_send()
            else:
                pl.when(when)(copy.wait_send)


def signal(barrier, device):
    pl.semaphore_signal(barrier, inc=1, device_id=device, device_id_type=MESH)


def dot(left, right):
    return jnp.dot(left, right, preferred_element_type=F32)


def dot_nt(left, right):
    return lax.dot_general(left, right, (((1,), (1,)), ((), ())), preferred_element_type=F32)


SENDS = 192
RECVS = 192
LOCALS = 16


def layer_kernel(
    tokens, seg, gain_one, gain_two, freq,
    cot, wq, wk, wv, wo, wg, wu, wd,
    output, gtok, gain_o,
    attn_o, wide_o, d_o,
    misc, wqk, wvo, st, wgu, wdv, acts, da, kv, kc, vc, kt, vt, qs, mask, mixt, mid, gains, trig, lse,
    gua, own, pa, fr, dgu, dwd,
    gmt, own_cot, dkv, rkv, gqk,
    rz, sz, rx, sgu, agu, wide, rxd, sdx, rzd, agd, fin,
    xa, sa, rya, ta, rzb, sb, rza, ryb, tile, rh, aout,
    gvec, gx, gsum, gy, gz, gh,
    ssem, rsem, lsem,
):
    x, y, z, c = coords()
    xl, xh = lax.rem(x, 2), lax.div(x, 2)
    s = xl * 4 + y
    t = 2 * y + c
    core_peer = place(x, y, z, 1 - c)
    net = Net(ssem, rsem, core_peer)

    def of_sequence(k):
        other = lax.rem(s + k, 8)
        return other, place(xh * 2 + lax.div(other, 4), lax.rem(other, 4), z, c)

    def along_z(k):
        return place(x, y, wrap(z + k), c)

    def along_x(k):
        return place(wrap(x + k), y, z, c)

    rows = part_of(s, WR, 16)
    own_rows = part_of(s, ROWS, 16)
    own_tokens = part_of(t, ROWS, 16)
    core_half = part_of(c, 512, 128)

    kv[...] = jnp.zeros_like(kv)
    rkv[...] = jnp.zeros_like(rkv)

    barrier = pltpu.get_barrier_semaphore()
    for k in range(1, 4):
        signal(barrier, place(x, wrap(y + k), z, c))
        signal(barrier, along_z(k))
    for d in (1, 3):
        for k in range(4):
            signal(barrier, place(wrap(x + d), wrap(y + k), z, c))
        signal(barrier, place(wrap(x + d), y, z, 1 - c))
    signal(barrier, along_x(2))
    signal(barrier, core_peer)
    local = [
        pltpu.make_async_copy(wq, wqk.at[rows, pl.ds(0, D)], lsem.at[2]),
        pltpu.make_async_copy(wk, wqk.at[rows, pl.ds(D, 128)], lsem.at[3]),
        pltpu.make_async_copy(cot, acts.at[1, own_tokens], lsem.at[5]),
    ]
    own_index = 4 * c + z
    own_lanes = part_of(own_index, 128, 128)
    own_v = pltpu.make_async_copy(wv, wvo.at[rows, own_lanes], lsem.at[0])
    own_o = pltpu.make_async_copy(
        wo.at[:, part_of(jnp.maximum(own_index - 1, 0), 128, 128)], wvo.at[rows, own_lanes], lsem.at[0]
    )
    pl.when(own_index == 0)(own_v.start)
    pl.when(own_index != 0)(own_o.start)
    for copy in local:
        copy.start()
    sender = xl == lax.div(z, 2)
    own_gate = pltpu.make_async_copy(wg, wide.at[0], lsem.at[6])
    own_up = pltpu.make_async_copy(wu, wide.at[0], lsem.at[6])
    pl.when(sender & (lax.rem(z, 2) == 0))(own_gate.start)
    pl.when(sender & (lax.rem(z, 2) == 1))(own_up.start)
    own_down = pltpu.make_async_copy(wd, wdv, lsem.at[7])
    pl.when(c == xl)(own_down.start)

    misc[s] = jnp.zeros((8, 128), F32)
    misc[s, 0:1, 0:WR] = gain_one[...].astype(F32)
    misc[s, 1:2, 0:WR] = gain_two[...].astype(F32)
    misc[s, 2:3, :] = seg[...].astype(F32)

    pl.semaphore_wait(barrier, 18)

    ms, mr = net.pair(7)
    for k in range(1, 8):
        net.go(misc.at[s], misc.at[s], ms(k - 1), mr(k - 1), of_sequence(k)[1])

    pl.when(own_index == 0)(own_v.wait)
    pl.when(own_index != 0)(own_o.wait)
    os_, or_ = net.pair(7)
    for k in range(1, 8):
        part = wvo.at[rows, own_lanes]
        net.go(part, part, os_(k - 1), or_(k - 1), of_sequence(k)[1])

    local[0].wait()
    local[1].wait()
    qs_s, qs_r = net.pair(11)
    for k in range(1, 4):
        part = wqk.at[rows, core_half]
        net.go(part, part, qs_s(k - 1), qs_r(k - 1), place(x, wrap(y + k), z, c))
    for k in range(4):
        for d in range(2):
            part = wqk.at[rows, part_of(2 * c + d, 256, 128)]
            i = 3 + 2 * k + d
            net.go(part, part, qs_s(i), qs_r(i), place(wrap(x + 1 - 2 * d), wrap(y + k), z, c))

    pl.when(sender & (lax.rem(z, 2) == 0))(own_gate.wait)
    pl.when(sender & (lax.rem(z, 2) == 1))(own_up.wait)

    @pl.when(sender)
    def _():
        for k in range(8):
            st[k] = wide[0, :, FC * k : FC * (k + 1)]

    matrix = lax.rem(z, 2)
    gs, gr = net.pair(8)
    for d in range(2):
        for k in range(4):
            if d == 0 and k == 0:
                continue
            target = place(xh * 2 + lax.rem(xl + d, 2), wrap(y + k), z, c)
            block = st.at[4 * c + wrap(y + k)]
            net.go(block, wgu.at[matrix, rows], gs(4 * d + k), gr(4 * d + k), target, when=sender)

    @pl.when(sender)
    def _():
        wgu[matrix, rows] = st[4 * c + y]

    for k in range(1, 8):
        net.landed(wvo.at[rows, own_lanes], or_(k - 1))
    oz_s, oz_r = net.pair(3)
    for k in range(1, 4):
        part = wvo.at[:, own_lanes]
        net.go(part, part, oz_s(k - 1), oz_r(k - 1), along_z(k))

    tok = tokens[...].astype(F32)
    unit = tok * lax.rsqrt(jnp.mean(tok * tok, axis=-1, keepdims=True) + EPS)

    for k in range(1, 8):
        net.landed(misc.at[0], mr(k - 1))
    for k in range(8):
        gains[0:8, WR * k : WR * (k + 1)] = misc[k, 0:8, 0:WR]
    numbers = misc[:, 2, :]
    zeros = jnp.sum(jnp.where(numbers < 0.5, 1.0, 0.0), keepdims=True)
    ones = jnp.sum(jnp.where((numbers > 0.5) & (numbers < 1.5), 1.0, 0.0), keepdims=True)
    own_numbers = misc[s, 2:3, :]
    begin = jnp.where(own_numbers < 0.5, 0.0, jnp.where(own_numbers < 1.5, zeros, zeros + ones))
    lane = lax.broadcasted_iota(jnp.int32, (1, ROWS), 1) + s * ROWS
    angle = freq[...] * (lane.astype(F32) - begin)
    trig[0] = jnp.cos(angle)
    trig[1] = jnp.sin(angle)
    key_place = lax.broadcasted_iota(jnp.int32, (LENGTH, ROWS), 0)
    allowed = (key_place >= begin.astype(jnp.int32)) & (key_place <= lane)
    mask[...] = jnp.where(allowed, 0.0, -1e30)
    normed = (unit * gains[0:1, :]).astype(BF16)
    normed_t = jnp.transpose(normed)

    qf_s, qf_r = net.pair(11)
    for i in range(11):
        if i < 3:
            part = wqk.at[part_of(xl * 4 + wrap(y - (i + 1)), WR, 16), core_half]
        else:
            k, d = divmod(i - 3, 2)
            part = wqk.at[part_of((1 - xl) * 4 + wrap(y - k), WR, 16), part_of(2 * c + d, 256, 128)]
        net.landed(part, qs_r(i))
        net.go(part, part, qf_s(i), qf_r(i), core_peer)
    for i in range(11):
        part = wqk.at[rows, pl.ds(0, 512 if i < 3 else 256)]
        net.landed(part, qf_r(i))
    raw = jnp.transpose(dot(normed, wqk[...]))
    cosine, sine = trig[0], trig[1]

    def rotated(head):
        first = raw[HD * head : HD * head + 32]
        second = raw[HD * head + 32 : HD * head + 64]
        return first * cosine - second * sine, second * cosine + first * sine

    keys = jnp.concatenate([*rotated(H), *rotated(H + 1)], axis=0)
    kv[own_rows, 0:128] = jnp.transpose(keys).astype(BF16)
    of_s, of_r = net.pair(4)
    for k in range(4):
        part = wvo.at[:, part_of(4 * c + wrap(z - k), 128, 128)]
        if k:
            net.landed(part, oz_r(k - 1))
        net.go(part, part, of_s(k), of_r(k), core_peer)
    for k in range(4):
        net.landed(wvo.at[:, own_lanes], of_r(k))

    kv[own_rows, 128:256] = dot(normed, wvo[:, 0:128]).astype(BF16)

    ks, kr = net.pair(7)
    for k in range(1, 8):
        net.go(kv.at[own_rows], kv.at[own_rows], ks(k - 1), kr(k - 1), of_sequence(k)[1], when=s + k < 8)

    ds_, dr = net.sends(1), net.recvs(2)
    half = part_of(c, FH, 16)
    net.go(wd.at[half], wdv.at[half], ds_(0), dr(c), place(wrap(x + 1 - 2 * c), y, z, xl))

    def gather_tokens(which):
        ts, tr = net.pair(3)
        part = acts.at[which, own_tokens]
        for k in (1, 3, 2):
            net.go(part, part, ts(k - 1), tr(k - 1), place(x, wrap(y + k), z, c))
        return tr

    local[2].wait()
    cot_r = gather_tokens(1)

    for head in range(H):
        kv_head, j = divmod(head, GROUP)
        first, second = rotated(head)
        qs[kv_head, 0:32, ROWS * j : ROWS * (j + 1)] = (first * SCALE).astype(BF16)
        qs[kv_head, 32:64, ROWS * j : ROWS * (j + 1)] = (second * SCALE).astype(BF16)

    is_far = jnp.where(sender, 0, 1)
    for k in range(4):
        if k == 0:
            net.landed(wgu.at[0, rows], gr(4), when=jnp.logical_not(sender))
        else:
            net.landed(wgu.at[0, rows], gr(4 * is_far + k))
    gz_s, gz_r = net.pair(3)
    for k in range(1, 4):
        part = wgu.at[matrix, part_of(lax.div(z, 2), 4 * WR, 16)]
        net.go(part, part, gz_s(k - 1), gz_r(k - 1), along_z(k))

    for k in range(1, 8):
        net.landed(kv.at[own_rows], kr(k - 1), when=s - k >= 0)
    for head in range(KVH):
        keys = kv[:, HD * head : HD * (head + 1)]
        values = kv[:, 128 + HD * head : 128 + HD * (head + 1)]
        kc[head] = keys
        vc[head] = values
        kt[head] = jnp.transpose(keys)
        vt[head] = jnp.transpose(values)

    @pl.loop(0, GROUP)
    def _(j):
        lanes = part_of(j, ROWS, 128)
        for head in range(KVH):
            scores = dot(kc[head], qs[head, :, lanes]) + mask[...]
            highest = jnp.max(scores, axis=0, keepdims=True)
            weights = jnp.exp(scores - highest)
            total = jnp.sum(weights, axis=0, keepdims=True)
            probs = (weights * (1.0 / total)).astype(BF16)
            lse[GROUP * head + j] = jnp.broadcast_to(highest + jnp.log(total), (8, ROWS))
            mixt[part_of(GROUP * head + j, HD, HD)] = dot(vt[head], probs)

    attended_t = mixt[...].astype(BF16)
    attended = jnp.transpose(mixt[...]).astype(BF16)
    middle = tokens[...].astype(F32) + dot(attended, wvo[:, 128:1024])
    mid[...] = middle
    factor = lax.rsqrt(jnp.mean(middle * middle, axis=-1, keepdims=True) + EPS)
    acts[0, own_tokens] = (middle * factor * gains[1:2, :]).astype(BF16)

    n2_r = gather_tokens(0)

    def forward(which, off, send, recv):
        part = acts.at[which, part_of(2 * wrap(y - off) + c, ROWS, 16)]
        return remote(part, part, send(off), recv(off), core_peer)

    nf_s, nf_r = net.pair(4)
    cf_s, cf_r = net.pair(4)
    forward(0, 0, nf_s, nf_r).start()
    for off in (0, 1, 3, 2):
        if off:
            net.landed(acts.at[1, own_tokens], cot_r(off - 1))
        forward(1, off, cf_s, cf_r).start()
    pl.when(c == xl)(own_down.wait)
    for i in range(2):
        net.landed(wdv.at[pl.ds(FH * i, FH)], dr(i), when=c != xl)
    for k in range(1, 4):
        net.landed(wgu.at[0, pl.ds(0, 4 * WR)], gz_r(k - 1))

    xsend, xrecv = net.pair(4)
    psend, precv = net.sends(8), net.recvs(8)

    def offset(k):
        return k + lax.div(k, 2) - 2 * lax.div(k, 3)

    def exchange(off):
        block = part_of(off, 256, 256)
        return remote(pa.at[0, block], pa.at[1, block], xsend(off), xrecv(off), core_peer)

    def part_copy(off, core):
        return remote(
            pa.at[0, part_of(2 * off + core, ROWS, ROWS)], fr.at[c, off], psend(2 * off + core), precv(4 * c + off),
            place(x, wrap(y - off), z, core),
        )

    def add_cores(off):
        exchange(off).wait()
        block = part_of(off, 256, 256)
        pa[0, block] = (own[lax.rem(off, 2)] + pa[1, block].astype(F32)).astype(BF16)

    def feed_forward(k):
        off = offset(k)
        block = part_of(wrap(y - off), 256, 256)
        normed_two = acts[0, block]
        cotangent = acts[1, block]
        gate = dot(normed_two, wgu[0])
        up = dot(normed_two, wgu[1])
        grad_hidden = dot_nt(cotangent, wdv[...])
        opening = 1.0 / (1.0 + jnp.exp(-gate))
        act = gate * opening
        hidden = (act * up).astype(BF16)
        grad_gate = (grad_hidden * up * opening * (1.0 + gate * (1.0 - opening))).astype(BF16)
        grad_up = (grad_hidden * act).astype(BF16)
        gua[0, block] = grad_gate
        gua[1, block] = grad_up
        da[1, 0:FC, block] = jnp.transpose(hidden)
        da[0, :, block] = jnp.transpose(normed_two)
        out_part = dot(hidden, wdv[...])
        grad_part = dot_nt(grad_gate, wgu[0]) + dot_nt(grad_up, wgu[1])
        return off, out_part, grad_part

    def to_owners(off):
        add_cores(off)
        for core in range(2):

            @pl.when((off == 0) & (c == core))
            def _():
                fr[core, 0] = pa[0, ROWS * core : ROWS * (core + 1)]

            pl.when((off != 0) | (c != core))(part_copy(off, core).start)

    @pl.loop(0, 4)
    def _(k):
        @pl.when(k < 3)
        def _():
            after = offset(k + 1)
            net.landed(acts.at[0, own_tokens], n2_r(after - 1))
            forward(0, after, nf_s, nf_r).start()

        net.landed(acts.at[0, own_tokens], nf_r(offset(k)))
        net.landed(acts.at[1, own_tokens], cf_r(offset(k)))
        off, out_part, grad_part = feed_forward(k)

        pl.when(k >= 1)(lambda: to_owners(offset(k - 1)))

        own[lax.rem(off, 2)] = jnp.where(c == 0, out_part, grad_part)
        pa[0, part_of(off, 256, 256)] = jnp.where(c == 0, grad_part, out_part).astype(BF16)
        exchange(off).start()

    for off in range(4):
        forward(0, off, nf_s, nf_r).wait_send()
        forward(1, off, cf_s, cf_r).wait_send()
    net.drain()

    for matrix_ in range(2):
        for h in range(2):
            tall = dot(da[0, 448 * h : 448 * (h + 1)], gua[matrix_]).astype(BF16)
            for k in range(4):
                dgu[2 * matrix_ + h, wrap(k - y)] = tall[WR * k : WR * (k + 1)]
        if matrix_ == 0:
            to_owners(2)

    zs, zr = net.pair(3)
    for k in range(1, 4):
        net.go(dgu.at[:, wrap(z + k)], rz.at[k - 1], zs(k - 1), zr(k - 1), along_z(k))

    for h in range(2):
        tall = dot(da[1, FH * h : FH * (h + 1)], acts[1]).astype(BF16)
        for i in range(7):
            q = 7 * h + i
            dwd[q // 4, q % 4] = tall[:, 128 * i : 128 * (i + 1)]
    for q in (14, 15):
        dwd[q // 4, q % 4] = jnp.zeros((FH, 128), BF16)
    xds, xdr = net.pair(3)
    for k in range(1, 4):
        net.go(dwd.at[wrap(x + k)], rxd.at[k - 1], xds(k - 1), xdr(k - 1), along_x(k))

    own_cot[...] = acts[1, own_tokens]

    @pl.loop(0, GROUP)
    def _(j):
        lanes = part_of(j, ROWS, 128)
        for head in range(KVH):
            scores = dot(kc[head], qs[head, :, lanes]) + mask[...]
            acts[head, :, lanes] = jnp.exp(scores - lse[GROUP * head + j, 0:1, :]).astype(BF16)

    for kind in range(2):
        for off in range(4):
            net.landed(fr.at[kind, off], precv(4 * kind + off), when=None if off else c != kind)
    middle = mid[...]
    total = fr[0, 0].astype(F32)
    grad_normed = fr[1, 0].astype(F32)
    for off in range(1, 4):
        total = total + fr[0, off].astype(F32)
        grad_normed = grad_normed + fr[1, off].astype(F32)
    output[...] = (middle + total).astype(BF16)
    factor = lax.rsqrt(jnp.mean(middle * middle, axis=-1, keepdims=True) + EPS)
    unit_two = middle * factor
    scaled = grad_normed * gains[1:2, :]
    gvec[...] = jnp.broadcast_to(jnp.sum(grad_normed * unit_two, axis=0, keepdims=True), (8, D))
    grad_middle = own_cot[...].astype(F32) + factor * (
        scaled - unit_two * jnp.mean(scaled * unit_two, axis=-1, keepdims=True)
    )
    mid[...] = grad_middle

    branch = grad_middle.astype(BF16)
    grad_mixed = jnp.transpose(dot_nt(branch, wvo[:, 128:1024]))
    for head in range(H):
        kv_head, j = divmod(head, GROUP)
        gmt[kv_head, :, ROWS * j : ROWS * (j + 1)] = grad_mixed[HD * head : HD * (head + 1)].astype(BF16)
    da[1, :, 128:1024] = dot(attended_t, branch).astype(BF16)

    for off in range(4):
        for core in range(2):
            if off:
                part_copy(off, core).wait_send()
            else:
                pl.when(c != core)(part_copy(off, core).wait_send)
    @pl.loop(0, GROUP)
    def _(j):
        lanes = part_of(j, ROWS, 128)
        for head in range(KVH):
            row = GROUP * head + j
            probs = acts[head, :, lanes].astype(F32)
            grad_probs = dot(vc[head], gmt[head, :, lanes])
            delta = jnp.sum(grad_probs * probs, axis=0, keepdims=True)
            grad_scores = (probs * (grad_probs - delta)).astype(BF16)
            pa[head, :, lanes] = grad_scores
            rot = dot(kt[head], grad_scores) * SCALE
            cosine, sine = trig[0], trig[1]
            mixt[pl.ds(pl.multiple_of(HD * row, 32), 32)] = rot[0:32] * cosine + rot[32:64] * sine
            mixt[pl.ds(pl.multiple_of(HD * row + 32, 32), 32)] = rot[32:64] * cosine - rot[0:32] * sine

    for head in range(KVH):
        dkv[:, HD * head : HD * (head + 1)] = dot_nt(pa[head], qs[head]).astype(BF16)
        dkv[:, 128 + HD * head : 128 + HD * (head + 1)] = dot_nt(acts[head], gmt[head]).astype(BF16)

    kvs, kvr = net.pair(7)
    for k in range(1, 8):
        other, target = of_sequence(k)
        net.go(dkv.at[part_of(other, ROWS, 16)], rkv.at[k - 1], kvs(k - 1), kvr(k - 1), target, when=s + k >= 8)
    gqk[:, 0:D] = jnp.transpose(mixt[...]).astype(BF16)

    for k in range(1, 4):
        net.landed(rxd.at[k - 1], xdr(k - 1))
    sdx[...] = (
        dwd[x].astype(F32) + rxd[0].astype(F32) + rxd[1].astype(F32) + rxd[2].astype(F32)
    ).astype(BF16)
    zds, zdr = net.pair(3)
    for k in range(1, 4):
        net.go(sdx.at[wrap(z + k)], rzd.at[k - 1], zds(k - 1), zdr(k - 1), along_z(k))

    for k in range(1, 4):
        net.landed(rz.at[k - 1], zr(k - 1))
    for i in range(4):
        sz[lax.div(i, 2), lax.rem(i, 2)] = (
            dgu[i, z].astype(F32) + rz[0, i].astype(F32) + rz[1, i].astype(F32) + rz[2, i].astype(F32)
        ).astype(BF16)
    xs_s, xs_r = net.pair(3)
    for k in range(1, 4):
        net.go(sz.at[:, lax.rem(xl + k, 2)], rx.at[k - 1], xs_s(k - 1), xs_r(k - 1), along_x(k))

    total = dkv[own_rows].astype(F32)
    for k in range(1, 8):
        net.landed(rkv.at[k - 1], kvr(k - 1), when=k > s)
        total = total + rkv[k - 1].astype(F32)
    keys = jnp.transpose(total[:, 0:128])
    cosine, sine = trig[0], trig[1]
    back = []
    for head in range(KVH):
        first = keys[HD * head : HD * head + 32]
        second = keys[HD * head + 32 : HD * head + 64]
        back += [first * cosine + second * sine, second * cosine - first * sine]
    gqk[:, D:1024] = jnp.transpose(jnp.concatenate(back, axis=0)).astype(BF16)
    grad_value = total[:, 128:256].astype(BF16)

    da[0] = dot(normed_t, gqk[...]).astype(BF16)
    da[1, :, 0:128] = dot(normed_t, grad_value).astype(BF16)
    xas, xar = net.pair(3)
    for i in range(2):
        net.go(da.at[i, :, part_of(1 - c, 512, 128)], xa.at[i], xas(i), xar(i), core_peer)

    for k in range(1, 4):
        net.landed(rzd.at[k - 1], zdr(k - 1))
    agd[x, z] = (
        sdx[z].astype(F32) + rzd[0].astype(F32) + rzd[1].astype(F32) + rzd[2].astype(F32)
    ).astype(BF16)
    zas, zar = net.pair(3)
    for k in range(1, 4):
        net.go(agd.at[x, z], agd.at[x, z], zas(k - 1), zar(k - 1), along_z(k))

    grad_normed = dot_nt(gqk[...], wqk[...]) + dot_nt(grad_value, wvo[:, 0:128])
    tok = tokens[...].astype(F32)
    factor = lax.rsqrt(jnp.mean(tok * tok, axis=-1, keepdims=True) + EPS)
    unit = tok * factor
    scaled = grad_normed * gains[0:1, :]
    gtok[...] = mid[...] + factor * (scaled - unit * jnp.mean(scaled * unit, axis=-1, keepdims=True))
    gvec[0:1, :] = jnp.sum(grad_normed * unit, axis=0, keepdims=True)
    net.go(gvec, gx, xas(2), xar(2), core_peer)

    net.landed(xa.at[0], xar(0))
    sa[0] = (da[0, :, core_half].astype(F32) + xa[0].astype(F32)).astype(BF16)
    yas, yar = net.pair(11)
    for k in range(1, 4):
        other = xl * 4 + wrap(y + k)
        net.go(
            sa.at[0, part_of(other, WR, 16)], rya.at[0, k - 1], yas(k - 1), yar(k - 1), place(x, wrap(y + k), z, c)
        )
    for k in range(4):
        for d in range(2):
            other = (1 - xl) * 4 + wrap(y + k)
            lanes = pl.ds(256 * d, 256)
            net.go(
                sa.at[0, part_of(other, WR, 16), lanes], rya.at[1, k, :, lanes], yas(3 + 2 * k + d), yar(3 + 2 * k + d),
                place(wrap(x + 1 - 2 * d), wrap(y + k), z, c),
            )
    net.landed(xa.at[1], xar(1))
    sa[1] = (da[1, :, core_half].astype(F32) + xa[1].astype(F32)).astype(BF16)
    zbs, zbr = net.pair(3)
    for k in range(1, 4):
        net.go(sa.at[1, :, part_of(wrap(z + k), 128, 128)], rzb.at[k - 1], zbs(k - 1), zbr(k - 1), along_z(k))
    net.landed(gx, xar(2))
    gsum[...] = gvec[...] + gx[...]
    gys, gyr = net.pair(7)
    for k in range(1, 8):
        net.go(gsum, gy.at[k - 1], gys(k - 1), gyr(k - 1), of_sequence(k)[1])

    for k in range(1, 4):
        net.landed(agd.at[x, z], zar(k - 1))
    dxs, dxr = net.pair(3)
    for k in range(1, 4):
        net.go(
            agd.at[x], agd.at[x], dxs(k - 1), dxr(k - 1), along_x(k), when=lax.rem(xl + k, 2) == c
        )
    for k in range(1, 4):
        net.landed(rx.at[k - 1], xs_r(k - 1))
    sgu[...] = (
        sz[:, xl].astype(F32) + rx[0].astype(F32) + rx[1].astype(F32) + rx[2].astype(F32)
    ).astype(BF16)

    ags, agr = net.pair(4)
    own_block = 4 * c + y
    held = 4 * c + wrap(y - z)
    net.go(sgu, agu.at[own_block], ags(0), agr(0), place(x, wrap(y + z), z, c), when=z != 0)

    @pl.when(z == 0)
    def _():
        agu[own_block] = sgu[...]

    for k in range(1, 4):
        net.landed(rya.at[0, k - 1], yar(k - 1))
    for k in range(4):
        for d in range(2):
            net.landed(rya.at[1, k, :, pl.ds(256 * d, 256)], yar(3 + 2 * k + d))
    total = sa[0, rows].astype(F32)
    for k in range(3):
        total = total + rya[0, k].astype(F32)
    for k in range(4):
        total = total + rya[1, k].astype(F32)
    ta[...] = total.astype(BF16)
    zas2, zar2 = net.pair(3)
    for k in range(1, 4):
        net.go(ta.at[:, part_of(wrap(z + k), 128, 128)], rza.at[k - 1], zas2(k - 1), zar2(k - 1), along_z(k))

    for k in range(1, 4):
        net.landed(rzb.at[k - 1], zbr(k - 1))
    sb[...] = (
        sa[1, :, part_of(z, 128, 128)].astype(F32)
        + rzb[0].astype(F32) + rzb[1].astype(F32) + rzb[2].astype(F32)
    ).astype(BF16)
    ybs, ybr = net.pair(7)
    for k in range(1, 8):
        other, target = of_sequence(k)
        net.go(sb.at[part_of(other, WR, 16)], ryb.at[k - 1], ybs(k - 1), ybr(k - 1), target)
    total = gsum[...]
    for k in range(1, 8):
        net.landed(gy.at[k - 1], gyr(k - 1))
        total = total + gy[k - 1]
    gz[3] = total
    gzs, gzr = net.pair(3)
    for k in range(1, 4):
        net.go(gz.at[3], gz.at[k - 1], gzs(k - 1), gzr(k - 1), along_z(k))

    net.landed(agu.at[held], agr(0), when=z != 0)
    for k in range(1, 4):
        net.go(agu.at[held], agu.at[held], ags(k), agr(k), along_z(k))
    afs, afr = net.pair(4)
    net.go(agu.at[held], agu.at[held], afs(0), afr(0), core_peer)

    for k in range(1, 4):
        net.landed(rza.at[k - 1], zar2(k - 1))
    tile[0] = (
        ta[:, part_of(z, 128, 128)].astype(F32)
        + rza[0].astype(F32) + rza[1].astype(F32) + rza[2].astype(F32)
    ).astype(BF16)
    total = sb[rows].astype(F32)
    for k in range(1, 8):
        net.landed(ryb.at[k - 1], ybr(k - 1))
        total = total + ryb[k - 1].astype(F32)
    tile[1] = total.astype(BF16)
    total = gz[3]
    for k in range(1, 4):
        net.landed(gz.at[k - 1], gzr(k - 1))
        total = total + gz[k - 1]
    gh[1] = total
    hs, hr = net.pair(2)
    net.go(tile, rh, hs(0), hr(0), along_x(2))
    net.go(gh.at[1], gh.at[0], hs(1), hr(1), along_x(2))

    net.landed(rh, hr(0))
    own_tile = aout.at[:, :, own_lanes]
    aout[:, :, own_lanes] = (tile[...].astype(F32) + rh[...].astype(F32)).astype(BF16)
    lasts, lastr = net.pair(3)
    for k in range(1, 4):
        net.go(own_tile, own_tile, lasts(k - 1), lastr(k - 1), along_z(k))

    for k in range(1, 4):
        net.landed(agd.at[x], dxr(k - 1), when=xl == c)
    dfs, dfr = net.pair(1)
    net.go(agd, fin, dfs(0), dfr(0), core_peer, when=xl == c)
    own_sums = pltpu.make_async_copy(agd, d_o, lsem.at[8])
    pl.when(xl == c)(own_sums.start)

    net.landed(gh.at[0], hr(1))
    gain_o[...] = gh[0] + gh[1]

    for k in range(1, 4):
        net.landed(own_tile, lastr(k - 1))
    fs, fr_ = net.pair(1)
    part = aout.at[:, :, core_half]
    net.go(part, part, fs(0), fr_(0), core_peer)

    for k in (1, 3, 2):
        part = agu.at[4 * c + wrap(y - wrap(z - k))]
        net.landed(part, agr(k))
        net.go(part, part, afs(k), afr(k), core_peer)

    net.landed(fin, dfr(0), when=xl != c)
    peer_sums = pltpu.make_async_copy(fin, d_o, lsem.at[8])
    pl.when(xl != c)(peer_sums.start)
    outs = [
        pltpu.make_async_copy(aout, attn_o, lsem.at[9]),
        pltpu.make_async_copy(wide, wide_o, lsem.at[10]),
    ]
    net.landed(aout.at[:, :, pl.ds(0, 512)], fr_(0))
    outs[0].start()
    for k in range(4):
        net.landed(agu.at[held], afr(k))
    for k in range(8):
        for matrix_ in range(2):
            wide[matrix_, :, FC * k : FC * (k + 1)] = agu[k, matrix_]
    outs[1].start()

    net.drain()
    for copy in outs:
        copy.wait()
    pl.when(xl == c)(own_sums.wait)
    pl.when(xl != c)(peer_sums.wait)


def finish_kernel(
    out_in, tok_in, gain_in, attn_in, wide_in, down_in,
    one, two, out, tok, gq, gk, gv, go, gate, up, gdown,
    vout, vtok, gain, attn, wide, down, fq, fk, fv, fo, fgate, fup, fdown, isem, osem,
):
    ins = [
        pltpu.make_async_copy(source, target, isem.at[i])
        for i, (source, target) in enumerate(
            [(wide_in, wide), (down_in, down), (attn_in, attn), (tok_in, vtok), (out_in, vout), (gain_in, gain)]
        )
    ]
    for copy in ins:
        copy.start()
    outs = []

    def store(source, target):
        copy = pltpu.make_async_copy(source, target, osem.at[len(outs)])
        copy.start()
        outs.append(copy)

    ins[0].wait()
    fgate[...] = wide[0].astype(F32)
    store(fgate, gate)
    fup[...] = wide[1].astype(F32)
    store(fup, up)
    ins[1].wait()
    for q in range(14):
        h, i = divmod(q, 7)
        fdown[FH * h : FH * (h + 1), 128 * i : 128 * (i + 1)] = down[q // 4, q % 4].astype(F32)
    store(fdown, gdown)
    ins[2].wait()
    fq[...] = attn[0, :, 0:D].astype(F32)
    store(fq, gq)
    fo[...] = attn[1, :, 128:1024].astype(F32)
    store(fo, go)
    fk[...] = attn[0, :, D:1024].astype(F32)
    store(fk, gk)
    fv[...] = attn[1, :, 0:128].astype(F32)
    store(fv, gv)
    ins[3].wait()
    store(vtok, tok)
    ins[4].wait()
    store(vout, out)
    ins[5].wait()
    shard = lax.axis_index("shard")
    for k in range(8):

        @pl.when(shard == k)
        def _():
            one[...] = gain[0:1, WR * k : WR * (k + 1)]
            two[...] = gain[1:2, WR * k : WR * (k + 1)]

    for copy in outs:
        copy.wait()


def vmem():
    return pl.BlockSpec(memory_space=pltpu.VMEM)


def anywhere():
    return pl.BlockSpec(memory_space=pl.ANY)


def shape(dims, dtype):
    return jax.ShapeDtypeStruct(dims, dtype)


def body(
    tokens, segments, attn_gain, w_query, w_key, w_value, w_out, ffn_gain, w_gate, w_up, w_down, cotangent
):
    half = HD // 2
    frequency = THETA ** (-(jnp.arange(half, dtype=F32) * 2.0 / HD))
    freq = jnp.broadcast_to(frequency[:, None], (half, ROWS))
    layer = pl.pallas_call(
        layer_kernel,
        name="layer",
        out_shape=[
            shape((ROWS, D), BF16),
            shape((ROWS, D), F32),
            shape((8, D), F32),
            shape((2, WR, 1024), BF16),
            shape((2, WR, FF), BF16),
            shape((4, 4, FH, 128), BF16),
        ],
        in_specs=[vmem()] * 5 + [anywhere()] * 8,
        out_specs=[vmem()] * 3 + [anywhere()] * 3,
        scratch_shapes=[
            pltpu.VMEM((8, 8, 128), F32),
            pltpu.VMEM((D, 1024), BF16),
            pltpu.VMEM((D, 1024), BF16),
            pltpu.VMEM((8, WR, FC), BF16),
            pltpu.VMEM((2, D, FC), BF16),
            pltpu.VMEM((FC, D), BF16),
            pltpu.VMEM((2, LENGTH, D), BF16),
            pltpu.VMEM((2, D, LENGTH), BF16),
            pltpu.VMEM((LENGTH, 256), BF16),
            pltpu.VMEM((KVH, LENGTH, HD), BF16),
            pltpu.VMEM((KVH, LENGTH, HD), BF16),
            pltpu.VMEM((KVH, HD, LENGTH), BF16),
            pltpu.VMEM((KVH, HD, LENGTH), BF16),
            pltpu.VMEM((KVH, HD, D), BF16),
            pltpu.VMEM((LENGTH, ROWS), F32),
            pltpu.VMEM((D, ROWS), F32),
            pltpu.VMEM((ROWS, D), F32),
            pltpu.VMEM((8, D), F32),
            pltpu.VMEM((2, half, ROWS), F32),
            pltpu.VMEM((H, 8, ROWS), F32),
            pltpu.VMEM((2, LENGTH, FC), BF16),
            pltpu.VMEM((2, 256, D), F32),
            pltpu.VMEM((2, LENGTH, D), BF16),
            pltpu.VMEM((2, 4, ROWS, D), BF16),
            pltpu.VMEM((4, 4, WR, FC), BF16),
            pltpu.VMEM((4, 4, FH, 128), BF16),
            pltpu.VMEM((KVH, HD, D), BF16),
            pltpu.VMEM((ROWS, D), BF16),
            pltpu.VMEM((LENGTH, 256), BF16),
            pltpu.VMEM((7, ROWS, 256), BF16),
            pltpu.VMEM((ROWS, 1024), BF16),
            pltpu.VMEM((3, 4, WR, FC), BF16),
            pltpu.VMEM((2, 2, WR, FC), BF16),
            pltpu.VMEM((3, 2, WR, FC), BF16),
            pltpu.VMEM((2, WR, FC), BF16),
            pltpu.VMEM((8, 2, WR, FC), BF16),
            pltpu.VMEM((2, WR, FF), BF16),
            pltpu.VMEM((3, 4, FH, 128), BF16),
            pltpu.VMEM((4, FH, 128), BF16),
            pltpu.VMEM((3, FH, 128), BF16),
            pltpu.VMEM((4, 4, FH, 128), BF16),
            pltpu.VMEM((4, 4, FH, 128), BF16),
            pltpu.VMEM((2, D, 512), BF16),
            pltpu.VMEM((2, D, 512), BF16),
            pltpu.VMEM((2, 4, WR, 512), BF16),
            pltpu.VMEM((WR, 512), BF16),
            pltpu.VMEM((3, D, 128), BF16),
            pltpu.VMEM((D, 128), BF16),
            pltpu.VMEM((3, WR, 128), BF16),
            pltpu.VMEM((7, WR, 128), BF16),
            pltpu.VMEM((2, WR, 128), BF16),
            pltpu.VMEM((2, WR, 128), BF16),
            pltpu.VMEM((2, WR, 1024), BF16),
            pltpu.VMEM((8, D), F32),
            pltpu.VMEM((8, D), F32),
            pltpu.VMEM((8, D), F32),
            pltpu.VMEM((7, 8, D), F32),
            pltpu.VMEM((4, 8, D), F32),
            pltpu.VMEM((2, 8, D), F32),
            pltpu.SemaphoreType.DMA((SENDS,)),
            pltpu.SemaphoreType.DMA((RECVS,)),
            pltpu.SemaphoreType.DMA((LOCALS,)),
        ],
        compiler_params=pltpu.CompilerParams(
            collective_id=0, has_side_effects=True, vmem_limit_bytes=60 << 20
        ),
    )
    results = layer(
        tokens,
        segments.reshape(1, ROWS),
        attn_gain.reshape(1, WR),
        ffn_gain.reshape(1, WR),
        freq,
        cotangent,
        w_query,
        w_key,
        w_value,
        w_out,
        w_gate,
        w_up,
        w_down,
    )
    finish = pl.pallas_call(
        finish_kernel,
        name="finish",
        out_shape=[
            shape((1, WR), F32),
            shape((1, WR), F32),
            shape((ROWS, D), BF16),
            shape((ROWS, D), F32),
            shape((WR, D), F32),
            shape((WR, 128), F32),
            shape((WR, 128), F32),
            shape((WR, D), F32),
            shape((WR, FF), F32),
            shape((WR, FF), F32),
            shape((FC, D), F32),
        ],
        in_specs=[anywhere()] * 6,
        out_specs=[vmem()] * 2 + [anywhere()] * 9,
        scratch_shapes=[
            pltpu.VMEM((ROWS, D), BF16),
            pltpu.VMEM((ROWS, D), F32),
            pltpu.VMEM((8, D), F32),
            pltpu.VMEM((2, WR, 1024), BF16),
            pltpu.VMEM((2, WR, FF), BF16),
            pltpu.VMEM((4, 4, FH, 128), BF16),
            pltpu.VMEM((WR, D), F32),
            pltpu.VMEM((WR, 128), F32),
            pltpu.VMEM((WR, 128), F32),
            pltpu.VMEM((WR, D), F32),
            pltpu.VMEM((WR, FF), F32),
            pltpu.VMEM((WR, FF), F32),
            pltpu.VMEM((FC, D), F32),
            pltpu.SemaphoreType.DMA((6,)),
            pltpu.SemaphoreType.DMA((9,)),
        ],
        compiler_params=pltpu.CompilerParams(vmem_limit_bytes=62 << 20),
    )
    one, two, out, tok, gq, gk, gv, go, gate, up, down = finish(*results)
    return out, tok, one.reshape(WR), gq, gk, gv, go, two.reshape(WR), gate, up, down


def solution(mesh):
    tokens = P(("replica", "shard"), None)
    weight = P("shard", None)
    return jax.shard_map(
        body,
        mesh=mesh,
        in_specs=(
            tokens, P(("replica", "shard")), P("shard"), weight, weight, weight, weight,
            P("shard"), weight, weight, weight, tokens,
        ),
        out_specs=(
            tokens, tokens, P("shard"), weight, weight, weight, weight, P("shard"), weight, weight, weight,
        ),
        check_vma=False,
    )
```

```python
import jax
import jax.numpy as jnp
import numpy as np
from jax import lax
from jax.experimental import pallas as pl
from jax.experimental.pallas import tpu as pltpu
from jax.sharding import PartitionSpec as P

D = 896
H = 14
HD = 64
KVH = 2
GROUP = H // KVH
FF = 4864
FC = FF // 8
FH = FC // 2
ROWS = 128
LENGTH = 1024
WR = D // 8
EPS = 1e-05
THETA = 10000.0
SCALE = 0.125

F32 = jnp.float32
BF16 = jnp.bfloat16
MESH = pl.DeviceIdType.MESH


def coords():
    replica = lax.axis_index("replica")
    shard = lax.axis_index("shard")
    x = lax.div(replica, 8) * 2 + lax.div(shard, 4)
    return x, lax.rem(shard, 4), lax.rem(lax.div(replica, 2), 4), lax.rem(replica, 2)


def place(x, y, z, core):
    return (lax.div(x, 2) * 8 + z * 2 + core, lax.rem(x, 2) * 4 + y)


def wrap(value):
    return lax.rem(value + 8, 4)


def part_of(index, size, unit):
    return pl.ds(pl.multiple_of(index * size, unit), size)


def remote(src, dst, send, recv, device):
    return pltpu.make_async_remote_copy(
        src_ref=src, dst_ref=dst, send_sem=send, recv_sem=recv, device_id=device, device_id_type=MESH
    )


class Net:
    def __init__(self, ssem, rsem, peer):
        self.ssem, self.rsem, self.peer = ssem, rsem, peer
        self.ns = self.nr = 0
        self.open = []

    def sends(self, count):
        base = self.ns
        self.ns += count
        assert self.ns <= self.ssem.shape[0]
        return lambda index: self.ssem.at[base + index]

    def recvs(self, count):
        base = self.nr
        self.nr += count
        assert self.nr <= self.rsem.shape[0]
        return lambda index: self.rsem.at[base + index]

    def pair(self, count):
        return self.sends(count), self.recvs(count)

    def go(self, src, dst, send, recv, device, when=None):
        copy = remote(src, dst, send, recv, device)
        if when is None:
            copy.start()
        else:
            pl.when(when)(copy.start)
        self.open.append((copy, when))

    def landed(self, ref, recv, when=None):
        copy = remote(ref, ref, self.ssem.at[0], recv, self.peer)
        if when is None:
            copy.wait_recv()
        else:
            pl.when(when)(copy.wait_recv)

    def drain(self):
        done, self.open = self.open, []
        for copy, when in done:
            if when is None:
                copy.wait_send()
            else:
                pl.when(when)(copy.wait_send)


def signal(barrier, device):
    pl.semaphore_signal(barrier, inc=1, device_id=device, device_id_type=MESH)


def dot(left, right):
    return jnp.dot(left, right, preferred_element_type=F32)


def dot_nt(left, right):
    return lax.dot_general(left, right, (((1,), (1,)), ((), ())), preferred_element_type=F32)


SENDS = 256
RECVS = 256
LOCALS = 16


def layer_kernel(
    tokens, seg, gain_one, gain_two, freq,
    cot, wq, wk, wv, wo, wg, wu, wd,
    output, gtok, gain_o,
    attn_o, wide_o, d_o,
    misc, wqk, wvo, st, wgu, wdv, acts, da, kv, kc, vc, kt, vt, qs, mask, mixt, mid, gains, trig, lse,
    gua, own, pa, fr, via, dgate, dup, dwd,
    gmt, own_cot, dkv, rkv, gqk,
    rz, sz, rx, ru, su, ruz, sgu, agu, wide, rzd, sdz, rxd, agd, fin,
    xa, sa, rya, ryl, ta, rza, tile, rh, aout,
    gvec, gpack, gx, gsum, gy, gz, gh,
    ssem, rsem, lsem,
):
    x, y, z, c = coords()
    xl, xh = lax.rem(x, 2), lax.div(x, 2)
    s = xl * 4 + y
    t = 2 * y + c
    core_peer = place(x, y, z, 1 - c)
    net = Net(ssem, rsem, core_peer)

    def of_sequence(k):
        other = lax.rem(s + k, 8)
        return other, place(xh * 2 + lax.div(other, 4), lax.rem(other, 4), z, c)

    def along_z(k):
        return place(x, y, wrap(z + k), c)

    def along_x(k):
        return place(wrap(x + k), y, z, c)

    rows = part_of(s, WR, 16)
    own_rows = part_of(s, ROWS, 16)
    own_tokens = part_of(t, ROWS, 16)
    core_half = part_of(c, 512, 128)

    local = [
        pltpu.make_async_copy(wq.at[:, pl.ds(0, 384)], wqk.at[rows, pl.ds(0, 384)], lsem.at[2]),
        pltpu.make_async_copy(wk, wqk.at[rows, pl.ds(384, 128)], lsem.at[3]),
        pltpu.make_async_copy(wq.at[:, pl.ds(384, 512)], wqk.at[rows, pl.ds(512, 512)], lsem.at[4]),
        pltpu.make_async_copy(cot, acts.at[1, own_tokens], lsem.at[5]),
    ]
    own_index = 4 * c + z
    own_lanes = part_of(own_index, 128, 128)
    own_v = pltpu.make_async_copy(wv, wvo.at[rows, own_lanes], lsem.at[0])
    own_o = pltpu.make_async_copy(
        wo.at[:, part_of(own_index - jnp.where(own_index > 3, 1, 0), 128, 128)], wvo.at[rows, own_lanes], lsem.at[0]
    )
    pl.when(own_index == 3)(own_v.start)
    pl.when(own_index != 3)(own_o.start)
    for copy in local:
        copy.start()
    sender = xl == lax.div(z, 2)
    own_gate = pltpu.make_async_copy(wg, wide.at[0], lsem.at[6])
    own_up = pltpu.make_async_copy(wu, wide.at[0], lsem.at[6])
    pl.when(sender & (lax.rem(z, 2) == 0))(own_gate.start)
    pl.when(sender & (lax.rem(z, 2) == 1))(own_up.start)
    own_down = pltpu.make_async_copy(wd, wdv, lsem.at[7])
    pl.when(c == xl)(own_down.start)

    kv[...] = jnp.zeros_like(kv)
    rkv[...] = jnp.zeros_like(rkv)

    barrier = pltpu.get_barrier_semaphore()
    for k in range(1, 4):
        signal(barrier, place(x, wrap(y + k), z, c))
        signal(barrier, along_z(k))
    for d in (1, 3):
        for k in range(4):
            signal(barrier, place(wrap(x + d), wrap(y + k), z, c))
        signal(barrier, place(wrap(x + d), y, z, 1 - c))
    for k in range(4):
        signal(barrier, place(wrap(x + 2), wrap(y + k), z, c))
    signal(barrier, core_peer)
    misc[s] = jnp.zeros((8, 128), F32)
    misc[s, 0:1, 0:WR] = gain_one[...].astype(F32)
    misc[s, 1:2, 0:WR] = gain_two[...].astype(F32)
    misc[s, 2:3, :] = seg[...].astype(F32)

    pl.semaphore_wait(barrier, 21)

    ms, mr = net.pair(7)
    for k in range(1, 8):
        net.go(misc.at[s], misc.at[s], ms(k - 1), mr(k - 1), of_sequence(k)[1])

    pl.when(own_index == 3)(own_v.wait)
    pl.when(own_index != 3)(own_o.wait)
    os_, or_ = net.pair(7)
    for k in range(1, 8):
        part = wvo.at[rows, own_lanes]
        net.go(part, part, os_(k - 1), or_(k - 1), of_sequence(k)[1])

    for copy in local[0:3]:
        copy.wait()
    qs_s, qs_r = net.pair(11)
    for k in range(1, 4):
        part = wqk.at[rows, core_half]
        net.go(part, part, qs_s(k - 1), qs_r(k - 1), place(x, wrap(y + k), z, c))
    for k in range(4):
        for d in range(2):
            part = wqk.at[rows, part_of(2 * c + d, 256, 128)]
            i = 3 + 2 * k + d
            net.go(part, part, qs_s(i), qs_r(i), place(wrap(x + 1 - 2 * d), wrap(y + k), z, c))

    pl.when(sender & (lax.rem(z, 2) == 0))(own_gate.wait)
    pl.when(sender & (lax.rem(z, 2) == 1))(own_up.wait)

    @pl.when(sender)
    def _():
        for k in range(8):
            st[k] = wide[0, :, FC * k : FC * (k + 1)]

    matrix = lax.rem(z, 2)
    gs, gr = net.pair(8)
    for d in range(2):
        for k in range(4):
            if d == 0 and k == 0:
                continue
            target = place(xh * 2 + lax.rem(xl + d, 2), wrap(y + k), z, c)
            block = st.at[4 * c + wrap(y + k)]
            net.go(block, wgu.at[matrix, rows], gs(4 * d + k), gr(4 * d + k), target, when=sender)

    @pl.when(sender)
    def _():
        wgu[matrix, rows] = st[4 * c + y]

    for k in range(1, 8):
        net.landed(wvo.at[rows, own_lanes], or_(k - 1))
    oz_s, oz_r = net.pair(3)
    for k in range(1, 4):
        part = wvo.at[:, own_lanes]
        net.go(part, part, oz_s(k - 1), oz_r(k - 1), along_z(k))

    def block_rows(k):
        return part_of(4 * lax.div(z, 2) + wrap(y - k), WR, 16)

    gz_s, gz_r = net.pair(12)

    def block_along_z(k):
        part = wgu.at[matrix, block_rows(k)]
        for to in range(1, 4):
            net.go(part, part, gz_s(4 * to + k - 4), gz_r(4 * to + k - 4), along_z(to))

    net.landed(wgu.at[0, rows], gr(4), when=jnp.logical_not(sender))
    block_along_z(0)

    tok = tokens[...].astype(F32)
    unit = tok * lax.rsqrt(jnp.mean(tok * tok, axis=-1, keepdims=True) + EPS)

    for k in range(1, 8):
        net.landed(misc.at[0], mr(k - 1))
    for k in range(8):
        gains[0:8, WR * k : WR * (k + 1)] = misc[k, 0:8, 0:WR]
    numbers = misc[:, 2, :]
    zeros = jnp.sum(jnp.where(numbers < 0.5, 1.0, 0.0), keepdims=True)
    ones = jnp.sum(jnp.where((numbers > 0.5) & (numbers < 1.5), 1.0, 0.0), keepdims=True)
    own_numbers = misc[s, 2:3, :]
    begin = jnp.where(own_numbers < 0.5, 0.0, jnp.where(own_numbers < 1.5, zeros, zeros + ones))
    lane = lax.broadcasted_iota(jnp.int32, (1, ROWS), 1) + s * ROWS
    angle = freq[...] * (lane.astype(F32) - begin)
    trig[0] = jnp.cos(angle)
    trig[1] = jnp.sin(angle)
    key_place = lax.broadcasted_iota(jnp.int32, (LENGTH, ROWS), 0)
    allowed = (key_place >= begin.astype(jnp.int32)) & (key_place <= lane)
    mask[...] = jnp.where(allowed, 0.0, -1e30)
    normed = (unit * gains[0:1, :]).astype(BF16)
    normed_t = jnp.transpose(normed)

    qf_s, qf_r = net.pair(11)
    for i in range(11):
        if i < 3:
            part = wqk.at[part_of(xl * 4 + wrap(y - (i + 1)), WR, 16), core_half]
        else:
            k, d = divmod(i - 3, 2)
            part = wqk.at[part_of((1 - xl) * 4 + wrap(y - k), WR, 16), part_of(2 * c + d, 256, 128)]
        net.landed(part, qs_r(i))
        net.go(part, part, qf_s(i), qf_r(i), core_peer)
    for i in range(11):
        part = wqk.at[rows, pl.ds(0, 512 if i < 3 else 256)]
        net.landed(part, qf_r(i))
    raw = jnp.transpose(dot(normed, wqk[...]))
    cosine, sine = trig[0], trig[1]

    def rotated(head):
        at = HD * head + (128 if head > 5 else 0) if head < H else 384 + HD * (head - H)
        first = raw[at : at + 32]
        second = raw[at + 32 : at + 64]
        return first * cosine - second * sine, second * cosine + first * sine

    keys = jnp.concatenate([*rotated(H), *rotated(H + 1)], axis=0)
    kv[own_rows, 0:128] = jnp.transpose(keys).astype(BF16)

    ks, kr = net.pair(14)

    def to_later(which):
        part = kv.at[own_rows, pl.ds(128 * which, 128)]
        for k in range(1, 8):
            i = 7 * which + k - 1
            net.go(part, part, ks(i), kr(i), of_sequence(k)[1], when=s + k < 8)

    to_later(0)
    of_s, of_r = net.pair(4)
    for k in range(4):
        part = wvo.at[:, part_of(4 * c + wrap(z - k), 128, 128)]
        if k:
            net.landed(part, oz_r(k - 1))
        net.go(part, part, of_s(k), of_r(k), core_peer)
    for k in range(4):
        net.landed(wvo.at[:, own_lanes], of_r(k))

    kv[own_rows, 128:256] = dot(normed, wvo[:, 384:512]).astype(BF16)

    to_later(1)

    ds_, dr = net.sends(1), net.recvs(2)
    half = part_of(c, FH, 16)
    net.go(wd.at[half], wdv.at[half], ds_(0), dr(c), place(wrap(x + 1 - 2 * c), y, z, xl))

    def gather_tokens(which):
        ts, tr = net.pair(3)
        part = acts.at[which, own_tokens]
        for k in (1, 3, 2):
            net.go(part, part, ts(k - 1), tr(k - 1), place(x, wrap(y + k), z, c))
        return tr

    local[3].wait()
    cot_r = gather_tokens(1)

    for head in range(H):
        kv_head, j = divmod(head, GROUP)
        first, second = rotated(head)
        qs[kv_head, 0:32, ROWS * j : ROWS * (j + 1)] = (first * SCALE).astype(BF16)
        qs[kv_head, 32:64, ROWS * j : ROWS * (j + 1)] = (second * SCALE).astype(BF16)

    is_far = jnp.where(sender, 0, 1)
    for k in range(1, 4):
        net.landed(wgu.at[0, rows], gr(4 * is_far + k))
        block_along_z(k)

    for k in range(1, 8):
        for which in range(2):
            net.landed(kv.at[own_rows, pl.ds(0, 128)], kr(7 * which + k - 1), when=s - k >= 0)
    for head in range(KVH):
        keys = kv[:, HD * head : HD * (head + 1)]
        values = kv[:, 128 + HD * head : 128 + HD * (head + 1)]
        kc[head] = keys
        vc[head] = values
        kt[head] = jnp.transpose(keys)
        vt[head] = jnp.transpose(values)

    def attend(head, j, width):
        lanes = part_of(j, ROWS, 128) if width == 1 else pl.ds(pl.multiple_of(ROWS * j, 256), 2 * ROWS)
        raw_scores = dot(kc[head], qs[head, :, lanes])
        parts = []
        for i in range(width):
            scores = raw_scores[:, ROWS * i : ROWS * (i + 1)] + mask[...]
            highest = jnp.max(scores, axis=0, keepdims=True)
            weights = jnp.exp(scores - highest)
            total = jnp.sum(weights, axis=0, keepdims=True)
            parts.append((weights * (1.0 / total)).astype(BF16))
            lse[GROUP * head + j + i] = jnp.broadcast_to(highest + jnp.log(total), (8, ROWS))
        heads = dot(vt[head], jnp.concatenate(parts, axis=1) if width == 2 else parts[0])
        for i in range(width):
            mixt[part_of(GROUP * head + j + i, HD, HD)] = heads[:, ROWS * i : ROWS * (i + 1)]

    for p in range(GROUP // 2):
        for head in range(KVH):
            attend(head, 2 * p, 2)
    for head in range(KVH):
        attend(head, GROUP - 1, 1)

    attended_t = mixt[...].astype(BF16)
    attended = jnp.transpose(mixt[...]).astype(BF16)
    middle = tokens[...].astype(F32) + jnp.concatenate(
        [dot(attended, wvo[:, 0:384]), dot(attended, wvo[:, 512:1024])], axis=1
    )
    mid[...] = middle
    factor = lax.rsqrt(jnp.mean(middle * middle, axis=-1, keepdims=True) + EPS)
    acts[0, own_tokens] = (middle * factor * gains[1:2, :]).astype(BF16)

    n2_r = gather_tokens(0)

    def forward(which, off, send, recv):
        part = acts.at[which, part_of(2 * wrap(y - off) + c, ROWS, 16)]
        return remote(part, part, send(off), recv(off), core_peer)

    nf_s, nf_r = net.pair(4)
    cf_s, cf_r = net.pair(4)
    forward(0, 0, nf_s, nf_r).start()
    for off in (0, 1, 3, 2):
        if off:
            net.landed(acts.at[1, own_tokens], cot_r(off - 1))
        forward(1, off, cf_s, cf_r).start()
    pl.when(c == xl)(own_down.wait)
    for i in range(2):
        net.landed(wdv.at[pl.ds(FH * i, FH)], dr(i), when=c != xl)
    for i in range(12):
        net.landed(wgu.at[0, rows], gz_r(i))

    xsend, xrecv = net.pair(4)
    psend, precv = net.sends(8), net.recvs(6)
    vsend, vrecv = net.pair(2)

    def offset(k):
        return k

    def exchange(off):
        block = part_of(off, 256, 256)
        return remote(pa.at[0, block], pa.at[1, block], xsend(off), xrecv(off), core_peer)

    def part_copy(slot, core):
        off = (0, 1, 3)[slot]
        return remote(
            pa.at[0, pl.ds(256 * off + ROWS * core, ROWS)], fr.at[c, slot], psend(2 * slot + core),
            precv(3 * c + slot), place(x, wrap(y - off), z, core),
        )

    def through(side):
        rows_of = pl.ds(512 + ROWS * side, ROWS)
        return remote(pa.at[0, rows_of], via.at[side], vsend(side), vrecv(side), place(x, wrap(y - 1 + 2 * side), z, c))

    def add_cores(off):
        exchange(off).wait()
        block = pl.ds(256 * off, 256)
        total = own[off] + pa[1, block].astype(F32)
        if off % 2:
            side = off // 2
            through(side).wait_recv()
            half_of = slice(ROWS * side, ROWS * (side + 1))
            other = slice(ROWS * (1 - side), ROWS * (2 - side))
            pa[0, pl.ds(256 * off + ROWS * (1 - side), ROWS)] = total[other].astype(BF16)
            pa[0, pl.ds(256 * off + ROWS * side, ROWS)] = (total[half_of] + via[side].astype(F32)).astype(BF16)
        else:
            pa[0, block] = total.astype(BF16)

    def to_owners(off):
        add_cores(off)
        for core in range(2):
            if off == 2:
                through(core).start()
            elif off:
                part_copy(off - off // 3, core).start()
            else:

                @pl.when(c == core)
                def _():
                    fr[core, 0] = pa[0, ROWS * core : ROWS * (core + 1)]

                pl.when(c != core)(part_copy(0, core).start)

    @pl.loop(0, 4)
    def _(k):
        net.landed(acts.at[0, own_tokens], nf_r(offset(k)))
        net.landed(acts.at[1, own_tokens], cf_r(offset(k)))
        off = offset(k)
        block = part_of(wrap(y - off), 256, 256)
        normed_two = acts[0, block]
        cotangent = acts[1, block]
        gate = dot(normed_two, wgu[0])
        up = dot(normed_two, wgu[1])
        grad_hidden = dot_nt(cotangent, wdv[...])
        opening = 1.0 / (1.0 + jnp.exp(-gate))
        act = gate * opening
        hidden = (act * up).astype(BF16)
        grad_gate = (grad_hidden * up * opening * (1.0 + gate * (1.0 - opening))).astype(BF16)
        grad_up = (grad_hidden * act).astype(BF16)
        gua[0, block] = grad_gate
        gua[1, block] = grad_up
        da[1, 0:FC, block] = jnp.transpose(hidden)
        da[0, :, block] = jnp.transpose(normed_two)

        @pl.when(k < 3)
        def _():
            after = offset(k + 1)
            net.landed(acts.at[0, own_tokens], n2_r(after - 1))
            forward(0, after, nf_s, nf_r).start()

        pl.when(k == 1)(lambda: to_owners(0))
        pl.when(k == 3)(lambda: to_owners(2))

        out_part = dot(hidden, wdv[...])
        grad_part = dot_nt(grad_gate, wgu[0]) + dot_nt(grad_up, wgu[1])
        own[off] = jnp.where(c == 0, out_part, grad_part)
        pa[0, part_of(off, 256, 256)] = jnp.where(c == 0, grad_part, out_part).astype(BF16)
        exchange(off).start()

    for off in range(4):
        forward(0, off, nf_s, nf_r).wait_send()
        forward(1, off, cf_s, cf_r).wait_send()
    net.drain()

    def gradient(matrix_, store):
        for h in range(2):
            tall = dot(da[0, 448 * h : 448 * (h + 1)], gua[matrix_]).astype(BF16)
            for k in range(4):
                store[h, wrap(k - y)] = tall[WR * k : WR * (k + 1)]

    gradient(0, dgate)
    zs, zr = net.pair(3)
    for k in range(1, 4):
        net.go(dgate.at[:, wrap(z + k)], rz.at[k - 1], zs(k - 1), zr(k - 1), along_z(k))
    gradient(1, dup)
    us, ur = net.pair(3)
    for k in range(1, 4):
        part = dup.at[lax.rem(xl + k, 2), pl.ds(2 * lax.div(wrap(x + k), 2), 2)]
        net.go(part, ru.at[k - 1], us(k - 1), ur(k - 1), along_x(k))

    to_owners(1)
    to_owners(3)

    for h in range(2):
        tall = dot(da[1, FH * h : FH * (h + 1)], acts[1]).astype(BF16)
        for i in range(7):
            q = 7 * h + i
            dwd[q // 4, q % 4] = tall[:, 128 * i : 128 * (i + 1)]
    for q in (14, 15):
        dwd[q // 4, q % 4] = jnp.zeros((FH, 128), BF16)

    own_cot[...] = acts[1, own_tokens]

    @pl.loop(0, GROUP)
    def _(j):
        lanes = part_of(j, ROWS, 128)
        for head in range(KVH):
            scores = dot(kc[head], qs[head, :, lanes]) + mask[...]
            acts[head, :, lanes] = jnp.exp(scores - lse[GROUP * head + j, 0:1, :]).astype(BF16)

    for kind in range(2):
        for slot in range(3):
            net.landed(fr.at[kind, slot], precv(3 * kind + slot), when=None if slot else c != kind)
    middle = mid[...]
    total = fr[0, 0].astype(F32)
    grad_normed = fr[1, 0].astype(F32)
    for slot in range(1, 3):
        total = total + fr[0, slot].astype(F32)
        grad_normed = grad_normed + fr[1, slot].astype(F32)
    output[...] = (middle + total).astype(BF16)
    factor = lax.rsqrt(jnp.mean(middle * middle, axis=-1, keepdims=True) + EPS)
    unit_two = middle * factor
    scaled = grad_normed * gains[1:2, :]
    gvec[...] = jnp.broadcast_to(jnp.sum(grad_normed * unit_two, axis=0, keepdims=True), (8, D))
    grad_middle = own_cot[...].astype(F32) + factor * (
        scaled - unit_two * jnp.mean(scaled * unit_two, axis=-1, keepdims=True)
    )
    mid[...] = grad_middle

    branch = grad_middle.astype(BF16)
    grad_mixed = jnp.transpose(
        dot_nt(branch[:, 0:384], wvo[:, 0:384]) + dot_nt(branch[:, 384:D], wvo[:, 512:1024])
    )
    for head in range(H):
        kv_head, j = divmod(head, GROUP)
        gmt[kv_head, :, ROWS * j : ROWS * (j + 1)] = grad_mixed[HD * head : HD * (head + 1)].astype(BF16)
    grad_out = dot(attended_t, branch).astype(BF16)
    da[1, :, 0:384] = grad_out[:, 0:384]
    da[1, :, 512:1024] = grad_out[:, 384:D]
    first_of_peer = pl.ds(pl.multiple_of(512 * (1 - c), 128), 384)
    last_of_peer = pl.ds(pl.multiple_of(512 * (1 - c) + 384, 128), 128)
    first_own = pl.ds(pl.multiple_of(512 * c, 128), 384)
    last_own = pl.ds(pl.multiple_of(512 * c + 384, 128), 128)
    firsts, lasts_ = pl.ds(0, 384), pl.ds(384, 128)
    xas, xar = net.pair(5)
    net.go(da.at[1, :, first_of_peer], xa.at[1, :, firsts], xas(1), xar(1), core_peer)
    net.go(da.at[1, :, last_of_peer], xa.at[1, :, lasts_], xas(3), xar(3), core_peer, when=c == 0)

    for slot in range(3):
        for core in range(2):
            if slot:
                part_copy(slot, core).wait_send()
            else:
                pl.when(c != core)(part_copy(slot, core).wait_send)
    for side in range(2):
        through(side).wait_send()

    for k in range(1, 4):
        net.landed(ru.at[k - 1], ur(k - 1))
    for i in range(2):
        su[i] = (
            dup[xl, 2 * xh + i].astype(F32) + ru[0, i].astype(F32) + ru[1, i].astype(F32) + ru[2, i].astype(F32)
        ).astype(BF16)
    vs, vr = net.sends(2), net.recvs(4)
    for i in range(2):
        target = 2 * xh + i
        net.go(su.at[i], ruz.at[z], vs(i), vr(z), place(x, y, target, c), when=z != target)
    for k in range(1, 4):
        net.landed(rz.at[k - 1], zr(k - 1))
    for i in range(2):
        sz[i] = (
            dgate[i, z].astype(F32) + rz[0, i].astype(F32) + rz[1, i].astype(F32) + rz[2, i].astype(F32)
        ).astype(BF16)
    xs_s, xs_r = net.pair(3)
    for k in range(1, 4):
        net.go(sz.at[lax.rem(xl + k, 2)], rx.at[k - 1], xs_s(k - 1), xs_r(k - 1), along_x(k))

    def to_rows_owners(i, lanes, half_size, sems):
        for k in range(1, 4):
            other = part_of(xl * 4 + wrap(y + k), WR, 16)
            net.go(
                sa.at[i, other, lanes], rya.at[i, 0, k - 1, :, lanes], sems[0](k - 1), sems[1](k - 1),
                place(x, wrap(y + k), z, c),
            )
        for k in range(4):
            other = part_of((1 - xl) * 4 + wrap(y + k), WR, 16)
            for d, cut in enumerate(half_size):
                net.go(
                    sa.at[i, other, cut], rya.at[i, 1, k, :, cut], sems[0](3 + 2 * k + d), sems[1](3 + 2 * k + d),
                    place(wrap(x + 1 - 2 * d), wrap(y + k), z, c),
                )

    def from_rows_owners(i, lanes, half_size, sems):
        for k in range(1, 4):
            net.landed(rya.at[i, 0, k - 1, :, lanes], sems[1](k - 1))
        for k in range(4):
            for d, cut in enumerate(half_size):
                net.landed(rya.at[i, 1, k, :, cut], sems[1](3 + 2 * k + d))

    def last_tile(i, when):
        net.landed(xa.at[i, :, lasts_], xar(2 + i), when=when)

        @pl.when(when)
        def _():
            sa[i, :, 384:512] = (da[i, :, last_own].astype(F32) + xa[i, :, 384:512].astype(F32)).astype(BF16)

        for k in range(1, 8):
            other, target = of_sequence(k)
            part = sa.at[i, part_of(other, WR, 16), lasts_]
            net.go(part, ryl.at[i, k - 1], yl[i][0](k - 1), yl[i][1](k - 1), target, when=when)

    first_cuts = (pl.ds(0, 256), pl.ds(256, 128))
    yf = [net.pair(11), net.pair(11)]
    yl = [net.pair(7), net.pair(7)]
    net.landed(xa.at[1, :, firsts], xar(1))
    sa[1, :, 0:384] = (da[1, :, first_own].astype(F32) + xa[1, :, 0:384].astype(F32)).astype(BF16)
    to_rows_owners(1, firsts, first_cuts, yf[1])
    last_tile(1, c == 1)

    zds, zdr = net.pair(3)
    for k in range(1, 4):
        net.go(dwd.at[:, wrap(z + k)], rzd.at[k - 1], zds(k - 1), zdr(k - 1), along_z(k))

    def attend_back(head, j, width):
        lanes = part_of(j, ROWS, 128) if width == 1 else pl.ds(pl.multiple_of(ROWS * j, 256), 2 * ROWS)
        probs = acts[head, :, lanes].astype(F32)
        grad_probs = dot(vc[head], gmt[head, :, lanes])
        delta = jnp.sum(grad_probs * probs, axis=0, keepdims=True)
        grad_scores = (probs * (grad_probs - delta)).astype(BF16)
        pa[head, :, lanes] = grad_scores
        both = dot(kt[head], grad_scores) * SCALE
        cosine, sine = trig[0], trig[1]
        for i in range(width):
            rot = both[:, ROWS * i : ROWS * (i + 1)]
            at = HD * (GROUP * head + j + i)
            mixt[pl.ds(pl.multiple_of(at, 32), 32)] = rot[0:32] * cosine + rot[32:64] * sine
            mixt[pl.ds(pl.multiple_of(at + 32, 32), 32)] = rot[32:64] * cosine - rot[0:32] * sine

    kvs, kvr = net.pair(14)
    for head in range(KVH):
        for p in range(GROUP // 2):
            attend_back(head, 2 * p, 2)
        attend_back(head, GROUP - 1, 1)
        dkv[:, 128 * head : 128 * head + HD] = dot_nt(pa[head], qs[head]).astype(BF16)
        dkv[:, 128 * head + HD : 128 * (head + 1)] = dot_nt(acts[head], gmt[head]).astype(BF16)
        for k in range(1, 8):
            other, target = of_sequence(k)
            lanes = pl.ds(128 * head, 128)
            i = 7 * head + k - 1
            net.go(
                dkv.at[part_of(other, ROWS, 16), lanes], rkv.at[k - 1, :, lanes], kvs(i), kvr(i), target, when=s + k >= 8
            )

    grad_query = jnp.transpose(mixt[...]).astype(BF16)
    gqk[:, 0:384] = grad_query[:, 0:384]
    gqk[:, 512:1024] = grad_query[:, 384:D]
    part = dot(normed_t, grad_query).astype(BF16)
    da[0, :, 0:384] = part[:, 0:384]
    da[0, :, 512:1024] = part[:, 384:D]
    net.go(da.at[0, :, first_of_peer], xa.at[0, :, firsts], xas(0), xar(0), core_peer)
    net.go(da.at[0, :, last_of_peer], xa.at[0, :, lasts_], xas(2), xar(2), core_peer, when=c == 0)

    net.landed(xa.at[0, :, firsts], xar(0))
    sa[0, :, 0:384] = (da[0, :, first_own].astype(F32) + xa[0, :, 0:384].astype(F32)).astype(BF16)
    to_rows_owners(0, firsts, first_cuts, yf[0])
    last_tile(0, c == 1)

    for k in range(1, 4):
        net.landed(rx.at[k - 1], xs_r(k - 1))
    sgu[0] = (
        sz[xl].astype(F32) + rx[0].astype(F32) + rx[1].astype(F32) + rx[2].astype(F32)
    ).astype(BF16)
    own_block = 4 * c + y
    held = 4 * c + wrap(y - z)
    ags, agr = net.pair(4)
    net.go(sgu.at[0], agu.at[0, own_block], ags(0), agr(0), place(x, wrap(y + z), z, c), when=z != 0)

    @pl.when(z == 0)
    def _():
        agu[0, own_block] = sgu[0]

    cosine, sine = trig[0], trig[1]
    back, grad_values = [], []
    for head in range(KVH):
        lanes = slice(128 * head, 128 * (head + 1))
        total = dkv[own_rows, lanes].astype(F32)
        for k in range(1, 8):
            net.landed(rkv.at[k - 1, :, pl.ds(0, 128)], kvr(7 * head + k - 1), when=k > s)
            total = total + rkv[k - 1, :, lanes].astype(F32)
        keys = jnp.transpose(total)
        first, second = keys[0:32], keys[32:64]
        back += [first * cosine + second * sine, second * cosine - first * sine]
        grad_values.append(total[:, HD:128])
    grad_key = jnp.transpose(jnp.concatenate(back, axis=0)).astype(BF16)
    gqk[:, 384:512] = grad_key
    grad_value = jnp.concatenate(grad_values, axis=1).astype(BF16)
    da[0, :, 384:512] = dot(normed_t, grad_key).astype(BF16)
    da[1, :, 384:512] = dot(normed_t, grad_value).astype(BF16)
    for i in range(2):
        net.go(da.at[i, :, last_of_peer], xa.at[i, :, lasts_], xas(2 + i), xar(2 + i), core_peer, when=c == 1)

    for k in range(1, 4):
        net.landed(rzd.at[k - 1], zdr(k - 1))
    for i in range(4):
        sdz[i] = (
            dwd[i, z].astype(F32) + rzd[0, i].astype(F32) + rzd[1, i].astype(F32) + rzd[2, i].astype(F32)
        ).astype(BF16)
    xds, xdr = net.pair(3)
    for k in range(1, 4):
        net.go(sdz.at[wrap(x + k)], rxd.at[k - 1], xds(k - 1), xdr(k - 1), along_x(k))

    owner = xh == lax.div(z, 2)
    for k in range(4):
        net.landed(su.at[0], vr(k), when=owner & (z != k))
    ucs, ucr = net.pair(1)
    uhs = net.sends(1)

    @pl.when(owner)
    def _():
        ruz[z] = su[lax.rem(z, 2)]
        sgu[1] = (
            ruz[0].astype(F32) + ruz[1].astype(F32) + ruz[2].astype(F32) + ruz[3].astype(F32)
        ).astype(BF16)

    net.go(sgu.at[1], agu.at[1, own_block], ucs(0), ucr(0), place(x, wrap(y + z), z, c), when=owner & (z != 0))
    net.go(sgu.at[1], agu.at[1, own_block], uhs(0), ucr(0), place(wrap(x + 2), wrap(y + z), z, c), when=owner)

    @pl.when(owner & (z == 0))
    def _():
        agu[1, own_block] = sgu[1]

    grad_normed = dot_nt(gqk[...], wqk[...]) + dot_nt(grad_value, wvo[:, 384:512])
    tok = tokens[...].astype(F32)
    factor = lax.rsqrt(jnp.mean(tok * tok, axis=-1, keepdims=True) + EPS)
    unit = tok * factor
    scaled = grad_normed * gains[0:1, :]
    gtok[...] = mid[...] + factor * (scaled - unit * jnp.mean(scaled * unit, axis=-1, keepdims=True))
    gvec[0:1, :] = jnp.sum(grad_normed * unit, axis=0, keepdims=True)
    for row in range(2):
        for i in range(7):
            gpack[7 * row + i : 7 * row + i + 1, :] = gvec[row : row + 1, 128 * i : 128 * (i + 1)]
    net.go(gpack, gx, xas(4), xar(4), core_peer)

    for i in range(2):
        last_tile(i, c == 0)
    net.landed(gx, xar(4))
    gsum[...] = gpack[...] + gx[...]
    gys, gyr = net.pair(7)
    for k in range(1, 8):
        net.go(gsum, gy.at[k - 1], gys(k - 1), gyr(k - 1), of_sequence(k)[1])

    for k in range(1, 4):
        net.landed(rxd.at[k - 1], xdr(k - 1))
    agd[x, z] = (
        sdz[x].astype(F32) + rxd[0].astype(F32) + rxd[1].astype(F32) + rxd[2].astype(F32)
    ).astype(BF16)
    zas, zar = net.pair(3)
    for k in range(1, 4):
        net.go(agd.at[x, z], agd.at[x, z], zas(k - 1), zar(k - 1), along_z(k))

    afs, afr = net.pair(8)

    def spread(matrix_, sends, recvs):
        for k in range(1, 4):
            net.go(agu.at[matrix_, held], agu.at[matrix_, held], sends(k), recvs(k), along_z(k))
        net.go(agu.at[matrix_, held], agu.at[matrix_, held], afs(4 * matrix_), afr(4 * matrix_), core_peer)

    net.landed(agu.at[0, held], agr(0), when=z != 0)
    spread(0, ags, agr)

    zas2, zar2 = net.pair(6)
    for i in range(2):
        from_rows_owners(i, firsts, first_cuts, yf[i])
        total = sa[i, rows, 0:384].astype(F32)
        for k in range(3):
            total = total + rya[i, 0, k, :, 0:384].astype(F32)
        for k in range(4):
            total = total + rya[i, 1, k, :, 0:384].astype(F32)
        ta[i, :, 0:384] = total.astype(BF16)
        total = sa[i, rows, 384:512].astype(F32)
        for k in range(1, 8):
            net.landed(ryl.at[i, k - 1], yl[i][1](k - 1))
            total = total + ryl[i, k - 1].astype(F32)
        ta[i, :, 384:512] = total.astype(BF16)
    for k in range(1, 4):
        net.go(ta.at[:, :, part_of(wrap(z + k), 128, 128)], rza.at[k - 1], zas2(k - 1), zar2(k - 1), along_z(k))
    total = gsum[...]
    for k in range(1, 8):
        net.landed(gy.at[k - 1], gyr(k - 1))
        total = total + gy[k - 1]
    gz[3] = total
    for k in range(1, 4):
        net.go(gz.at[3], gz.at[k - 1], zas2(k + 2), zar2(k + 2), along_z(k))

    for k in range(1, 4):
        net.landed(agd.at[x, z], zar(k - 1))
    dxs, dxr = net.pair(3)
    for k in range(1, 4):
        net.go(agd.at[x], agd.at[x], dxs(k - 1), dxr(k - 1), along_x(k), when=lax.rem(xl + k, 2) == c)

    uas, uar = net.pair(4)
    net.landed(agu.at[1, held], ucr(0), when=jnp.logical_not(owner) | (z != 0))
    spread(1, uas, uar)

    for k in range(1, 4):
        net.landed(rza.at[k - 1], zar2(k - 1))
    tile[...] = (
        ta[:, :, part_of(z, 128, 128)].astype(F32)
        + rza[0].astype(F32) + rza[1].astype(F32) + rza[2].astype(F32)
    ).astype(BF16)
    total = gz[3]
    for k in range(1, 4):
        net.landed(gz.at[k - 1], zar2(k + 2))
        total = total + gz[k - 1]
    gh[1] = total
    hs, hr = net.pair(2)
    net.go(tile, rh, hs(0), hr(0), along_x(2))
    net.go(gh.at[1], gh.at[0], hs(1), hr(1), along_x(2))

    net.landed(rh, hr(0))
    own_tile = aout.at[:, :, own_lanes]
    aout[:, :, own_lanes] = (tile[...].astype(F32) + rh[...].astype(F32)).astype(BF16)
    lasts, lastr = net.pair(3)
    for k in range(1, 4):
        net.go(own_tile, own_tile, lasts(k - 1), lastr(k - 1), along_z(k))
    net.landed(gh.at[0], hr(1))
    gpack_sum = gh[0] + gh[1]
    gain_o[...] = jnp.zeros_like(gain_o)
    for row in range(2):
        for i in range(7):
            gain_o[row : row + 1, 128 * i : 128 * (i + 1)] = gpack_sum[7 * row + i : 7 * row + i + 1]

    outs = [
        pltpu.make_async_copy(aout, attn_o, lsem.at[9]),
        pltpu.make_async_copy(wide.at[0], wide_o.at[0], lsem.at[10]),
        pltpu.make_async_copy(wide.at[1], wide_o.at[1], lsem.at[11]),
    ]

    def to_other_core(matrix_, recvs):
        for k in (1, 3, 2):
            part = agu.at[matrix_, 4 * c + wrap(y - wrap(z - k))]
            net.landed(part, recvs(k))
            net.go(part, part, afs(4 * matrix_ + k), afr(4 * matrix_ + k), core_peer)

    def assemble(matrix_):
        for k in range(4):
            net.landed(agu.at[matrix_, held], afr(4 * matrix_ + k))
        for k in range(8):
            wide[matrix_, :, FC * k : FC * (k + 1)] = agu[matrix_, k]
        outs[1 + matrix_].start()

    to_other_core(0, agr)
    assemble(0)
    for k in range(1, 4):
        net.landed(agd.at[x], dxr(k - 1), when=xl == c)
    dfs, dfr = net.pair(1)
    net.go(agd, fin, dfs(0), dfr(0), core_peer, when=xl == c)
    own_sums = pltpu.make_async_copy(agd, d_o, lsem.at[8])
    pl.when(xl == c)(own_sums.start)
    for k in range(1, 4):
        net.landed(own_tile, lastr(k - 1))
    fs, fr_ = net.pair(1)
    part = aout.at[:, :, core_half]
    net.go(part, part, fs(0), fr_(0), core_peer)
    to_other_core(1, uar)
    net.landed(fin, dfr(0), when=xl != c)
    peer_sums = pltpu.make_async_copy(fin, d_o, lsem.at[8])
    pl.when(xl != c)(peer_sums.start)
    net.landed(aout.at[:, :, pl.ds(0, 512)], fr_(0))
    outs[0].start()
    assemble(1)

    net.drain()
    for copy in outs:
        copy.wait()
    pl.when(xl == c)(own_sums.wait)
    pl.when(xl != c)(peer_sums.wait)


def finish_kernel(
    out_in, tok_in, gain_in, attn_in, wide_in, down_in,
    one, two, out, tok, gq, gk, gv, go, gate, up, gdown,
    vout, vtok, gain, attn, wide, down, fq, fk, fv, fo, fgate, fup, fdown, isem, osem,
):
    ins = [
        pltpu.make_async_copy(source, target, isem.at[i])
        for i, (source, target) in enumerate(
            [(wide_in, wide), (down_in, down), (attn_in, attn), (tok_in, vtok), (out_in, vout), (gain_in, gain)]
        )
    ]
    for copy in ins:
        copy.start()
    outs = []

    def store(source, target):
        copy = pltpu.make_async_copy(source, target, osem.at[len(outs)])
        copy.start()
        outs.append(copy)

    ins[0].wait()
    fgate[...] = wide[0].astype(F32)
    store(fgate, gate)
    fup[...] = wide[1].astype(F32)
    store(fup, up)
    ins[1].wait()
    for q in range(14):
        h, i = divmod(q, 7)
        fdown[FH * h : FH * (h + 1), 128 * i : 128 * (i + 1)] = down[q // 4, q % 4].astype(F32)
    store(fdown, gdown)
    ins[2].wait()
    fq[:, 0:384] = attn[0, :, 0:384].astype(F32)
    fq[:, 384:D] = attn[0, :, 512:1024].astype(F32)
    store(fq, gq)
    fo[:, 0:384] = attn[1, :, 0:384].astype(F32)
    fo[:, 384:D] = attn[1, :, 512:1024].astype(F32)
    store(fo, go)
    fk[...] = attn[0, :, 384:512].astype(F32)
    store(fk, gk)
    fv[...] = attn[1, :, 384:512].astype(F32)
    store(fv, gv)
    ins[3].wait()
    store(vtok, tok)
    ins[4].wait()
    store(vout, out)
    ins[5].wait()
    shard = lax.axis_index("shard")
    for k in range(8):

        @pl.when(shard == k)
        def _():
            one[...] = gain[0:1, WR * k : WR * (k + 1)]
            two[...] = gain[1:2, WR * k : WR * (k + 1)]

    for copy in outs:
        copy.wait()


def vmem():
    return pl.BlockSpec(memory_space=pltpu.VMEM)


def anywhere():
    return pl.BlockSpec(memory_space=pl.ANY)


def shape(dims, dtype):
    return jax.ShapeDtypeStruct(dims, dtype)


def body(
    tokens, segments, attn_gain, w_query, w_key, w_value, w_out, ffn_gain, w_gate, w_up, w_down, cotangent
):
    half = HD // 2
    frequency = THETA ** (-(np.arange(half) * 2.0 / HD))
    freq = np.broadcast_to(frequency[:, None], (half, ROWS)).astype(np.float32)
    layer = pl.pallas_call(
        layer_kernel,
        name="layer",
        out_shape=[
            shape((ROWS, D), BF16),
            shape((ROWS, D), F32),
            shape((8, D), F32),
            shape((2, WR, 1024), BF16),
            shape((2, WR, FF), BF16),
            shape((4, 4, FH, 128), BF16),
        ],
        in_specs=[vmem()] * 5 + [anywhere()] * 8,
        out_specs=[vmem()] * 3 + [anywhere()] * 3,
        scratch_shapes=[
            pltpu.VMEM((8, 8, 128), F32),
            pltpu.VMEM((D, 1024), BF16),
            pltpu.VMEM((D, 1024), BF16),
            pltpu.VMEM((8, WR, FC), BF16),
            pltpu.VMEM((2, D, FC), BF16),
            pltpu.VMEM((FC, D), BF16),
            pltpu.VMEM((2, LENGTH, D), BF16),
            pltpu.VMEM((2, D, LENGTH), BF16),
            pltpu.VMEM((LENGTH, 256), BF16),
            pltpu.VMEM((KVH, LENGTH, HD), BF16),
            pltpu.VMEM((KVH, LENGTH, HD), BF16),
            pltpu.VMEM((KVH, HD, LENGTH), BF16),
            pltpu.VMEM((KVH, HD, LENGTH), BF16),
            pltpu.VMEM((KVH, HD, D), BF16),
            pltpu.VMEM((LENGTH, ROWS), F32),
            pltpu.VMEM((D, ROWS), F32),
            pltpu.VMEM((ROWS, D), F32),
            pltpu.VMEM((8, D), F32),
            pltpu.VMEM((2, half, ROWS), F32),
            pltpu.VMEM((H, 8, ROWS), F32),
            pltpu.VMEM((2, LENGTH, FC), BF16),
            pltpu.VMEM((4, 256, D), F32),
            pltpu.VMEM((2, LENGTH, D), BF16),
            pltpu.VMEM((2, 3, ROWS, D), BF16),
            pltpu.VMEM((2, ROWS, D), BF16),
            pltpu.VMEM((2, 4, WR, FC), BF16),
            pltpu.VMEM((2, 4, WR, FC), BF16),
            pltpu.VMEM((4, 4, FH, 128), BF16),
            pltpu.VMEM((KVH, HD, D), BF16),
            pltpu.VMEM((ROWS, D), BF16),
            pltpu.VMEM((LENGTH, 256), BF16),
            pltpu.VMEM((7, ROWS, 256), BF16),
            pltpu.VMEM((ROWS, 1024), BF16),
            pltpu.VMEM((3, 2, WR, FC), BF16),
            pltpu.VMEM((2, WR, FC), BF16),
            pltpu.VMEM((3, WR, FC), BF16),
            pltpu.VMEM((3, 2, WR, FC), BF16),
            pltpu.VMEM((2, WR, FC), BF16),
            pltpu.VMEM((4, WR, FC), BF16),
            pltpu.VMEM((2, WR, FC), BF16),
            pltpu.VMEM((2, 8, WR, FC), BF16),
            pltpu.VMEM((2, WR, FF), BF16),
            pltpu.VMEM((3, 4, FH, 128), BF16),
            pltpu.VMEM((4, FH, 128), BF16),
            pltpu.VMEM((3, FH, 128), BF16),
            pltpu.VMEM((4, 4, FH, 128), BF16),
            pltpu.VMEM((4, 4, FH, 128), BF16),
            pltpu.VMEM((2, D, 512), BF16),
            pltpu.VMEM((2, D, 512), BF16),
            pltpu.VMEM((2, 2, 4, WR, 384), BF16),
            pltpu.VMEM((2, 7, WR, 128), BF16),
            pltpu.VMEM((2, WR, 512), BF16),
            pltpu.VMEM((3, 2, WR, 128), BF16),
            pltpu.VMEM((2, WR, 128), BF16),
            pltpu.VMEM((2, WR, 128), BF16),
            pltpu.VMEM((2, WR, 1024), BF16),
            pltpu.VMEM((8, D), F32),
            pltpu.VMEM((16, 128), F32),
            pltpu.VMEM((16, 128), F32),
            pltpu.VMEM((16, 128), F32),
            pltpu.VMEM((7, 16, 128), F32),
            pltpu.VMEM((4, 16, 128), F32),
            pltpu.VMEM((2, 16, 128), F32),
            pltpu.SemaphoreType.DMA((SENDS,)),
            pltpu.SemaphoreType.DMA((RECVS,)),
            pltpu.SemaphoreType.DMA((LOCALS,)),
        ],
        compiler_params=pltpu.CompilerParams(
            collective_id=0, has_side_effects=True, vmem_limit_bytes=60 << 20
        ),
    )
    results = layer(
        tokens,
        segments.reshape(1, ROWS),
        attn_gain.reshape(1, WR),
        ffn_gain.reshape(1, WR),
        freq,
        cotangent,
        w_query,
        w_key,
        w_value,
        w_out,
        w_gate,
        w_up,
        w_down,
    )
    finish = pl.pallas_call(
        finish_kernel,
        name="finish",
        out_shape=[
            shape((1, WR), F32),
            shape((1, WR), F32),
            shape((ROWS, D), BF16),
            shape((ROWS, D), F32),
            shape((WR, D), F32),
            shape((WR, 128), F32),
            shape((WR, 128), F32),
            shape((WR, D), F32),
            shape((WR, FF), F32),
            shape((WR, FF), F32),
            shape((FC, D), F32),
        ],
        in_specs=[anywhere()] * 6,
        out_specs=[vmem()] * 2 + [anywhere()] * 9,
        scratch_shapes=[
            pltpu.VMEM((ROWS, D), BF16),
            pltpu.VMEM((ROWS, D), F32),
            pltpu.VMEM((8, D), F32),
            pltpu.VMEM((2, WR, 1024), BF16),
            pltpu.VMEM((2, WR, FF), BF16),
            pltpu.VMEM((4, 4, FH, 128), BF16),
            pltpu.VMEM((WR, D), F32),
            pltpu.VMEM((WR, 128), F32),
            pltpu.VMEM((WR, 128), F32),
            pltpu.VMEM((WR, D), F32),
            pltpu.VMEM((WR, FF), F32),
            pltpu.VMEM((WR, FF), F32),
            pltpu.VMEM((FC, D), F32),
            pltpu.SemaphoreType.DMA((6,)),
            pltpu.SemaphoreType.DMA((9,)),
        ],
        compiler_params=pltpu.CompilerParams(vmem_limit_bytes=62 << 20),
    )
    one, two, out, tok, gq, gk, gv, go, gate, up, down = finish(*results)
    return out, tok, one.reshape(WR), gq, gk, gv, go, two.reshape(WR), gate, up, down


def solution(mesh):
    tokens = P(("replica", "shard"), None)
    weight = P("shard", None)
    return jax.shard_map(
        body,
        mesh=mesh,
        in_specs=(
            tokens, P(("replica", "shard")), P("shard"), weight, weight, weight, weight,
            P("shard"), weight, weight, weight, tokens,
        ),
        out_specs=(
            tokens, tokens, P("shard"), weight, weight, weight, weight, P("shard"), weight, weight, weight,
        ),
        check_vma=False,
    )
```

```python
import jax
import jax.numpy as jnp
import numpy as np
from jax import lax
from jax.experimental import pallas as pl
from jax.experimental.pallas import tpu as pltpu
from jax.sharding import PartitionSpec as P

D = 896
H = 14
HD = 64
KVH = 2
GROUP = H // KVH
FF = 4864
FC = FF // 8
FH = FC // 2
ROWS = 128
LENGTH = 1024
WR = D // 8
EPS = 1e-05
THETA = 10000.0
SCALE = 0.125

F32 = jnp.float32
BF16 = jnp.bfloat16
MESH = pl.DeviceIdType.MESH


def coords():
    replica = lax.axis_index("replica")
    shard = lax.axis_index("shard")
    x = lax.div(replica, 8) * 2 + lax.div(shard, 4)
    return x, lax.rem(shard, 4), lax.rem(lax.div(replica, 2), 4), lax.rem(replica, 2)


def place(x, y, z, core):
    return (lax.div(x, 2) * 8 + z * 2 + core, lax.rem(x, 2) * 4 + y)


def wrap(value):
    return lax.rem(value + 16, 4)


def part_of(index, size, unit):
    return pl.ds(pl.multiple_of(index * size, unit), size)


def remote(src, dst, send, recv, device):
    return pltpu.make_async_remote_copy(
        src_ref=src, dst_ref=dst, send_sem=send, recv_sem=recv, device_id=device, device_id_type=MESH
    )


class Net:
    def __init__(self, ssem, rsem, peer):
        self.ssem, self.rsem, self.peer = ssem, rsem, peer
        self.ns = self.nr = 0
        self.open = []

    def sends(self, count):
        base = self.ns
        self.ns += count
        assert self.ns <= self.ssem.shape[0]
        return lambda index: self.ssem.at[base + index]

    def recvs(self, count):
        base = self.nr
        self.nr += count
        assert self.nr <= self.rsem.shape[0]
        return lambda index: self.rsem.at[base + index]

    def pair(self, count):
        return self.sends(count), self.recvs(count)

    def go(self, src, dst, send, recv, device, when=None):
        copy = remote(src, dst, send, recv, device)
        if when is None:
            copy.start()
        else:
            pl.when(when)(copy.start)
        self.open.append((copy, when))

    def landed(self, ref, recv, when=None):
        copy = remote(ref, ref, self.ssem.at[0], recv, self.peer)
        if when is None:
            copy.wait_recv()
        else:
            pl.when(when)(copy.wait_recv)

    def drain(self):
        done, self.open = self.open, []
        for copy, when in done:
            if when is None:
                copy.wait_send()
            else:
                pl.when(when)(copy.wait_send)


def signal(barrier, device):
    pl.semaphore_signal(barrier, inc=1, device_id=device, device_id_type=MESH)


def dot(left, right):
    return jnp.dot(left, right, preferred_element_type=F32)


def dot_nt(left, right):
    return lax.dot_general(left, right, (((1,), (1,)), ((), ())), preferred_element_type=F32)


SENDS = 272
RECVS = 272
LOCALS = 16


def layer_kernel(
    tokens, seg, gain_one, gain_two, freq,
    cot, wq, wk, wv, wo, wg, wu, wd,
    gain_o,
    out_o, tok_o, attn_o, wide_o, d_o,
    misc, wqk, wvo, wkv, st, wgu, wdv, acts, da, kv, kc, vc, kt, vt, qs, mask, mixt, mid, gains, trig, lse,
    gua, own, pa, fr, via, dgate, dup, dwd,
    gmt, own_cot, dkv, rkv, gqk,
    rz, sz, rx, ru, su, ruz, sgu, agu, wide, rzd, sdz, rxd, agd, fin,
    xa, sa, rya, ryl, ta, rza, tile, rh, aout,
    vout, vtok, gvec, gpack, gx, gsum, gy, gz, gh,
    ssem, rsem, lsem,
):
    x, y, z, c = coords()
    xl, xh = lax.rem(x, 2), lax.div(x, 2)
    s = xl * 4 + y
    t = 2 * y + c
    core_peer = place(x, y, z, 1 - c)
    net = Net(ssem, rsem, core_peer)

    def of_sequence(k):
        other = lax.rem(s + k, 8)
        return other, place(xh * 2 + lax.div(other, 4), lax.rem(other, 4), z, c)

    def along_z(k):
        return place(x, y, wrap(z + k), c)

    def along_x(k):
        return place(wrap(x + k), y, z, c)

    rows = part_of(s, WR, 16)
    own_rows = part_of(s, ROWS, 16)
    own_tokens = part_of(t, ROWS, 16)
    core_half = part_of(c, 512, 128)

    barrier = pltpu.get_barrier_semaphore()
    for k in range(1, 4):
        signal(barrier, place(x, wrap(y + k), z, c))
        signal(barrier, along_z(k))
    for d in (1, 3):
        for k in range(4):
            signal(barrier, place(wrap(x + d), wrap(y + k), z, c))
        signal(barrier, place(wrap(x + d), y, z, 1 - c))
    for k in range(4):
        signal(barrier, place(wrap(x + 2), wrap(y + k), z, c))
    signal(barrier, core_peer)
    local = [
        pltpu.make_async_copy(wq.at[:, pl.ds(0, 384)], wqk.at[rows, pl.ds(0, 384)], lsem.at[2]),
        pltpu.make_async_copy(wk, wqk.at[rows, pl.ds(384, 128)], lsem.at[3]),
        pltpu.make_async_copy(wq.at[:, pl.ds(384, 512)], wqk.at[rows, pl.ds(512, 512)], lsem.at[4]),
        pltpu.make_async_copy(cot, acts.at[1, own_tokens], lsem.at[5]),
        pltpu.make_async_copy(wk, wkv.at[0, rows], lsem.at[12]),
        pltpu.make_async_copy(wv, wkv.at[1, rows], lsem.at[13]),
    ]
    own_index = 4 * c + z
    own_lanes = part_of(own_index, 128, 128)
    own_v = pltpu.make_async_copy(wv, wvo.at[rows, own_lanes], lsem.at[0])
    own_o = pltpu.make_async_copy(
        wo.at[:, part_of(own_index - jnp.where(own_index > 3, 1, 0), 128, 128)], wvo.at[rows, own_lanes], lsem.at[0]
    )
    pl.when(own_index == 3)(own_v.start)
    pl.when(own_index != 3)(own_o.start)
    for copy in local:
        copy.start()
    sender = xl == lax.div(z, 2)
    own_gate = pltpu.make_async_copy(wg, wide.at[0], lsem.at[6])
    own_up = pltpu.make_async_copy(wu, wide.at[0], lsem.at[6])
    pl.when(sender & (lax.rem(z, 2) == 0))(own_gate.start)
    pl.when(sender & (lax.rem(z, 2) == 1))(own_up.start)
    own_down = pltpu.make_async_copy(wd, wdv, lsem.at[7])
    pl.when(c == xl)(own_down.start)

    misc[s] = jnp.zeros((8, 128), F32)
    misc[s, 0:1, 0:WR] = gain_one[...].astype(F32)
    misc[s, 1:2, 0:WR] = gain_two[...].astype(F32)
    misc[s, 2:3, :] = seg[...].astype(F32)

    pl.semaphore_wait(barrier, 21)

    ms, mr = net.pair(7)
    for k in range(1, 8):
        net.go(misc.at[s], misc.at[s], ms(k - 1), mr(k - 1), of_sequence(k)[1])

    for copy in local[4:6]:
        copy.wait()
    es, er = net.pair(7)
    for k in range(1, 8):
        net.go(wkv.at[c, rows], wkv.at[c, rows], es(k - 1), er(k - 1), of_sequence(k)[1])

    pl.when(own_index == 3)(own_v.wait)
    pl.when(own_index != 3)(own_o.wait)
    os_, or_ = net.pair(7)
    for k in range(1, 8):
        part = wvo.at[rows, own_lanes]
        net.go(part, part, os_(k - 1), or_(k - 1), of_sequence(k)[1])

    pl.when(sender & (lax.rem(z, 2) == 0))(own_gate.wait)
    pl.when(sender & (lax.rem(z, 2) == 1))(own_up.wait)

    for core in range(2):

        @pl.when(sender & (c == core))
        def _():
            for k in range(4):
                st[k] = wide[0, :, FC * (4 * core + k) : FC * (4 * core + k + 1)]

    matrix = lax.rem(z, 2)
    gs, gr = net.pair(8)
    for d in range(2):
        for k in range(4):
            if d == 0 and k == 0:
                continue
            target = place(xh * 2 + lax.rem(xl + d, 2), wrap(y + k), z, c)
            block = st.at[wrap(y + k)]
            net.go(block, wgu.at[matrix, rows], gs(4 * d + k), gr(4 * d + k), target, when=sender)

    @pl.when(sender)
    def _():
        wgu[matrix, rows] = st[y]

    for copy in local[0:3]:
        copy.wait()
    qs_s, qs_r = net.pair(11)
    for k in range(1, 4):
        part = wqk.at[rows, core_half]
        net.go(part, part, qs_s(k - 1), qs_r(k - 1), place(x, wrap(y + k), z, c))
    for k in range(4):
        for d in range(2):
            part = wqk.at[rows, part_of(2 * c + d, 256, 128)]
            i = 3 + 2 * k + d
            net.go(part, part, qs_s(i), qs_r(i), place(wrap(x + 1 - 2 * d), wrap(y + k), z, c))

    for k in range(1, 8):

        @pl.when(s + k < 8)
        def _():
            kv[part_of(s + k, ROWS, 16)] = jnp.zeros((ROWS, 256), BF16)

        @pl.when(k <= s)
        def _():
            rkv[k - 1] = jnp.zeros((ROWS, 256), BF16)

    def block_rows(k):
        return part_of(4 * lax.div(z, 2) + wrap(y - k), WR, 16)

    gz_s, gz_r = net.pair(12)

    def block_along_z(k):
        part = wgu.at[matrix, block_rows(k)]
        for to in range(1, 4):
            net.go(part, part, gz_s(4 * to + k - 4), gz_r(4 * to + k - 4), along_z(to))

    net.landed(wgu.at[0, rows], gr(4), when=jnp.logical_not(sender))
    block_along_z(0)

    for k in range(1, 8):
        net.landed(wvo.at[rows, own_lanes], or_(k - 1))
    oz_s, oz_r = net.pair(3)
    for k in range(1, 4):
        part = wvo.at[:, own_lanes]
        net.go(part, part, oz_s(k - 1), oz_r(k - 1), along_z(k))

    tok = tokens[...].astype(F32)
    unit = tok * lax.rsqrt(jnp.mean(tok * tok, axis=-1, keepdims=True) + EPS)

    for k in range(1, 8):
        net.landed(misc.at[0], mr(k - 1))
    for k in range(8):
        gains[0:8, WR * k : WR * (k + 1)] = misc[k, 0:8, 0:WR]
    numbers = misc[:, 2, :]
    zeros = jnp.sum(jnp.where(numbers < 0.5, 1.0, 0.0), keepdims=True)
    ones = jnp.sum(jnp.where((numbers > 0.5) & (numbers < 1.5), 1.0, 0.0), keepdims=True)
    own_numbers = misc[s, 2:3, :]
    begin = jnp.where(own_numbers < 0.5, 0.0, jnp.where(own_numbers < 1.5, zeros, zeros + ones))
    lane = lax.broadcasted_iota(jnp.int32, (1, ROWS), 1) + s * ROWS
    angle = freq[...] * (lane.astype(F32) - begin)
    trig[0] = jnp.cos(angle)
    trig[1] = jnp.sin(angle)
    key_place = lax.broadcasted_iota(jnp.int32, (LENGTH, ROWS), 0)
    allowed = (key_place >= begin.astype(jnp.int32)) & (key_place <= lane)
    mask[...] = jnp.where(allowed, 0.0, -1e30)
    normed = (unit * gains[0:1, :]).astype(BF16)
    normed_t = jnp.transpose(normed)

    ef_s, ef_r = net.pair(7)
    for k in range(1, 8):
        part = wkv.at[c, part_of(lax.rem(s + 8 - k, 8), WR, 16)]
        net.landed(part, er(k - 1))
        net.go(part, part, ef_s(k - 1), ef_r(k - 1), core_peer)
    for k in range(1, 8):
        net.landed(wkv.at[c, rows], ef_r(k - 1))
    cosine, sine = trig[0], trig[1]

    def rotated(raw, at):
        first = raw[at : at + 32]
        second = raw[at + 32 : at + 64]
        return first * cosine - second * sine, second * cosine + first * sine

    raw_keys = jnp.transpose(dot(normed, wkv[0]))
    keys = jnp.concatenate([*rotated(raw_keys, 0), *rotated(raw_keys, HD)], axis=0)
    kv[own_rows, 0:128] = jnp.transpose(keys).astype(BF16)
    kv[own_rows, 128:256] = dot(normed, wkv[1]).astype(BF16)

    ks, kr = net.pair(7)
    for k in range(1, 8):
        net.go(kv.at[own_rows], kv.at[own_rows], ks(k - 1), kr(k - 1), of_sequence(k)[1], when=s + k < 8)

    is_far = jnp.where(sender, 0, 1)
    for k in range(1, 4):
        net.landed(wgu.at[0, rows], gr(4 * is_far + k))
        block_along_z(k)

    ds_, dr = net.sends(1), net.recvs(2)
    half = part_of(c, FH, 16)
    net.go(wd.at[half], wdv.at[half], ds_(0), dr(c), place(wrap(x + 1 - 2 * c), y, z, xl))

    def gather_tokens(which):
        ts, tr = net.pair(3)
        part = acts.at[which, own_tokens]
        for k in (1, 3, 2):
            net.go(part, part, ts(k - 1), tr(k - 1), place(x, wrap(y + k), z, c))
        return tr

    local[3].wait()
    cot_r = gather_tokens(1)

    qf_s, qf_r = net.pair(11)
    for i in range(11):
        if i < 3:
            part = wqk.at[part_of(xl * 4 + wrap(y - (i + 1)), WR, 16), core_half]
        else:
            k, d = divmod(i - 3, 2)
            part = wqk.at[part_of((1 - xl) * 4 + wrap(y - k), WR, 16), part_of(2 * c + d, 256, 128)]
        net.landed(part, qs_r(i))
        net.go(part, part, qf_s(i), qf_r(i), core_peer)

    for i in range(11):
        net.landed(wqk.at[rows, pl.ds(0, 512 if i < 3 else 256)], qf_r(i))
    raw = jnp.transpose(dot(normed, wqk[...]))
    for head in range(H):
        kv_head, j = divmod(head, GROUP)
        first, second = rotated(raw, HD * head + (128 if head > 5 else 0))
        qs[kv_head, 0:32, ROWS * j : ROWS * (j + 1)] = (first * SCALE).astype(BF16)
        qs[kv_head, 32:64, ROWS * j : ROWS * (j + 1)] = (second * SCALE).astype(BF16)

    for k in range(1, 8):
        net.landed(kv.at[own_rows], kr(k - 1), when=s - k >= 0)
    for head in range(KVH):
        keys = kv[:, HD * head : HD * (head + 1)]
        values = kv[:, 128 + HD * head : 128 + HD * (head + 1)]
        kc[head] = keys
        vc[head] = values
        kt[head] = jnp.transpose(keys)
        vt[head] = jnp.transpose(values)

    def attend(head, j, width):
        lanes = part_of(j, ROWS, 128) if width == 1 else pl.ds(pl.multiple_of(ROWS * j, 256), 2 * ROWS)
        raw_scores = dot(kc[head], qs[head, :, lanes])
        parts = []
        for i in range(width):
            scores = raw_scores[:, ROWS * i : ROWS * (i + 1)] + mask[...]
            highest = jnp.max(scores, axis=0, keepdims=True)
            weights = jnp.exp(scores - highest)
            total = jnp.sum(weights, axis=0, keepdims=True)
            parts.append((weights * (1.0 / total)).astype(BF16))
            lse[GROUP * head + j + i] = jnp.broadcast_to(highest + jnp.log(total), (8, ROWS))
        heads = dot(vt[head], jnp.concatenate(parts, axis=1) if width == 2 else parts[0])
        for i in range(width):
            mixt[part_of(GROUP * head + j + i, HD, HD)] = heads[:, ROWS * i : ROWS * (i + 1)]

    for p in range(GROUP // 2):
        for head in range(KVH):
            attend(head, 2 * p, 2)
    for head in range(KVH):
        attend(head, GROUP - 1, 1)

    of_s, of_r = net.pair(4)
    for k in range(4):
        part = wvo.at[:, part_of(4 * c + wrap(z - k), 128, 128)]
        if k:
            net.landed(part, oz_r(k - 1))
        net.go(part, part, of_s(k), of_r(k), core_peer)
    for k in range(4):
        net.landed(wvo.at[:, own_lanes], of_r(k))
    attended_t = mixt[...].astype(BF16)
    attended = jnp.transpose(mixt[...]).astype(BF16)
    middle = tokens[...].astype(F32) + jnp.concatenate(
        [dot(attended, wvo[:, 0:384]), dot(attended, wvo[:, 512:1024])], axis=1
    )
    mid[...] = middle
    factor = lax.rsqrt(jnp.mean(middle * middle, axis=-1, keepdims=True) + EPS)
    acts[0, own_tokens] = (middle * factor * gains[1:2, :]).astype(BF16)

    n2_r = gather_tokens(0)

    def forward(which, off, send, recv):
        part = acts.at[which, part_of(2 * wrap(y - off) + c, ROWS, 16)]
        return remote(part, part, send(off), recv(off), core_peer)

    nf_s, nf_r = net.pair(4)
    cf_s, cf_r = net.pair(4)
    forward(0, 0, nf_s, nf_r).start()
    for off in (0, 1, 3, 2):
        if off:
            net.landed(acts.at[1, own_tokens], cot_r(off - 1))
        forward(1, off, cf_s, cf_r).start()
    pl.when(c == xl)(own_down.wait)
    for i in range(2):
        net.landed(wdv.at[pl.ds(FH * i, FH)], dr(i), when=c != xl)
    for i in range(12):
        net.landed(wgu.at[0, rows], gz_r(i))

    xsend, xrecv = net.pair(4)
    psend, precv = net.sends(8), net.recvs(6)
    vsend, vrecv = net.pair(2)

    def offset(k):
        return k

    def exchange(off):
        block = part_of(off, 256, 256)
        return remote(pa.at[0, block], pa.at[1, block], xsend(off), xrecv(off), core_peer)

    def part_copy(slot, core):
        off = (0, 1, 3)[slot]
        return remote(
            pa.at[0, pl.ds(256 * off + ROWS * core, ROWS)], fr.at[c, slot], psend(2 * slot + core),
            precv(3 * c + slot), place(x, wrap(y - off), z, core),
        )

    def through(side):
        rows_of = pl.ds(512 + ROWS * side, ROWS)
        return remote(pa.at[0, rows_of], via.at[side], vsend(side), vrecv(side), place(x, wrap(y - 1 + 2 * side), z, c))

    def add_cores(off):
        exchange(off).wait()
        block = pl.ds(256 * off, 256)
        total = own[(0, 1, 0, 2)[off]] + pa[1, block].astype(F32)
        if off % 2:
            side = off // 2
            through(side).wait_recv()
            half_of = slice(ROWS * side, ROWS * (side + 1))
            other = slice(ROWS * (1 - side), ROWS * (2 - side))
            pa[0, pl.ds(256 * off + ROWS * (1 - side), ROWS)] = total[other].astype(BF16)
            pa[0, pl.ds(256 * off + ROWS * side, ROWS)] = (total[half_of] + via[side].astype(F32)).astype(BF16)
        else:
            pa[0, block] = total.astype(BF16)

    def to_owners(off):
        add_cores(off)
        for core in range(2):
            if off == 2:
                through(core).start()
            elif off:
                part_copy(off - off // 3, core).start()
            else:

                @pl.when(c == core)
                def _():
                    fr[core, 0] = pa[0, ROWS * core : ROWS * (core + 1)]

                pl.when(c != core)(part_copy(0, core).start)

    @pl.loop(0, 4)
    def _(k):
        net.landed(acts.at[0, own_tokens], nf_r(offset(k)))
        net.landed(acts.at[1, own_tokens], cf_r(offset(k)))
        off = offset(k)
        block = part_of(wrap(y - off), 256, 256)
        normed_two = acts[0, block]
        cotangent = acts[1, block]
        gate = dot(normed_two, wgu[0])
        up = dot(normed_two, wgu[1])
        grad_hidden = dot_nt(cotangent, wdv[...])
        opening = 1.0 / (1.0 + jnp.exp(-gate))
        act = gate * opening
        hidden = (act * up).astype(BF16)
        grad_gate = (grad_hidden * up * opening * (1.0 + gate * (1.0 - opening))).astype(BF16)
        grad_up = (grad_hidden * act).astype(BF16)
        gua[0, block] = grad_gate
        gua[1, block] = grad_up
        da[1, 0:FC, block] = jnp.transpose(hidden)
        da[0, :, block] = jnp.transpose(normed_two)

        @pl.when(k < 3)
        def _():
            after = offset(k + 1)
            net.landed(acts.at[0, own_tokens], n2_r(after - 1))
            forward(0, after, nf_s, nf_r).start()

        pl.when(k == 1)(lambda: to_owners(0))
        pl.when((k == 3) & (c == 1))(lambda: to_owners(2))

        out_part = dot(hidden, wdv[...])
        grad_part = dot_nt(grad_gate, wgu[0]) + dot_nt(grad_up, wgu[1])
        own[off - 2 * lax.div(off, 2) + lax.div(off, 3)] = jnp.where(c == 0, out_part, grad_part)
        pa[0, part_of(off, 256, 256)] = jnp.where(c == 0, grad_part, out_part).astype(BF16)
        exchange(off).start()

    for off in range(4):
        forward(0, off, nf_s, nf_r).wait_send()
        forward(1, off, cf_s, cf_r).wait_send()
    net.drain()
    pl.when(c == 0)(lambda: to_owners(2))

    def gradient(matrix_, store):
        shift = y + 2 * matrix_
        for h in range(2):
            tall = dot(da[0, 448 * h : 448 * (h + 1)], gua[matrix_]).astype(BF16)
            for k in range(4):
                store[h, wrap(k - shift)] = tall[WR * k : WR * (k + 1)]

    gradient(0, dgate)
    zs, zr = net.pair(3)
    for k in range(1, 4):
        net.go(dgate.at[:, wrap(z + k)], rz.at[k - 1], zs(k - 1), zr(k - 1), along_z(k))
    gradient(1, dup)
    us, ur = net.pair(3)
    for k in range(1, 4):
        part = dup.at[lax.rem(xl + k, 2), pl.ds(2 * lax.div(wrap(x + k), 2), 2)]
        net.go(part, ru.at[k - 1], us(k - 1), ur(k - 1), along_x(k))

    @pl.when(c == 1)
    def _():
        to_owners(1)
        to_owners(3)

    for h in range(2):
        tall = dot(da[1, FH * h : FH * (h + 1)], acts[1]).astype(BF16)
        for i in range(7):
            q = 7 * h + i
            dwd[q // 4, q % 4] = tall[:, 128 * i : 128 * (i + 1)]
    for q in (14, 15):
        dwd[q // 4, q % 4] = jnp.zeros((FH, 128), BF16)

    zds, zdr = net.pair(3)
    for k in range(1, 4):
        net.go(dwd.at[:, wrap(z + k)], rzd.at[k - 1], zds(k - 1), zdr(k - 1), along_z(k))

    own_cot[...] = acts[1, own_tokens]

    @pl.loop(0, GROUP)
    def _(j):
        lanes = part_of(j, ROWS, 128)
        for head in range(KVH):
            scores = dot(kc[head], qs[head, :, lanes]) + mask[...]
            acts[head, :, lanes] = jnp.exp(scores - lse[GROUP * head + j, 0:1, :]).astype(BF16)

    def landed_parts(kind):
        for slot in range(3):
            net.landed(fr.at[kind, slot], precv(3 * kind + slot), when=None if slot else c != kind)
        return fr[kind, 0].astype(F32) + fr[kind, 1].astype(F32) + fr[kind, 2].astype(F32)

    @pl.when(c == 0)
    def _():
        to_owners(1)
        to_owners(3)

    grad_normed = landed_parts(1)
    middle = mid[...]
    own[0, 0:ROWS] = middle
    factor = lax.rsqrt(jnp.mean(middle * middle, axis=-1, keepdims=True) + EPS)
    unit_two = middle * factor
    scaled = grad_normed * gains[1:2, :]
    gvec[...] = jnp.broadcast_to(jnp.sum(grad_normed * unit_two, axis=0, keepdims=True), (8, D))
    grad_middle = own_cot[...].astype(F32) + factor * (
        scaled - unit_two * jnp.mean(scaled * unit_two, axis=-1, keepdims=True)
    )
    mid[...] = grad_middle

    branch = grad_middle.astype(BF16)
    grad_mixed = jnp.transpose(
        dot_nt(branch[:, 0:384], wvo[:, 0:384]) + dot_nt(branch[:, 384:D], wvo[:, 512:1024])
    )
    for head in range(H):
        kv_head, j = divmod(head, GROUP)
        gmt[kv_head, :, ROWS * j : ROWS * (j + 1)] = grad_mixed[HD * head : HD * (head + 1)].astype(BF16)
    grad_out = dot(attended_t, branch).astype(BF16)
    da[1, :, 0:384] = grad_out[:, 0:384]
    da[1, :, 512:1024] = grad_out[:, 384:D]
    first_of_peer = pl.ds(pl.multiple_of(512 * (1 - c), 128), 384)
    last_of_peer = pl.ds(pl.multiple_of(512 * (1 - c) + 384, 128), 128)
    first_own = pl.ds(pl.multiple_of(512 * c, 128), 384)
    last_own = pl.ds(pl.multiple_of(512 * c + 384, 128), 128)
    firsts, lasts_ = pl.ds(0, 384), pl.ds(384, 128)
    xas, xar = net.pair(5)
    net.go(da.at[1, :, first_of_peer], xa.at[1, :, firsts], xas(1), xar(1), core_peer)
    net.go(da.at[1, :, last_of_peer], xa.at[1, :, lasts_], xas(3), xar(3), core_peer, when=c == 0)

    for slot in range(3):
        for core in range(2):
            if slot:
                part_copy(slot, core).wait_send()
            else:
                pl.when(c != core)(part_copy(slot, core).wait_send)
    for side in range(2):
        through(side).wait_send()

    def to_rows_owners(i, lanes, sems):
        for k in range(1, 4):
            other = part_of(xl * 4 + wrap(y + k), WR, 16)
            net.go(
                sa.at[i, other, lanes], rya.at[i, 0, k - 1, :, lanes], sems[0](k - 1), sems[1](k - 1),
                place(x, wrap(y + k), z, c),
            )

    def to_rows_owners_across(i, half_size, sems):
        for k in range(4):
            other = part_of((1 - xl) * 4 + wrap(y + k), WR, 16)
            for d, cut in enumerate(half_size):
                net.go(
                    sa.at[i, other, cut], rya.at[i, 1, k, :, cut], sems[0](3 + 2 * k + d), sems[1](3 + 2 * k + d),
                    place(wrap(x + 1 - 2 * d), wrap(y + k), z, c),
                )

    def from_rows_owners(i, lanes, half_size, sems):
        for k in range(1, 4):
            net.landed(rya.at[i, 0, k - 1, :, lanes], sems[1](k - 1))
        for k in range(4):
            for d, cut in enumerate(half_size):
                net.landed(rya.at[i, 1, k, :, cut], sems[1](3 + 2 * k + d))

    def last_tile(i, when):
        net.landed(xa.at[i, :, lasts_], xar(2 + i), when=when)

        @pl.when(when)
        def _():
            sa[i, :, 384:512] = (da[i, :, last_own].astype(F32) + xa[i, :, 384:512].astype(F32)).astype(BF16)

        for k in range(1, 8):
            far = k > 3
            other = (1 - xl if far else xl) * 4 + wrap(y + k)
            target = place(wrap(x + (1 - 2 * i if far else 0)), wrap(y + k), z, c)
            part = sa.at[i, part_of(other, WR, 16), lasts_]
            net.go(part, ryl.at[i, k - 1], yl[i][0](k - 1), yl[i][1](k - 1), target, when=when)

    first_cuts = ((pl.ds(0, 256), pl.ds(256, 128)), (pl.ds(0, 128), pl.ds(128, 256)))
    yf = [net.pair(11), net.pair(11)]
    yl = [net.pair(7), net.pair(7)]
    net.landed(xa.at[1, :, firsts], xar(1))
    sa[1, :, 0:384] = (da[1, :, first_own].astype(F32) + xa[1, :, 0:384].astype(F32)).astype(BF16)
    to_rows_owners(1, firsts, yf[1])


    for k in range(1, 4):
        net.landed(ru.at[k - 1], ur(k - 1))
    for i in range(2):
        su[i] = (
            dup[xl, 2 * xh + i].astype(F32) + ru[0, i].astype(F32) + ru[1, i].astype(F32) + ru[2, i].astype(F32)
        ).astype(BF16)
    vs, vr = net.sends(2), net.recvs(4)
    for i in range(2):
        target = 2 * xh + i
        net.go(su.at[i], ruz.at[z], vs(i), vr(z), place(x, y, target, c), when=z != target)
    for k in range(1, 4):
        net.landed(rz.at[k - 1], zr(k - 1))
    for i in range(2):
        sz[i] = (
            dgate[i, z].astype(F32) + rz[0, i].astype(F32) + rz[1, i].astype(F32) + rz[2, i].astype(F32)
        ).astype(BF16)
    xs_s, xs_r = net.pair(3)
    for k in range(1, 4):
        net.go(sz.at[lax.rem(xl + k, 2)], rx.at[k - 1], xs_s(k - 1), xs_r(k - 1), along_x(k))

    def attend_back(head, j, width):
        lanes = part_of(j, ROWS, 128) if width == 1 else pl.ds(pl.multiple_of(ROWS * j, 256), 2 * ROWS)
        probs = acts[head, :, lanes].astype(F32)
        grad_probs = dot(vc[head], gmt[head, :, lanes])
        delta = jnp.sum(grad_probs * probs, axis=0, keepdims=True)
        grad_scores = (probs * (grad_probs - delta)).astype(BF16)
        pa[head, :, lanes] = grad_scores
        both = dot(kt[head], grad_scores) * SCALE
        cosine, sine = trig[0], trig[1]
        for i in range(width):
            rot = both[:, ROWS * i : ROWS * (i + 1)]
            at = HD * (GROUP * head + j + i)
            mixt[pl.ds(pl.multiple_of(at, 32), 32)] = rot[0:32] * cosine + rot[32:64] * sine
            mixt[pl.ds(pl.multiple_of(at + 32, 32), 32)] = rot[32:64] * cosine - rot[0:32] * sine

    kvs, kvr = net.pair(14)
    for head in range(KVH):
        for p in range(GROUP // 2):
            attend_back(head, 2 * p, 2)
        attend_back(head, GROUP - 1, 1)
        dkv[:, 128 * head : 128 * head + HD] = dot_nt(pa[head], qs[head]).astype(BF16)
        dkv[:, 128 * head + HD : 128 * (head + 1)] = dot_nt(acts[head], gmt[head]).astype(BF16)
        for k in range(1, 8):
            other, target = of_sequence(k)
            lanes = pl.ds(128 * head, 128)
            i = 7 * head + k - 1
            net.go(
                dkv.at[part_of(other, ROWS, 16), lanes], rkv.at[k - 1, :, lanes], kvs(i), kvr(i), target, when=s + k >= 8
            )

    vout[...] = (own[0, 0:ROWS] + landed_parts(0)).astype(BF16)
    out_copy = pltpu.make_async_copy(vout, out_o, lsem.at[14])
    out_copy.start()

    grad_query = jnp.transpose(mixt[...]).astype(BF16)
    gqk[:, 0:384] = grad_query[:, 0:384]
    gqk[:, 512:1024] = grad_query[:, 384:D]
    part = dot(normed_t, grad_query).astype(BF16)
    da[0, :, 0:384] = part[:, 0:384]
    da[0, :, 512:1024] = part[:, 384:D]
    net.go(da.at[0, :, first_of_peer], xa.at[0, :, firsts], xas(0), xar(0), core_peer)
    net.go(da.at[0, :, last_of_peer], xa.at[0, :, lasts_], xas(2), xar(2), core_peer, when=c == 0)

    for k in range(1, 4):
        net.landed(rx.at[k - 1], xs_r(k - 1))
    sgu[0] = (
        sz[xl].astype(F32) + rx[0].astype(F32) + rx[1].astype(F32) + rx[2].astype(F32)
    ).astype(BF16)
    own_block = 4 * c + y
    held = [4 * c + wrap(y - z), 4 * c + wrap(y - z - 2)]
    ags, agr = net.pair(4)
    net.go(sgu.at[0], agu.at[0, own_block], ags(0), agr(0), place(x, wrap(y + z), z, c), when=z != 0)

    @pl.when(z == 0)
    def _():
        agu[0, own_block] = sgu[0]

    cosine, sine = trig[0], trig[1]
    back, grad_values = [], []
    for head in range(KVH):
        lanes = slice(128 * head, 128 * (head + 1))
        total = dkv[own_rows, lanes].astype(F32)
        for k in range(1, 8):
            net.landed(rkv.at[k - 1, :, pl.ds(0, 128)], kvr(7 * head + k - 1), when=k > s)
            total = total + rkv[k - 1, :, lanes].astype(F32)
        keys = jnp.transpose(total)
        first, second = keys[0:32], keys[32:64]
        back += [first * cosine + second * sine, second * cosine - first * sine]
        grad_values.append(total[:, HD:128])
    grad_key = jnp.transpose(jnp.concatenate(back, axis=0)).astype(BF16)
    gqk[:, 384:512] = grad_key
    grad_value = jnp.concatenate(grad_values, axis=1).astype(BF16)
    da[0, :, 384:512] = dot(normed_t, grad_key).astype(BF16)
    da[1, :, 384:512] = dot(normed_t, grad_value).astype(BF16)
    for i in range(2):
        net.go(da.at[i, :, last_of_peer], xa.at[i, :, lasts_], xas(2 + i), xar(2 + i), core_peer, when=c == 1)

    net.landed(xa.at[0, :, firsts], xar(0))
    sa[0, :, 0:384] = (da[0, :, first_own].astype(F32) + xa[0, :, 0:384].astype(F32)).astype(BF16)
    to_rows_owners_across(1, first_cuts[1], yf[1])
    to_rows_owners(0, firsts, yf[0])
    to_rows_owners_across(0, first_cuts[0], yf[0])
    last_tile(1, c == 1)
    last_tile(0, c == 1)

    grad_normed = dot_nt(gqk[...], wqk[...]) + dot_nt(grad_value, wvo[:, 384:512])
    tok = tokens[...].astype(F32)
    factor = lax.rsqrt(jnp.mean(tok * tok, axis=-1, keepdims=True) + EPS)
    unit = tok * factor
    scaled = grad_normed * gains[0:1, :]
    vtok[...] = mid[...] + factor * (scaled - unit * jnp.mean(scaled * unit, axis=-1, keepdims=True))
    tok_copy = pltpu.make_async_copy(vtok, tok_o, lsem.at[15])
    tok_copy.start()
    gvec[0:1, :] = jnp.sum(grad_normed * unit, axis=0, keepdims=True)
    for row in range(2):
        for i in range(7):
            gpack[7 * row + i : 7 * row + i + 1, :] = gvec[row : row + 1, 128 * i : 128 * (i + 1)]
    net.go(gpack, gx, xas(4), xar(4), core_peer)

    for i in range(2):
        last_tile(i, c == 0)
    net.landed(gx, xar(4))
    gsum[...] = gpack[...] + gx[...]
    gys, gyr = net.pair(7)
    for k in range(1, 8):
        net.go(gsum, gy.at[k - 1], gys(k - 1), gyr(k - 1), of_sequence(k)[1])

    owner = xh == lax.div(z, 2)
    for k in range(4):
        net.landed(su.at[0], vr(k), when=owner & (z != k))
    ucs, ucr = net.pair(1)
    uhs = net.sends(1)

    @pl.when(owner)
    def _():
        ruz[z] = su[lax.rem(z, 2)]
        sgu[1] = (
            ruz[0].astype(F32) + ruz[1].astype(F32) + ruz[2].astype(F32) + ruz[3].astype(F32)
        ).astype(BF16)

    net.go(sgu.at[1], agu.at[1, own_block], ucs(0), ucr(0), place(x, wrap(y + z + 2), z, c), when=owner & (z != 2))
    net.go(sgu.at[1], agu.at[1, own_block], uhs(0), ucr(0), place(wrap(x + 2), wrap(y + z + 2), z, c), when=owner)

    @pl.when(owner & (z == 2))
    def _():
        agu[1, own_block] = sgu[1]

    for k in range(1, 4):
        net.landed(rzd.at[k - 1], zdr(k - 1))
    for i in range(4):
        sdz[i] = (
            dwd[i, z].astype(F32) + rzd[0, i].astype(F32) + rzd[1, i].astype(F32) + rzd[2, i].astype(F32)
        ).astype(BF16)
    xds, xdr = net.pair(3)
    for k in range(1, 4):
        net.go(sdz, rxd.at[k - 1], xds(k - 1), xdr(k - 1), along_x(k), when=lax.rem(xl + k, 2) == c)


    afs, afr = net.pair(8)

    def spread(matrix_, sends, recvs):
        for k in range(1, 4):
            net.go(agu.at[matrix_, held[matrix_]], agu.at[matrix_, held[matrix_]], sends(k), recvs(k), along_z(k))
        part = agu.at[matrix_, held[matrix_]]
        net.go(part, part, afs(4 * matrix_), afr(4 * matrix_), core_peer)

    net.landed(agu.at[0, held[0]], agr(0), when=z != 0)
    spread(0, ags, agr)

    zas2, zar2 = net.pair(6)
    for i in range(2):
        from_rows_owners(i, firsts, first_cuts[i], yf[i])
        total = sa[i, rows, 0:384].astype(F32)
        for k in range(3):
            total = total + rya[i, 0, k, :, 0:384].astype(F32)
        for k in range(4):
            total = total + rya[i, 1, k, :, 0:384].astype(F32)
        ta[i, :, 0:384] = total.astype(BF16)
        total = sa[i, rows, 384:512].astype(F32)
        for k in range(1, 8):
            net.landed(ryl.at[i, k - 1], yl[i][1](k - 1))
            total = total + ryl[i, k - 1].astype(F32)
        ta[i, :, 384:512] = total.astype(BF16)
    for k in range(1, 4):
        net.go(ta.at[:, :, part_of(wrap(z + k), 128, 128)], rza.at[k - 1], zas2(k - 1), zar2(k - 1), along_z(k))
    total = gsum[...]
    for k in range(1, 8):
        net.landed(gy.at[k - 1], gyr(k - 1))
        total = total + gy[k - 1]
    gz[3] = total
    for k in range(1, 4):
        net.go(gz.at[3], gz.at[k - 1], zas2(k + 2), zar2(k + 2), along_z(k))

    uas, uar = net.pair(4)
    net.landed(agu.at[1, held[1]], ucr(0), when=jnp.logical_not(owner) | (z != 2))
    spread(1, uas, uar)

    for k in range(1, 4):
        net.landed(rxd.at[k - 1], xdr(k - 1), when=xl == c)
    zas, zar = net.pair(3)

    @pl.when(xl == c)
    def _():
        for i in range(4):
            agd[i, z] = (
                sdz[i].astype(F32) + rxd[0, i].astype(F32) + rxd[1, i].astype(F32) + rxd[2, i].astype(F32)
            ).astype(BF16)

    for k in range(1, 4):
        net.go(agd.at[:, z], agd.at[:, z], zas(k - 1), zar(k - 1), along_z(k), when=xl == c)

    for k in range(1, 4):
        net.landed(rza.at[k - 1], zar2(k - 1))
    tile[...] = (
        ta[:, :, part_of(z, 128, 128)].astype(F32)
        + rza[0].astype(F32) + rza[1].astype(F32) + rza[2].astype(F32)
    ).astype(BF16)
    total = gz[3]
    for k in range(1, 4):
        net.landed(gz.at[k - 1], zar2(k + 2))
        total = total + gz[k - 1]
    gh[1] = total
    hs, hr = net.pair(2)
    net.go(tile, rh, hs(0), hr(0), along_x(2))
    net.go(gh.at[1], gh.at[0], hs(1), hr(1), along_x(2))

    net.landed(rh, hr(0))
    own_tile = aout.at[:, :, own_lanes]
    aout[:, :, own_lanes] = (tile[...].astype(F32) + rh[...].astype(F32)).astype(BF16)
    lasts, lastr = net.pair(3)
    for k in range(1, 4):
        net.go(own_tile, own_tile, lasts(k - 1), lastr(k - 1), along_z(k))
    net.landed(gh.at[0], hr(1))
    gpack_sum = gh[0] + gh[1]
    gain_o[...] = jnp.zeros_like(gain_o)
    for row in range(2):
        for i in range(7):
            gain_o[row : row + 1, 128 * i : 128 * (i + 1)] = gpack_sum[7 * row + i : 7 * row + i + 1]

    net.drain()
    out_copy.wait()
    tok_copy.wait()

    outs = [
        pltpu.make_async_copy(aout, attn_o, lsem.at[9]),
        pltpu.make_async_copy(wide.at[0], wide_o.at[0], lsem.at[10]),
        pltpu.make_async_copy(wide.at[1], wide_o.at[1], lsem.at[11]),
    ]

    def to_other_core(matrix_, recvs):
        for k in (1, 3, 2):
            part = agu.at[matrix_, 4 * c + wrap(y - wrap(z - k) - 2 * matrix_)]
            net.landed(part, recvs(k))
            net.go(part, part, afs(4 * matrix_ + k), afr(4 * matrix_ + k), core_peer)

    def assemble(matrix_):
        for k in range(4):
            net.landed(agu.at[matrix_, 0], afr(4 * matrix_ + k))
        for k in range(8):
            wide[matrix_, :, FC * k : FC * (k + 1)] = agu[matrix_, k]
        outs[1 + matrix_].start()

    to_other_core(0, agr)
    assemble(0)
    for k in range(1, 4):
        net.landed(agd.at[:, z], zar(k - 1), when=xl == c)
    dfs, dfr = net.pair(1)
    net.go(agd, fin, dfs(0), dfr(0), core_peer, when=xl == c)
    own_sums = pltpu.make_async_copy(agd, d_o, lsem.at[8])
    pl.when(xl == c)(own_sums.start)
    for k in range(1, 4):
        net.landed(own_tile, lastr(k - 1))
    fs, fr_ = net.pair(1)
    part = aout.at[:, :, core_half]
    net.go(part, part, fs(0), fr_(0), core_peer)
    to_other_core(1, uar)
    net.landed(fin, dfr(0), when=xl != c)
    peer_sums = pltpu.make_async_copy(fin, d_o, lsem.at[8])
    pl.when(xl != c)(peer_sums.start)
    net.landed(aout.at[:, :, pl.ds(0, 512)], fr_(0))
    outs[0].start()
    assemble(1)

    net.drain()
    for copy in outs:
        copy.wait()
    pl.when(xl == c)(own_sums.wait)
    pl.when(xl != c)(peer_sums.wait)


def finish_kernel(
    gain_in, out_in, tok_in, attn_in, wide_in, down_in,
    one, two, out, tok, gq, gk, gv, go, gate, up, gdown,
    vout, vtok, gain, attn, wide, down, fq, fk, fv, fo, fgate, fup, fdown, isem, osem,
):
    ins = [
        pltpu.make_async_copy(source, target, isem.at[i])
        for i, (source, target) in enumerate(
            [(wide_in, wide), (down_in, down), (attn_in, attn), (tok_in, vtok), (out_in, vout), (gain_in, gain)]
        )
    ]
    for copy in ins:
        copy.start()
    outs = []

    def store(source, target):
        copy = pltpu.make_async_copy(source, target, osem.at[len(outs)])
        copy.start()
        outs.append(copy)

    ins[0].wait()
    fgate[...] = wide[0].astype(F32)
    store(fgate, gate)
    fup[...] = wide[1].astype(F32)
    store(fup, up)
    ins[1].wait()
    for q in range(14):
        h, i = divmod(q, 7)
        fdown[FH * h : FH * (h + 1), 128 * i : 128 * (i + 1)] = down[q // 4, q % 4].astype(F32)
    store(fdown, gdown)
    ins[2].wait()
    fq[:, 0:384] = attn[0, :, 0:384].astype(F32)
    fq[:, 384:D] = attn[0, :, 512:1024].astype(F32)
    store(fq, gq)
    fo[:, 0:384] = attn[1, :, 0:384].astype(F32)
    fo[:, 384:D] = attn[1, :, 512:1024].astype(F32)
    store(fo, go)
    fk[...] = attn[0, :, 384:512].astype(F32)
    store(fk, gk)
    fv[...] = attn[1, :, 384:512].astype(F32)
    store(fv, gv)
    ins[3].wait()
    store(vtok, tok)
    ins[4].wait()
    store(vout, out)
    ins[5].wait()
    shard = lax.axis_index("shard")
    for k in range(8):

        @pl.when(shard == k)
        def _():
            one[...] = gain[0:1, WR * k : WR * (k + 1)]
            two[...] = gain[1:2, WR * k : WR * (k + 1)]

    for copy in outs:
        copy.wait()


def vmem():
    return pl.BlockSpec(memory_space=pltpu.VMEM)


def anywhere():
    return pl.BlockSpec(memory_space=pl.ANY)


def shape(dims, dtype):
    return jax.ShapeDtypeStruct(dims, dtype)


def body(
    tokens, segments, attn_gain, w_query, w_key, w_value, w_out, ffn_gain, w_gate, w_up, w_down, cotangent
):
    half = HD // 2
    frequency = THETA ** (-(np.arange(half) * 2.0 / HD))
    freq = np.broadcast_to(frequency[:, None], (half, ROWS)).astype(np.float32)
    layer = pl.pallas_call(
        layer_kernel,
        name="layer",
        out_shape=[
            shape((8, D), F32),
            shape((ROWS, D), BF16),
            shape((ROWS, D), F32),
            shape((2, WR, 1024), BF16),
            shape((2, WR, FF), BF16),
            shape((4, 4, FH, 128), BF16),
        ],
        in_specs=[vmem()] * 5 + [anywhere()] * 8,
        out_specs=[vmem()] + [anywhere()] * 5,
        scratch_shapes=[
            pltpu.VMEM((8, 8, 128), F32),
            pltpu.VMEM((D, 1024), BF16),
            pltpu.VMEM((D, 1024), BF16),
            pltpu.VMEM((2, D, 128), BF16),
            pltpu.VMEM((4, WR, FC), BF16),
            pltpu.VMEM((2, D, FC), BF16),
            pltpu.VMEM((FC, D), BF16),
            pltpu.VMEM((2, LENGTH, D), BF16),
            pltpu.VMEM((2, D, LENGTH), BF16),
            pltpu.VMEM((LENGTH, 256), BF16),
            pltpu.VMEM((KVH, LENGTH, HD), BF16),
            pltpu.VMEM((KVH, LENGTH, HD), BF16),
            pltpu.VMEM((KVH, HD, LENGTH), BF16),
            pltpu.VMEM((KVH, HD, LENGTH), BF16),
            pltpu.VMEM((KVH, HD, D), BF16),
            pltpu.VMEM((LENGTH, ROWS), F32),
            pltpu.VMEM((D, ROWS), F32),
            pltpu.VMEM((ROWS, D), F32),
            pltpu.VMEM((8, D), F32),
            pltpu.VMEM((2, half, ROWS), F32),
            pltpu.VMEM((H, 8, ROWS), F32),
            pltpu.VMEM((2, LENGTH, FC), BF16),
            pltpu.VMEM((3, 256, D), F32),
            pltpu.VMEM((2, LENGTH, D), BF16),
            pltpu.VMEM((2, 3, ROWS, D), BF16),
            pltpu.VMEM((2, ROWS, D), BF16),
            pltpu.VMEM((2, 4, WR, FC), BF16),
            pltpu.VMEM((2, 4, WR, FC), BF16),
            pltpu.VMEM((4, 4, FH, 128), BF16),
            pltpu.VMEM((KVH, HD, D), BF16),
            pltpu.VMEM((ROWS, D), BF16),
            pltpu.VMEM((LENGTH, 256), BF16),
            pltpu.VMEM((7, ROWS, 256), BF16),
            pltpu.VMEM((ROWS, 1024), BF16),
            pltpu.VMEM((3, 2, WR, FC), BF16),
            pltpu.VMEM((2, WR, FC), BF16),
            pltpu.VMEM((3, WR, FC), BF16),
            pltpu.VMEM((3, 2, WR, FC), BF16),
            pltpu.VMEM((2, WR, FC), BF16),
            pltpu.VMEM((4, WR, FC), BF16),
            pltpu.VMEM((2, WR, FC), BF16),
            pltpu.VMEM((2, 8, WR, FC), BF16),
            pltpu.VMEM((2, WR, FF), BF16),
            pltpu.VMEM((3, 4, FH, 128), BF16),
            pltpu.VMEM((4, FH, 128), BF16),
            pltpu.VMEM((3, 4, FH, 128), BF16),
            pltpu.VMEM((4, 4, FH, 128), BF16),
            pltpu.VMEM((4, 4, FH, 128), BF16),
            pltpu.VMEM((2, D, 512), BF16),
            pltpu.VMEM((2, D, 512), BF16),
            pltpu.VMEM((2, 2, 4, WR, 384), BF16),
            pltpu.VMEM((2, 7, WR, 128), BF16),
            pltpu.VMEM((2, WR, 512), BF16),
            pltpu.VMEM((3, 2, WR, 128), BF16),
            pltpu.VMEM((2, WR, 128), BF16),
            pltpu.VMEM((2, WR, 128), BF16),
            pltpu.VMEM((2, WR, 1024), BF16),
            pltpu.VMEM((ROWS, D), BF16),
            pltpu.VMEM((ROWS, D), F32),
            pltpu.VMEM((8, D), F32),
            pltpu.VMEM((16, 128), F32),
            pltpu.VMEM((16, 128), F32),
            pltpu.VMEM((16, 128), F32),
            pltpu.VMEM((7, 16, 128), F32),
            pltpu.VMEM((4, 16, 128), F32),
            pltpu.VMEM((2, 16, 128), F32),
            pltpu.SemaphoreType.DMA((SENDS,)),
            pltpu.SemaphoreType.DMA((RECVS,)),
            pltpu.SemaphoreType.DMA((LOCALS,)),
        ],
        compiler_params=pltpu.CompilerParams(
            collective_id=0, has_side_effects=True, vmem_limit_bytes=60 << 20
        ),
    )
    results = layer(
        tokens,
        segments.reshape(1, ROWS),
        attn_gain.reshape(1, WR),
        ffn_gain.reshape(1, WR),
        freq,
        cotangent,
        w_query,
        w_key,
        w_value,
        w_out,
        w_gate,
        w_up,
        w_down,
    )
    finish = pl.pallas_call(
        finish_kernel,
        name="finish",
        out_shape=[
            shape((1, WR), F32),
            shape((1, WR), F32),
            shape((ROWS, D), BF16),
            shape((ROWS, D), F32),
            shape((WR, D), F32),
            shape((WR, 128), F32),
            shape((WR, 128), F32),
            shape((WR, D), F32),
            shape((WR, FF), F32),
            shape((WR, FF), F32),
            shape((FC, D), F32),
        ],
        in_specs=[anywhere()] * 6,
        out_specs=[vmem()] * 2 + [anywhere()] * 9,
        scratch_shapes=[
            pltpu.VMEM((ROWS, D), BF16),
            pltpu.VMEM((ROWS, D), F32),
            pltpu.VMEM((8, D), F32),
            pltpu.VMEM((2, WR, 1024), BF16),
            pltpu.VMEM((2, WR, FF), BF16),
            pltpu.VMEM((4, 4, FH, 128), BF16),
            pltpu.VMEM((WR, D), F32),
            pltpu.VMEM((WR, 128), F32),
            pltpu.VMEM((WR, 128), F32),
            pltpu.VMEM((WR, D), F32),
            pltpu.VMEM((WR, FF), F32),
            pltpu.VMEM((WR, FF), F32),
            pltpu.VMEM((FC, D), F32),
            pltpu.SemaphoreType.DMA((6,)),
            pltpu.SemaphoreType.DMA((9,)),
        ],
        compiler_params=pltpu.CompilerParams(vmem_limit_bytes=62 << 20),
    )
    one, two, out, tok, gq, gk, gv, go, gate, up, down = finish(*results)
    return out, tok, one.reshape(WR), gq, gk, gv, go, two.reshape(WR), gate, up, down


def solution(mesh):
    tokens = P(("replica", "shard"), None)
    weight = P("shard", None)
    return jax.shard_map(
        body,
        mesh=mesh,
        in_specs=(
            tokens, P(("replica", "shard")), P("shard"), weight, weight, weight, weight,
            P("shard"), weight, weight, weight, tokens,
        ),
        out_specs=(
            tokens, tokens, P("shard"), weight, weight, weight, weight, P("shard"), weight, weight, weight,
        ),
        check_vma=False,
    )
```

```python
import jax
import jax.numpy as jnp
import numpy as np
from jax import lax
from jax.experimental import pallas as pl
from jax.experimental.pallas import tpu as pltpu
from jax.sharding import PartitionSpec as P

D = 896
H = 14
HD = 64
KVH = 2
GROUP = H // KVH
FF = 4864
FC = FF // 8
FH = FC // 2
ROWS = 128
LENGTH = 1024
WR = D // 8
EPS = 1e-05
THETA = 10000.0
SCALE = 0.125

F32 = jnp.float32
BF16 = jnp.bfloat16
MESH = pl.DeviceIdType.MESH


def coords():
    replica = lax.axis_index("replica")
    shard = lax.axis_index("shard")
    x = lax.div(replica, 8) * 2 + lax.div(shard, 4)
    return x, lax.rem(shard, 4), lax.rem(lax.div(replica, 2), 4), lax.rem(replica, 2)


def place(x, y, z, core):
    return (lax.div(x, 2) * 8 + z * 2 + core, lax.rem(x, 2) * 4 + y)


def wrap(value):
    return lax.rem(value + 16, 4)


def part_of(index, size, unit):
    return pl.ds(pl.multiple_of(index * size, unit), size)


def remote(src, dst, send, recv, device):
    return pltpu.make_async_remote_copy(
        src_ref=src, dst_ref=dst, send_sem=send, recv_sem=recv, device_id=device, device_id_type=MESH
    )


class Net:
    def __init__(self, ssem, rsem, peer):
        self.ssem, self.rsem, self.peer = ssem, rsem, peer
        self.ns = self.nr = 0
        self.open = []

    def sends(self, count):
        base = self.ns
        self.ns += count
        assert self.ns <= self.ssem.shape[0]
        return lambda index: self.ssem.at[base + index]

    def recvs(self, count):
        base = self.nr
        self.nr += count
        assert self.nr <= self.rsem.shape[0]
        return lambda index: self.rsem.at[base + index]

    def pair(self, count):
        return self.sends(count), self.recvs(count)

    def go(self, src, dst, send, recv, device, when=None):
        copy = remote(src, dst, send, recv, device)
        if when is None:
            copy.start()
        else:
            pl.when(when)(copy.start)
        self.open.append((copy, when))

    def landed(self, ref, recv, when=None):
        copy = remote(ref, ref, self.ssem.at[0], recv, self.peer)
        if when is None:
            copy.wait_recv()
        else:
            pl.when(when)(copy.wait_recv)

    def drain(self):
        done, self.open = self.open, []
        for copy, when in done:
            if when is None:
                copy.wait_send()
            else:
                pl.when(when)(copy.wait_send)


def signal(barrier, device):
    pl.semaphore_signal(barrier, inc=1, device_id=device, device_id_type=MESH)


def dot(left, right):
    return jnp.dot(left, right, preferred_element_type=F32)


def dot_nt(left, right):
    return lax.dot_general(left, right, (((1,), (1,)), ((), ())), preferred_element_type=F32)


SENDS = 272
RECVS = 272
LOCALS = 16


def layer_kernel(
    tokens, seg, gain_one, gain_two, freq,
    cot, wq, wk, wv, wo, wg, wu, wd,
    gain_o,
    vout, vtok, attn_o, wide, d_o,
    misc, wqk, wvo, wkv, st, wgu, wdv, acts, da, kv, kc, vc, kt, vt, qs, mask, mixt, mid, gains, trig, lse,
    gua, own, pa, fr, via, dgate, dup, dwd,
    gmt, own_cot, dkv, rkv, gqk,
    rz, sz, rx, ru, su, ruz, sgu, agu, rzd, sdz, rxd, agd, fin,
    xa, sa, rya, ryl, ta, rza, tile, rh, aout,
    gvec, gpack, gx, gsum, gy, gz, gh,
    ssem, rsem, lsem,
):
    x, y, z, c = coords()
    xl, xh = lax.rem(x, 2), lax.div(x, 2)
    s = xl * 4 + y
    t = 2 * y + c
    core_peer = place(x, y, z, 1 - c)
    net = Net(ssem, rsem, core_peer)

    def of_sequence(k):
        other = lax.rem(s + k, 8)
        return other, place(xh * 2 + lax.div(other, 4), lax.rem(other, 4), z, c)

    def along_z(k):
        return place(x, y, wrap(z + k), c)

    def along_x(k):
        return place(wrap(x + k), y, z, c)

    rows = part_of(s, WR, 16)
    own_rows = part_of(s, ROWS, 16)
    own_tokens = part_of(t, ROWS, 16)
    core_half = part_of(c, 512, 128)

    barrier = pltpu.get_barrier_semaphore()
    for k in range(1, 4):
        signal(barrier, place(x, wrap(y + k), z, c))
        signal(barrier, along_z(k))
    for d in (1, 3):
        for k in range(4):
            signal(barrier, place(wrap(x + d), wrap(y + k), z, c))
        signal(barrier, place(wrap(x + d), y, z, 1 - c))
    for k in range(4):
        signal(barrier, place(wrap(x + 2), wrap(y + k), z, c))
    signal(barrier, core_peer)
    local = [
        pltpu.make_async_copy(wq.at[:, pl.ds(0, 384)], wqk.at[rows, pl.ds(0, 384)], lsem.at[2]),
        pltpu.make_async_copy(wk, wqk.at[rows, pl.ds(384, 128)], lsem.at[3]),
        pltpu.make_async_copy(wq.at[:, pl.ds(384, 512)], wqk.at[rows, pl.ds(512, 512)], lsem.at[4]),
        pltpu.make_async_copy(cot, acts.at[1, own_tokens], lsem.at[5]),
        pltpu.make_async_copy(wk, wkv.at[0, rows], lsem.at[12]),
        pltpu.make_async_copy(wv, wkv.at[1, rows], lsem.at[13]),
    ]
    own_index = 4 * c + z
    own_lanes = part_of(own_index, 128, 128)
    own_v = pltpu.make_async_copy(wv, wvo.at[rows, own_lanes], lsem.at[0])
    own_o = pltpu.make_async_copy(
        wo.at[:, part_of(own_index - jnp.where(own_index > 3, 1, 0), 128, 128)], wvo.at[rows, own_lanes], lsem.at[0]
    )
    pl.when(own_index == 3)(own_v.start)
    pl.when(own_index != 3)(own_o.start)
    for copy in local:
        copy.start()
    sender = xl == lax.div(z, 2)
    own_gate = pltpu.make_async_copy(wg, wide.at[0], lsem.at[6])
    own_up = pltpu.make_async_copy(wu, wide.at[0], lsem.at[6])
    pl.when(sender & (lax.rem(z, 2) == 0))(own_gate.start)
    pl.when(sender & (lax.rem(z, 2) == 1))(own_up.start)
    own_down = pltpu.make_async_copy(wd, wdv, lsem.at[7])
    pl.when(c == xl)(own_down.start)

    misc[s] = jnp.zeros((8, 128), F32)
    misc[s, 0:1, 0:WR] = gain_one[...].astype(F32)
    misc[s, 1:2, 0:WR] = gain_two[...].astype(F32)
    misc[s, 2:3, :] = seg[...].astype(F32)

    pl.semaphore_wait(barrier, 21)

    ms, mr = net.pair(7)
    for k in range(1, 8):
        net.go(misc.at[s], misc.at[s], ms(k - 1), mr(k - 1), of_sequence(k)[1])

    for copy in local[4:6]:
        copy.wait()
    es, er = net.pair(7)
    for k in range(1, 8):
        net.go(wkv.at[c, rows], wkv.at[c, rows], es(k - 1), er(k - 1), of_sequence(k)[1])

    pl.when(own_index == 3)(own_v.wait)
    pl.when(own_index != 3)(own_o.wait)
    os_, or_ = net.pair(7)
    for k in range(1, 8):
        part = wvo.at[rows, own_lanes]
        net.go(part, part, os_(k - 1), or_(k - 1), of_sequence(k)[1])

    pl.when(sender & (lax.rem(z, 2) == 0))(own_gate.wait)
    pl.when(sender & (lax.rem(z, 2) == 1))(own_up.wait)

    for core in range(2):

        @pl.when(sender & (c == core))
        def _():
            for k in range(4):
                st[k] = wide[0, :, FC * (4 * core + k) : FC * (4 * core + k + 1)]

    matrix = lax.rem(z, 2)
    gs, gr = net.pair(8)
    for d in range(2):
        for k in range(4):
            if d == 0 and k == 0:
                continue
            target = place(xh * 2 + lax.rem(xl + d, 2), wrap(y + k), z, c)
            block = st.at[wrap(y + k)]
            net.go(block, wgu.at[matrix, rows], gs(4 * d + k), gr(4 * d + k), target, when=sender)

    @pl.when(sender)
    def _():
        wgu[matrix, rows] = st[y]

    for copy in local[0:3]:
        copy.wait()
    qs_s, qs_r = net.pair(11)
    for k in range(1, 4):
        part = wqk.at[rows, core_half]
        net.go(part, part, qs_s(k - 1), qs_r(k - 1), place(x, wrap(y + k), z, c))
    for k in range(4):
        for d in range(2):
            part = wqk.at[rows, part_of(2 * c + d, 256, 128)]
            i = 3 + 2 * k + d
            net.go(part, part, qs_s(i), qs_r(i), place(wrap(x + 1 - 2 * d), wrap(y + k), z, c))

    for k in range(1, 8):

        @pl.when(s + k < 8)
        def _():
            kv[part_of(s + k, ROWS, 16)] = jnp.zeros((ROWS, 256), BF16)

        @pl.when(k <= s)
        def _():
            rkv[k - 1] = jnp.zeros((ROWS, 256), BF16)

    def block_rows(k):
        return part_of(4 * lax.div(z, 2) + wrap(y - k), WR, 16)

    gz_s, gz_r = net.pair(12)

    def block_along_z(k):
        part = wgu.at[matrix, block_rows(k)]
        for to in range(1, 4):
            net.go(part, part, gz_s(4 * to + k - 4), gz_r(4 * to + k - 4), along_z(to))

    net.landed(wgu.at[0, rows], gr(4), when=jnp.logical_not(sender))
    block_along_z(0)

    for k in range(1, 8):
        net.landed(wvo.at[rows, own_lanes], or_(k - 1))
    oz_s, oz_r = net.pair(3)
    for k in range(1, 4):
        part = wvo.at[:, own_lanes]
        net.go(part, part, oz_s(k - 1), oz_r(k - 1), along_z(k))

    tok = tokens[...].astype(F32)
    unit = tok * lax.rsqrt(jnp.mean(tok * tok, axis=-1, keepdims=True) + EPS)

    for k in range(1, 8):
        net.landed(misc.at[0], mr(k - 1))
    for k in range(8):
        gains[0:8, WR * k : WR * (k + 1)] = misc[k, 0:8, 0:WR]
    numbers = misc[:, 2, :]
    zeros = jnp.sum(jnp.where(numbers < 0.5, 1.0, 0.0), keepdims=True)
    ones = jnp.sum(jnp.where((numbers > 0.5) & (numbers < 1.5), 1.0, 0.0), keepdims=True)
    own_numbers = misc[s, 2:3, :]
    begin = jnp.where(own_numbers < 0.5, 0.0, jnp.where(own_numbers < 1.5, zeros, zeros + ones))
    lane = lax.broadcasted_iota(jnp.int32, (1, ROWS), 1) + s * ROWS
    angle = freq[...] * (lane.astype(F32) - begin)
    trig[0] = jnp.cos(angle)
    trig[1] = jnp.sin(angle)
    key_place = lax.broadcasted_iota(jnp.int32, (LENGTH, ROWS), 0)
    allowed = (key_place >= begin.astype(jnp.int32)) & (key_place <= lane)
    mask[...] = jnp.where(allowed, 0.0, -1e30)
    normed = (unit * gains[0:1, :]).astype(BF16)
    normed_t = jnp.transpose(normed)

    ef_s, ef_r = net.pair(7)
    for k in range(1, 8):
        part = wkv.at[c, part_of(lax.rem(s + 8 - k, 8), WR, 16)]
        net.landed(part, er(k - 1))
        net.go(part, part, ef_s(k - 1), ef_r(k - 1), core_peer)
    for k in range(1, 8):
        net.landed(wkv.at[c, rows], ef_r(k - 1))
    cosine, sine = trig[0], trig[1]

    def rotated(raw, at):
        first = raw[at : at + 32]
        second = raw[at + 32 : at + 64]
        return first * cosine - second * sine, second * cosine + first * sine

    raw_keys = jnp.transpose(dot(normed, wkv[0]))
    keys = jnp.concatenate([*rotated(raw_keys, 0), *rotated(raw_keys, HD)], axis=0)
    kv[own_rows, 0:128] = jnp.transpose(keys).astype(BF16)
    kv[own_rows, 128:256] = dot(normed, wkv[1]).astype(BF16)

    ks, kr = net.pair(7)
    for k in range(1, 8):
        net.go(kv.at[own_rows], kv.at[own_rows], ks(k - 1), kr(k - 1), of_sequence(k)[1], when=s + k < 8)

    is_far = jnp.where(sender, 0, 1)
    for k in range(1, 4):
        net.landed(wgu.at[0, rows], gr(4 * is_far + k))
        block_along_z(k)

    ds_, dr = net.sends(1), net.recvs(2)
    half = part_of(c, FH, 16)
    net.go(wd.at[half], wdv.at[half], ds_(0), dr(c), place(wrap(x + 1 - 2 * c), y, z, xl))

    def gather_tokens(which):
        ts, tr = net.pair(3)
        part = acts.at[which, own_tokens]
        for k in (1, 3, 2):
            net.go(part, part, ts(k - 1), tr(k - 1), place(x, wrap(y + k), z, c))
        return tr

    local[3].wait()
    cot_r = gather_tokens(1)

    qf_s, qf_r = net.pair(11)
    for i in range(11):
        if i < 3:
            part = wqk.at[part_of(xl * 4 + wrap(y - (i + 1)), WR, 16), core_half]
        else:
            k, d = divmod(i - 3, 2)
            part = wqk.at[part_of((1 - xl) * 4 + wrap(y - k), WR, 16), part_of(2 * c + d, 256, 128)]
        net.landed(part, qs_r(i))
        net.go(part, part, qf_s(i), qf_r(i), core_peer)

    for i in range(11):
        net.landed(wqk.at[rows, pl.ds(0, 512 if i < 3 else 256)], qf_r(i))
    raw = jnp.transpose(dot(normed, wqk[...]))
    for head in range(H):
        kv_head, j = divmod(head, GROUP)
        first, second = rotated(raw, HD * head + (128 if head > 5 else 0))
        qs[kv_head, 0:32, ROWS * j : ROWS * (j + 1)] = (first * SCALE).astype(BF16)
        qs[kv_head, 32:64, ROWS * j : ROWS * (j + 1)] = (second * SCALE).astype(BF16)

    for k in range(1, 8):
        net.landed(kv.at[own_rows], kr(k - 1), when=s - k >= 0)
    for head in range(KVH):
        keys = kv[:, HD * head : HD * (head + 1)]
        values = kv[:, 128 + HD * head : 128 + HD * (head + 1)]
        kc[head] = keys
        vc[head] = values
        kt[head] = jnp.transpose(keys)
        vt[head] = jnp.transpose(values)

    def attend(head, j, width):
        lanes = part_of(j, ROWS, 128) if width == 1 else pl.ds(pl.multiple_of(ROWS * j, 256), 2 * ROWS)
        raw_scores = dot(kc[head], qs[head, :, lanes])
        parts = []
        for i in range(width):
            scores = raw_scores[:, ROWS * i : ROWS * (i + 1)] + mask[...]
            highest = jnp.max(scores, axis=0, keepdims=True)
            weights = jnp.exp(scores - highest)
            total = jnp.sum(weights, axis=0, keepdims=True)
            parts.append((weights * (1.0 / total)).astype(BF16))
            lse[GROUP * head + j + i] = jnp.broadcast_to(highest + jnp.log(total), (8, ROWS))
        heads = dot(vt[head], jnp.concatenate(parts, axis=1) if width == 2 else parts[0])
        for i in range(width):
            mixt[part_of(GROUP * head + j + i, HD, HD)] = heads[:, ROWS * i : ROWS * (i + 1)]

    for p in range(GROUP // 2):
        for head in range(KVH):
            attend(head, 2 * p, 2)
    for head in range(KVH):
        attend(head, GROUP - 1, 1)

    of_s, of_r = net.pair(4)
    for k in range(4):
        part = wvo.at[:, part_of(4 * c + wrap(z - k), 128, 128)]
        if k:
            net.landed(part, oz_r(k - 1))
        net.go(part, part, of_s(k), of_r(k), core_peer)
    for k in range(4):
        net.landed(wvo.at[:, own_lanes], of_r(k))
    attended_t = mixt[...].astype(BF16)
    attended = jnp.transpose(mixt[...]).astype(BF16)
    middle = tokens[...].astype(F32) + jnp.concatenate(
        [dot(attended, wvo[:, 0:384]), dot(attended, wvo[:, 512:1024])], axis=1
    )
    mid[...] = middle
    factor = lax.rsqrt(jnp.mean(middle * middle, axis=-1, keepdims=True) + EPS)
    acts[0, own_tokens] = (middle * factor * gains[1:2, :]).astype(BF16)

    n2_r = gather_tokens(0)

    def forward(which, off, send, recv):
        part = acts.at[which, part_of(2 * wrap(y - off) + c, ROWS, 16)]
        return remote(part, part, send(off), recv(off), core_peer)

    nf_s, nf_r = net.pair(4)
    cf_s, cf_r = net.pair(4)
    forward(0, 0, nf_s, nf_r).start()
    for off in (0, 1, 3, 2):
        if off:
            net.landed(acts.at[1, own_tokens], cot_r(off - 1))
        forward(1, off, cf_s, cf_r).start()
    pl.when(c == xl)(own_down.wait)
    for i in range(2):
        net.landed(wdv.at[pl.ds(FH * i, FH)], dr(i), when=c != xl)
    for i in range(12):
        net.landed(wgu.at[0, rows], gz_r(i))

    xsend, xrecv = net.pair(4)
    psend, precv = net.sends(8), net.recvs(6)
    vsend, vrecv = net.pair(2)

    def offset(k):
        return k

    def exchange(off):
        block = part_of(off, 256, 256)
        return remote(pa.at[0, block], pa.at[1, block], xsend(off), xrecv(off), core_peer)

    def part_copy(slot, core):
        off = (0, 1, 3)[slot]
        return remote(
            pa.at[0, pl.ds(256 * off + ROWS * core, ROWS)], fr.at[c, slot], psend(2 * slot + core),
            precv(3 * c + slot), place(x, wrap(y - off), z, core),
        )

    def through(side):
        rows_of = pl.ds(512 + ROWS * side, ROWS)
        return remote(pa.at[0, rows_of], via.at[side], vsend(side), vrecv(side), place(x, wrap(y - 1 + 2 * side), z, c))

    def add_cores(off):
        exchange(off).wait()
        block = pl.ds(256 * off, 256)
        total = own[(0, 1, 0, 2)[off]] + pa[1, block].astype(F32)
        if off % 2:
            side = off // 2
            through(side).wait_recv()
            half_of = slice(ROWS * side, ROWS * (side + 1))
            other = slice(ROWS * (1 - side), ROWS * (2 - side))
            pa[0, pl.ds(256 * off + ROWS * (1 - side), ROWS)] = total[other].astype(BF16)
            pa[0, pl.ds(256 * off + ROWS * side, ROWS)] = (total[half_of] + via[side].astype(F32)).astype(BF16)
        else:
            pa[0, block] = total.astype(BF16)

    def to_owners(off):
        add_cores(off)
        for core in range(2):
            if off == 2:
                through(core).start()
            elif off:
                part_copy(off - off // 3, core).start()
            else:

                @pl.when(c == core)
                def _():
                    fr[core, 0] = pa[0, ROWS * core : ROWS * (core + 1)]

                pl.when(c != core)(part_copy(0, core).start)

    @pl.loop(0, 4)
    def _(k):
        net.landed(acts.at[0, own_tokens], nf_r(offset(k)))
        net.landed(acts.at[1, own_tokens], cf_r(offset(k)))
        off = offset(k)
        block = part_of(wrap(y - off), 256, 256)
        normed_two = acts[0, block]
        cotangent = acts[1, block]
        gate = dot(normed_two, wgu[0])
        up = dot(normed_two, wgu[1])
        grad_hidden = dot_nt(cotangent, wdv[...])
        opening = 1.0 / (1.0 + jnp.exp(-gate))
        act = gate * opening
        hidden = (act * up).astype(BF16)
        grad_gate = (grad_hidden * up * opening * (1.0 + gate * (1.0 - opening))).astype(BF16)
        grad_up = (grad_hidden * act).astype(BF16)
        gua[0, block] = grad_gate
        gua[1, block] = grad_up
        da[1, 0:FC, block] = jnp.transpose(hidden)
        da[0, :, block] = jnp.transpose(normed_two)

        @pl.when(k < 3)
        def _():
            after = offset(k + 1)
            net.landed(acts.at[0, own_tokens], n2_r(after - 1))
            forward(0, after, nf_s, nf_r).start()

        pl.when(k == 1)(lambda: to_owners(0))
        pl.when((k == 3) & (c == 1))(lambda: to_owners(2))

        out_part = dot(hidden, wdv[...])
        grad_part = dot_nt(grad_gate, wgu[0]) + dot_nt(grad_up, wgu[1])
        own[off - 2 * lax.div(off, 2) + lax.div(off, 3)] = jnp.where(c == 0, out_part, grad_part)
        pa[0, part_of(off, 256, 256)] = jnp.where(c == 0, grad_part, out_part).astype(BF16)
        exchange(off).start()

    for off in range(4):
        forward(0, off, nf_s, nf_r).wait_send()
        forward(1, off, cf_s, cf_r).wait_send()
    net.drain()
    pl.when(c == 0)(lambda: to_owners(2))

    def gradient(matrix_, store):
        shift = y + 2 * matrix_
        for h in range(2):
            tall = dot(da[0, 448 * h : 448 * (h + 1)], gua[matrix_]).astype(BF16)
            for k in range(4):
                store[h, wrap(k - shift)] = tall[WR * k : WR * (k + 1)]

    gradient(0, dgate)
    zs, zr = net.pair(3)
    for k in range(1, 4):
        net.go(dgate.at[:, wrap(z + k)], rz.at[k - 1], zs(k - 1), zr(k - 1), along_z(k))
    gradient(1, dup)
    us, ur = net.pair(3)
    for k in range(1, 4):
        part = dup.at[lax.rem(xl + k, 2), pl.ds(2 * lax.div(wrap(x + k), 2), 2)]
        net.go(part, ru.at[k - 1], us(k - 1), ur(k - 1), along_x(k))

    @pl.when(c == 1)
    def _():
        to_owners(1)
        to_owners(3)

    for h in range(2):
        tall = dot(da[1, FH * h : FH * (h + 1)], acts[1]).astype(BF16)
        for i in range(7):
            q = 7 * h + i
            dwd[q // 4, q % 4] = tall[:, 128 * i : 128 * (i + 1)]
    for q in (14, 15):
        dwd[q // 4, q % 4] = jnp.zeros((FH, 128), BF16)

    zds, zdr = net.pair(3)
    for k in range(1, 4):
        net.go(dwd.at[:, wrap(z + k)], rzd.at[k - 1], zds(k - 1), zdr(k - 1), along_z(k))

    own_cot[...] = acts[1, own_tokens]

    @pl.loop(0, GROUP)
    def _(j):
        lanes = part_of(j, ROWS, 128)
        for head in range(KVH):
            scores = dot(kc[head], qs[head, :, lanes]) + mask[...]
            acts[head, :, lanes] = jnp.exp(scores - lse[GROUP * head + j, 0:1, :]).astype(BF16)

    def landed_parts(kind):
        for slot in range(3):
            net.landed(fr.at[kind, slot], precv(3 * kind + slot), when=None if slot else c != kind)
        return fr[kind, 0].astype(F32) + fr[kind, 1].astype(F32) + fr[kind, 2].astype(F32)

    @pl.when(c == 0)
    def _():
        to_owners(1)
        to_owners(3)

    grad_normed = landed_parts(1)
    middle = mid[...]
    own[0, 0:ROWS] = middle
    factor = lax.rsqrt(jnp.mean(middle * middle, axis=-1, keepdims=True) + EPS)
    unit_two = middle * factor
    scaled = grad_normed * gains[1:2, :]
    gvec[...] = jnp.broadcast_to(jnp.sum(grad_normed * unit_two, axis=0, keepdims=True), (8, D))
    grad_middle = own_cot[...].astype(F32) + factor * (
        scaled - unit_two * jnp.mean(scaled * unit_two, axis=-1, keepdims=True)
    )
    mid[...] = grad_middle

    branch = grad_middle.astype(BF16)
    grad_mixed = jnp.transpose(
        dot_nt(branch[:, 0:384], wvo[:, 0:384]) + dot_nt(branch[:, 384:D], wvo[:, 512:1024])
    )
    for head in range(H):
        kv_head, j = divmod(head, GROUP)
        gmt[kv_head, :, ROWS * j : ROWS * (j + 1)] = grad_mixed[HD * head : HD * (head + 1)].astype(BF16)
    grad_out = dot(attended_t, branch).astype(BF16)
    da[1, :, 0:384] = grad_out[:, 0:384]
    da[1, :, 512:1024] = grad_out[:, 384:D]
    first_of_peer = pl.ds(pl.multiple_of(512 * (1 - c), 128), 384)
    last_of_peer = pl.ds(pl.multiple_of(512 * (1 - c) + 384, 128), 128)
    first_own = pl.ds(pl.multiple_of(512 * c, 128), 384)
    last_own = pl.ds(pl.multiple_of(512 * c + 384, 128), 128)
    firsts, lasts_ = pl.ds(0, 384), pl.ds(384, 128)
    xas, xar = net.pair(5)
    net.go(da.at[1, :, first_of_peer], xa.at[1, :, firsts], xas(1), xar(1), core_peer)
    net.go(da.at[1, :, last_of_peer], xa.at[1, :, lasts_], xas(3), xar(3), core_peer, when=c == 0)

    for slot in range(3):
        for core in range(2):
            if slot:
                part_copy(slot, core).wait_send()
            else:
                pl.when(c != core)(part_copy(slot, core).wait_send)
    for side in range(2):
        through(side).wait_send()

    def to_rows_owners(i, lanes, sems):
        for k in range(1, 4):
            other = part_of(xl * 4 + wrap(y + k), WR, 16)
            net.go(
                sa.at[i, other, lanes], rya.at[i, 0, k - 1, :, lanes], sems[0](k - 1), sems[1](k - 1),
                place(x, wrap(y + k), z, c),
            )

    def to_rows_owners_across(i, half_size, sems):
        for k in range(4):
            other = part_of((1 - xl) * 4 + wrap(y + k), WR, 16)
            for d, cut in enumerate(half_size):
                net.go(
                    sa.at[i, other, cut], rya.at[i, 1, k, :, cut], sems[0](3 + 2 * k + d), sems[1](3 + 2 * k + d),
                    place(wrap(x + 1 - 2 * d), wrap(y + k), z, c),
                )

    def from_rows_owners(i, lanes, half_size, sems):
        for k in range(1, 4):
            net.landed(rya.at[i, 0, k - 1, :, lanes], sems[1](k - 1))
        for k in range(4):
            for d, cut in enumerate(half_size):
                net.landed(rya.at[i, 1, k, :, cut], sems[1](3 + 2 * k + d))

    def last_tile(i, when):
        net.landed(xa.at[i, :, lasts_], xar(2 + i), when=when)

        @pl.when(when)
        def _():
            sa[i, :, 384:512] = (da[i, :, last_own].astype(F32) + xa[i, :, 384:512].astype(F32)).astype(BF16)

        for k in range(1, 8):
            far = k > 3
            other = (1 - xl if far else xl) * 4 + wrap(y + k)
            target = place(wrap(x + (1 - 2 * i if far else 0)), wrap(y + k), z, c)
            part = sa.at[i, part_of(other, WR, 16), lasts_]
            net.go(part, ryl.at[i, k - 1], yl[i][0](k - 1), yl[i][1](k - 1), target, when=when)

    first_cuts = ((pl.ds(0, 256), pl.ds(256, 128)), (pl.ds(0, 128), pl.ds(128, 256)))
    yf = [net.pair(11), net.pair(11)]
    yl = [net.pair(7), net.pair(7)]
    net.landed(xa.at[1, :, firsts], xar(1))
    sa[1, :, 0:384] = (da[1, :, first_own].astype(F32) + xa[1, :, 0:384].astype(F32)).astype(BF16)
    to_rows_owners(1, firsts, yf[1])


    for k in range(1, 4):
        net.landed(ru.at[k - 1], ur(k - 1))
    for i in range(2):
        su[i] = (
            dup[xl, 2 * xh + i].astype(F32) + ru[0, i].astype(F32) + ru[1, i].astype(F32) + ru[2, i].astype(F32)
        ).astype(BF16)
    vs, vr = net.sends(2), net.recvs(4)
    for i in range(2):
        target = 2 * xh + i
        net.go(su.at[i], ruz.at[z], vs(i), vr(z), place(x, y, target, c), when=z != target)
    for k in range(1, 4):
        net.landed(rz.at[k - 1], zr(k - 1))
    for i in range(2):
        sz[i] = (
            dgate[i, z].astype(F32) + rz[0, i].astype(F32) + rz[1, i].astype(F32) + rz[2, i].astype(F32)
        ).astype(BF16)
    xs_s, xs_r = net.pair(3)
    for k in range(1, 4):
        net.go(sz.at[lax.rem(xl + k, 2)], rx.at[k - 1], xs_s(k - 1), xs_r(k - 1), along_x(k))

    def attend_back(head, j, width):
        lanes = part_of(j, ROWS, 128) if width == 1 else pl.ds(pl.multiple_of(ROWS * j, 256), 2 * ROWS)
        probs = acts[head, :, lanes].astype(F32)
        grad_probs = dot(vc[head], gmt[head, :, lanes])
        delta = jnp.sum(grad_probs * probs, axis=0, keepdims=True)
        grad_scores = (probs * (grad_probs - delta)).astype(BF16)
        pa[head, :, lanes] = grad_scores
        both = dot(kt[head], grad_scores) * SCALE
        cosine, sine = trig[0], trig[1]
        for i in range(width):
            rot = both[:, ROWS * i : ROWS * (i + 1)]
            at = HD * (GROUP * head + j + i)
            mixt[pl.ds(pl.multiple_of(at, 32), 32)] = rot[0:32] * cosine + rot[32:64] * sine
            mixt[pl.ds(pl.multiple_of(at + 32, 32), 32)] = rot[32:64] * cosine - rot[0:32] * sine

    kvs, kvr = net.pair(14)
    for head in range(KVH):
        for p in range(GROUP // 2):
            attend_back(head, 2 * p, 2)
        attend_back(head, GROUP - 1, 1)
        dkv[:, 128 * head : 128 * head + HD] = dot_nt(pa[head], qs[head]).astype(BF16)
        dkv[:, 128 * head + HD : 128 * (head + 1)] = dot_nt(acts[head], gmt[head]).astype(BF16)
        for k in range(1, 8):
            other, target = of_sequence(k)
            lanes = pl.ds(128 * head, 128)
            i = 7 * head + k - 1
            net.go(
                dkv.at[part_of(other, ROWS, 16), lanes], rkv.at[k - 1, :, lanes], kvs(i), kvr(i), target, when=s + k >= 8
            )

    vout[...] = (own[0, 0:ROWS] + landed_parts(0)).astype(BF16)

    grad_query = jnp.transpose(mixt[...]).astype(BF16)
    gqk[:, 0:384] = grad_query[:, 0:384]
    gqk[:, 512:1024] = grad_query[:, 384:D]
    part = dot(normed_t, grad_query).astype(BF16)
    da[0, :, 0:384] = part[:, 0:384]
    da[0, :, 512:1024] = part[:, 384:D]
    net.go(da.at[0, :, first_of_peer], xa.at[0, :, firsts], xas(0), xar(0), core_peer)
    net.go(da.at[0, :, last_of_peer], xa.at[0, :, lasts_], xas(2), xar(2), core_peer, when=c == 0)

    for k in range(1, 4):
        net.landed(rx.at[k - 1], xs_r(k - 1))
    sgu[0] = (
        sz[xl].astype(F32) + rx[0].astype(F32) + rx[1].astype(F32) + rx[2].astype(F32)
    ).astype(BF16)
    own_block = 4 * c + y
    held = [4 * c + wrap(y - z), 4 * c + wrap(y - z - 2)]
    ags, agr = net.pair(4)
    net.go(sgu.at[0], agu.at[0, own_block], ags(0), agr(0), place(x, wrap(y + z), z, c), when=z != 0)

    @pl.when(z == 0)
    def _():
        agu[0, own_block] = sgu[0]

    cosine, sine = trig[0], trig[1]
    back, grad_values = [], []
    for head in range(KVH):
        lanes = slice(128 * head, 128 * (head + 1))
        total = dkv[own_rows, lanes].astype(F32)
        for k in range(1, 8):
            net.landed(rkv.at[k - 1, :, pl.ds(0, 128)], kvr(7 * head + k - 1), when=k > s)
            total = total + rkv[k - 1, :, lanes].astype(F32)
        keys = jnp.transpose(total)
        first, second = keys[0:32], keys[32:64]
        back += [first * cosine + second * sine, second * cosine - first * sine]
        grad_values.append(total[:, HD:128])
    grad_key = jnp.transpose(jnp.concatenate(back, axis=0)).astype(BF16)
    gqk[:, 384:512] = grad_key
    grad_value = jnp.concatenate(grad_values, axis=1).astype(BF16)
    da[0, :, 384:512] = dot(normed_t, grad_key).astype(BF16)
    da[1, :, 384:512] = dot(normed_t, grad_value).astype(BF16)
    for i in range(2):
        net.go(da.at[i, :, last_of_peer], xa.at[i, :, lasts_], xas(2 + i), xar(2 + i), core_peer, when=c == 1)

    net.landed(xa.at[0, :, firsts], xar(0))
    sa[0, :, 0:384] = (da[0, :, first_own].astype(F32) + xa[0, :, 0:384].astype(F32)).astype(BF16)
    to_rows_owners_across(1, first_cuts[1], yf[1])
    to_rows_owners(0, firsts, yf[0])
    to_rows_owners_across(0, first_cuts[0], yf[0])
    last_tile(1, c == 1)
    last_tile(0, c == 1)

    grad_normed = dot_nt(gqk[...], wqk[...]) + dot_nt(grad_value, wvo[:, 384:512])
    tok = tokens[...].astype(F32)
    factor = lax.rsqrt(jnp.mean(tok * tok, axis=-1, keepdims=True) + EPS)
    unit = tok * factor
    scaled = grad_normed * gains[0:1, :]
    vtok[...] = mid[...] + factor * (scaled - unit * jnp.mean(scaled * unit, axis=-1, keepdims=True))
    gvec[0:1, :] = jnp.sum(grad_normed * unit, axis=0, keepdims=True)
    for row in range(2):
        for i in range(7):
            gpack[7 * row + i : 7 * row + i + 1, :] = gvec[row : row + 1, 128 * i : 128 * (i + 1)]
    net.go(gpack, gx, xas(4), xar(4), core_peer)

    for i in range(2):
        last_tile(i, c == 0)
    net.landed(gx, xar(4))
    gsum[...] = gpack[...] + gx[...]
    gys, gyr = net.pair(7)
    for k in range(1, 8):
        net.go(gsum, gy.at[k - 1], gys(k - 1), gyr(k - 1), of_sequence(k)[1])

    owner = xh == lax.div(z, 2)
    for k in range(4):
        net.landed(su.at[0], vr(k), when=owner & (z != k))
    ucs, ucr = net.pair(1)
    uhs = net.sends(1)

    @pl.when(owner)
    def _():
        ruz[z] = su[lax.rem(z, 2)]
        sgu[1] = (
            ruz[0].astype(F32) + ruz[1].astype(F32) + ruz[2].astype(F32) + ruz[3].astype(F32)
        ).astype(BF16)

    net.go(sgu.at[1], agu.at[1, own_block], ucs(0), ucr(0), place(x, wrap(y + z + 2), z, c), when=owner & (z != 2))
    net.go(sgu.at[1], agu.at[1, own_block], uhs(0), ucr(0), place(wrap(x + 2), wrap(y + z + 2), z, c), when=owner)

    @pl.when(owner & (z == 2))
    def _():
        agu[1, own_block] = sgu[1]

    for k in range(1, 4):
        net.landed(rzd.at[k - 1], zdr(k - 1))
    for i in range(4):
        sdz[i] = (
            dwd[i, z].astype(F32) + rzd[0, i].astype(F32) + rzd[1, i].astype(F32) + rzd[2, i].astype(F32)
        ).astype(BF16)
    xds, xdr = net.pair(3)
    for k in range(1, 4):
        net.go(sdz, rxd.at[k - 1], xds(k - 1), xdr(k - 1), along_x(k), when=lax.rem(xl + k, 2) == c)


    afs, afr = net.pair(8)

    def spread(matrix_, sends, recvs):
        for k in range(1, 4):
            net.go(agu.at[matrix_, held[matrix_]], agu.at[matrix_, held[matrix_]], sends(k), recvs(k), along_z(k))
        part = agu.at[matrix_, held[matrix_]]
        net.go(part, part, afs(4 * matrix_), afr(4 * matrix_), core_peer)

    net.landed(agu.at[0, held[0]], agr(0), when=z != 0)
    spread(0, ags, agr)

    zas2, zar2 = net.pair(6)
    for i in range(2):
        from_rows_owners(i, firsts, first_cuts[i], yf[i])
        total = sa[i, rows, 0:384].astype(F32)
        for k in range(3):
            total = total + rya[i, 0, k, :, 0:384].astype(F32)
        for k in range(4):
            total = total + rya[i, 1, k, :, 0:384].astype(F32)
        ta[i, :, 0:384] = total.astype(BF16)
        total = sa[i, rows, 384:512].astype(F32)
        for k in range(1, 8):
            net.landed(ryl.at[i, k - 1], yl[i][1](k - 1))
            total = total + ryl[i, k - 1].astype(F32)
        ta[i, :, 384:512] = total.astype(BF16)
    for k in range(1, 4):
        net.go(ta.at[:, :, part_of(wrap(z + k), 128, 128)], rza.at[k - 1], zas2(k - 1), zar2(k - 1), along_z(k))
    total = gsum[...]
    for k in range(1, 8):
        net.landed(gy.at[k - 1], gyr(k - 1))
        total = total + gy[k - 1]
    gz[3] = total
    for k in range(1, 4):
        net.go(gz.at[3], gz.at[k - 1], zas2(k + 2), zar2(k + 2), along_z(k))

    uas, uar = net.pair(4)
    net.landed(agu.at[1, held[1]], ucr(0), when=jnp.logical_not(owner) | (z != 2))
    spread(1, uas, uar)

    for k in range(1, 4):
        net.landed(rxd.at[k - 1], xdr(k - 1), when=xl == c)
    zas, zar = net.pair(3)

    @pl.when(xl == c)
    def _():
        for i in range(4):
            agd[i, z] = (
                sdz[i].astype(F32) + rxd[0, i].astype(F32) + rxd[1, i].astype(F32) + rxd[2, i].astype(F32)
            ).astype(BF16)

    for k in range(1, 4):
        net.go(agd.at[:, z], agd.at[:, z], zas(k - 1), zar(k - 1), along_z(k), when=xl == c)

    for k in range(1, 4):
        net.landed(rza.at[k - 1], zar2(k - 1))
    tile[...] = (
        ta[:, :, part_of(z, 128, 128)].astype(F32)
        + rza[0].astype(F32) + rza[1].astype(F32) + rza[2].astype(F32)
    ).astype(BF16)
    total = gz[3]
    for k in range(1, 4):
        net.landed(gz.at[k - 1], zar2(k + 2))
        total = total + gz[k - 1]
    gh[1] = total
    hs, hr = net.pair(2)
    net.go(tile, rh, hs(0), hr(0), along_x(2))
    net.go(gh.at[1], gh.at[0], hs(1), hr(1), along_x(2))

    net.landed(rh, hr(0))
    own_tile = aout.at[:, :, own_lanes]
    aout[:, :, own_lanes] = (tile[...].astype(F32) + rh[...].astype(F32)).astype(BF16)
    lasts, lastr = net.pair(3)
    for k in range(1, 4):
        net.go(own_tile, own_tile, lasts(k - 1), lastr(k - 1), along_z(k))
    net.landed(gh.at[0], hr(1))
    gpack_sum = gh[0] + gh[1]
    gain_o[...] = jnp.zeros_like(gain_o)
    for row in range(2):
        for i in range(7):
            gain_o[row : row + 1, 128 * i : 128 * (i + 1)] = gpack_sum[7 * row + i : 7 * row + i + 1]

    net.drain()

    outs = [
        pltpu.make_async_copy(aout, attn_o, lsem.at[9]),
    ]

    def to_other_core(matrix_, recvs):
        for k in (1, 3, 2):
            part = agu.at[matrix_, 4 * c + wrap(y - wrap(z - k) - 2 * matrix_)]
            net.landed(part, recvs(k))
            net.go(part, part, afs(4 * matrix_ + k), afr(4 * matrix_ + k), core_peer)

    def assemble(matrix_):
        for k in range(4):
            net.landed(agu.at[matrix_, 0], afr(4 * matrix_ + k))
        for k in range(8):
            wide[matrix_, :, FC * k : FC * (k + 1)] = agu[matrix_, k]

    to_other_core(0, agr)
    assemble(0)
    for k in range(1, 4):
        net.landed(agd.at[:, z], zar(k - 1), when=xl == c)
    dfs, dfr = net.pair(1)
    net.go(agd, fin, dfs(0), dfr(0), core_peer, when=xl == c)
    own_sums = pltpu.make_async_copy(agd, d_o, lsem.at[8])
    pl.when(xl == c)(own_sums.start)
    for k in range(1, 4):
        net.landed(own_tile, lastr(k - 1))
    fs, fr_ = net.pair(1)
    part = aout.at[:, :, core_half]
    net.go(part, part, fs(0), fr_(0), core_peer)
    to_other_core(1, uar)
    net.landed(fin, dfr(0), when=xl != c)
    peer_sums = pltpu.make_async_copy(fin, d_o, lsem.at[8])
    pl.when(xl != c)(peer_sums.start)
    net.landed(aout.at[:, :, pl.ds(0, 512)], fr_(0))
    outs[0].start()
    assemble(1)

    net.drain()
    for copy in outs:
        copy.wait()
    pl.when(xl == c)(own_sums.wait)
    pl.when(xl != c)(peer_sums.wait)


def finish_kernel(
    gain, vout, vtok, attn, wide, down,
    one, two, out, tok, gq, gk, gv, go, gate, up, gdown,
    fq, fk, fv, fo, fgate, fup, fdown, osem,
):
    outs = []

    def store(source, target):
        copy = pltpu.make_async_copy(source, target, osem.at[len(outs)])
        copy.start()
        outs.append(copy)

    store(vtok, tok)
    store(vout, out)
    fgate[...] = wide[0].astype(F32)
    store(fgate, gate)
    fup[...] = wide[1].astype(F32)
    store(fup, up)
    for q in range(14):
        h, i = divmod(q, 7)
        fdown[FH * h : FH * (h + 1), 128 * i : 128 * (i + 1)] = down[q // 4, q % 4].astype(F32)
    store(fdown, gdown)
    fq[:, 0:384] = attn[0, :, 0:384].astype(F32)
    fq[:, 384:D] = attn[0, :, 512:1024].astype(F32)
    store(fq, gq)
    fo[:, 0:384] = attn[1, :, 0:384].astype(F32)
    fo[:, 384:D] = attn[1, :, 512:1024].astype(F32)
    store(fo, go)
    fk[...] = attn[0, :, 384:512].astype(F32)
    store(fk, gk)
    fv[...] = attn[1, :, 384:512].astype(F32)
    store(fv, gv)
    shard = lax.axis_index("shard")
    for k in range(8):

        @pl.when(shard == k)
        def _():
            one[...] = gain[0:1, WR * k : WR * (k + 1)]
            two[...] = gain[1:2, WR * k : WR * (k + 1)]

    for copy in outs:
        copy.wait()


def vmem():
    return pl.BlockSpec(memory_space=pltpu.VMEM)


def anywhere():
    return pl.BlockSpec(memory_space=pl.ANY)


def shape(dims, dtype):
    return jax.ShapeDtypeStruct(dims, dtype)


def body(
    tokens, segments, attn_gain, w_query, w_key, w_value, w_out, ffn_gain, w_gate, w_up, w_down, cotangent
):
    half = HD // 2
    frequency = THETA ** (-(np.arange(half) * 2.0 / HD))
    freq = np.broadcast_to(frequency[:, None], (half, ROWS)).astype(np.float32)
    layer = pl.pallas_call(
        layer_kernel,
        name="layer",
        out_shape=[
            pltpu.VMEM((8, D), F32),
            pltpu.VMEM((ROWS, D), BF16),
            pltpu.VMEM((ROWS, D), F32),
            pltpu.VMEM((2, WR, 1024), BF16),
            pltpu.VMEM((2, WR, FF), BF16),
            pltpu.VMEM((4, 4, FH, 128), BF16),
        ],
        in_specs=[vmem()] * 5 + [anywhere()] * 8,
        out_specs=[vmem()] * 3 + [anywhere(), vmem(), anywhere()],
        scratch_shapes=[
            pltpu.VMEM((8, 8, 128), F32),
            pltpu.VMEM((D, 1024), BF16),
            pltpu.VMEM((D, 1024), BF16),
            pltpu.VMEM((2, D, 128), BF16),
            pltpu.VMEM((4, WR, FC), BF16),
            pltpu.VMEM((2, D, FC), BF16),
            pltpu.VMEM((FC, D), BF16),
            pltpu.VMEM((2, LENGTH, D), BF16),
            pltpu.VMEM((2, D, LENGTH), BF16),
            pltpu.VMEM((LENGTH, 256), BF16),
            pltpu.VMEM((KVH, LENGTH, HD), BF16),
            pltpu.VMEM((KVH, LENGTH, HD), BF16),
            pltpu.VMEM((KVH, HD, LENGTH), BF16),
            pltpu.VMEM((KVH, HD, LENGTH), BF16),
            pltpu.VMEM((KVH, HD, D), BF16),
            pltpu.VMEM((LENGTH, ROWS), F32),
            pltpu.VMEM((D, ROWS), F32),
            pltpu.VMEM((ROWS, D), F32),
            pltpu.VMEM((8, D), F32),
            pltpu.VMEM((2, half, ROWS), F32),
            pltpu.VMEM((H, 8, ROWS), F32),
            pltpu.VMEM((2, LENGTH, FC), BF16),
            pltpu.VMEM((3, 256, D), F32),
            pltpu.VMEM((2, LENGTH, D), BF16),
            pltpu.VMEM((2, 3, ROWS, D), BF16),
            pltpu.VMEM((2, ROWS, D), BF16),
            pltpu.VMEM((2, 4, WR, FC), BF16),
            pltpu.VMEM((2, 4, WR, FC), BF16),
            pltpu.VMEM((4, 4, FH, 128), BF16),
            pltpu.VMEM((KVH, HD, D), BF16),
            pltpu.VMEM((ROWS, D), BF16),
            pltpu.VMEM((LENGTH, 256), BF16),
            pltpu.VMEM((7, ROWS, 256), BF16),
            pltpu.VMEM((ROWS, 1024), BF16),
            pltpu.VMEM((3, 2, WR, FC), BF16),
            pltpu.VMEM((2, WR, FC), BF16),
            pltpu.VMEM((3, WR, FC), BF16),
            pltpu.VMEM((3, 2, WR, FC), BF16),
            pltpu.VMEM((2, WR, FC), BF16),
            pltpu.VMEM((4, WR, FC), BF16),
            pltpu.VMEM((2, WR, FC), BF16),
            pltpu.VMEM((2, 8, WR, FC), BF16),
            pltpu.VMEM((3, 4, FH, 128), BF16),
            pltpu.VMEM((4, FH, 128), BF16),
            pltpu.VMEM((3, 4, FH, 128), BF16),
            pltpu.VMEM((4, 4, FH, 128), BF16),
            pltpu.VMEM((4, 4, FH, 128), BF16),
            pltpu.VMEM((2, D, 512), BF16),
            pltpu.VMEM((2, D, 512), BF16),
            pltpu.VMEM((2, 2, 4, WR, 384), BF16),
            pltpu.VMEM((2, 7, WR, 128), BF16),
            pltpu.VMEM((2, WR, 512), BF16),
            pltpu.VMEM((3, 2, WR, 128), BF16),
            pltpu.VMEM((2, WR, 128), BF16),
            pltpu.VMEM((2, WR, 128), BF16),
            pltpu.VMEM((2, WR, 1024), BF16),
            pltpu.VMEM((8, D), F32),
            pltpu.VMEM((16, 128), F32),
            pltpu.VMEM((16, 128), F32),
            pltpu.VMEM((16, 128), F32),
            pltpu.VMEM((7, 16, 128), F32),
            pltpu.VMEM((4, 16, 128), F32),
            pltpu.VMEM((2, 16, 128), F32),
            pltpu.SemaphoreType.DMA((SENDS,)),
            pltpu.SemaphoreType.DMA((RECVS,)),
            pltpu.SemaphoreType.DMA((LOCALS,)),
        ],
        compiler_params=pltpu.CompilerParams(
            collective_id=0, has_side_effects=True, vmem_limit_bytes=58 << 20
        ),
    )
    results = layer(
        tokens,
        segments.reshape(1, ROWS),
        attn_gain.reshape(1, WR),
        ffn_gain.reshape(1, WR),
        freq,
        cotangent,
        w_query,
        w_key,
        w_value,
        w_out,
        w_gate,
        w_up,
        w_down,
    )
    finish = pl.pallas_call(
        finish_kernel,
        name="finish",
        out_shape=[
            shape((1, WR), F32),
            shape((1, WR), F32),
            shape((ROWS, D), BF16),
            shape((ROWS, D), F32),
            shape((WR, D), F32),
            shape((WR, 128), F32),
            shape((WR, 128), F32),
            shape((WR, D), F32),
            shape((WR, FF), F32),
            shape((WR, FF), F32),
            shape((FC, D), F32),
        ],
        in_specs=[vmem()] * 6,
        out_specs=[vmem()] * 2 + [anywhere()] * 9,
        scratch_shapes=[
            pltpu.VMEM((WR, D), F32),
            pltpu.VMEM((WR, 128), F32),
            pltpu.VMEM((WR, 128), F32),
            pltpu.VMEM((WR, D), F32),
            pltpu.VMEM((WR, FF), F32),
            pltpu.VMEM((WR, FF), F32),
            pltpu.VMEM((FC, D), F32),
            pltpu.SemaphoreType.DMA((9,)),
        ],
        compiler_params=pltpu.CompilerParams(vmem_limit_bytes=28 << 20),
    )
    one, two, out, tok, gq, gk, gv, go, gate, up, down = finish(*results)
    return out, tok, one.reshape(WR), gq, gk, gv, go, two.reshape(WR), gate, up, down


def solution(mesh):
    tokens = P(("replica", "shard"), None)
    weight = P("shard", None)
    return jax.shard_map(
        body,
        mesh=mesh,
        in_specs=(
            tokens, P(("replica", "shard")), P("shard"), weight, weight, weight, weight,
            P("shard"), weight, weight, weight, tokens,
        ),
        out_specs=(
            tokens, tokens, P("shard"), weight, weight, weight, weight, P("shard"), weight, weight, weight,
        ),
        check_vma=False,
    )
```

```python
import jax
import jax.numpy as jnp
import numpy as np
from jax import lax
from jax.experimental import pallas as pl
from jax.experimental.pallas import tpu as pltpu
from jax.sharding import PartitionSpec as P

D = 896
H = 14
HD = 64
KVH = 2
GROUP = H // KVH
FF = 4864
FC = FF // 8
FH = FC // 2
ROWS = 128
LENGTH = 1024
WR = D // 8
EPS = 1e-05
THETA = 10000.0
SCALE = 0.125

F32 = jnp.float32
BF16 = jnp.bfloat16
MESH = pl.DeviceIdType.MESH


def coords():
    replica = lax.axis_index("replica")
    shard = lax.axis_index("shard")
    x = lax.div(replica, 8) * 2 + lax.div(shard, 4)
    return x, lax.rem(shard, 4), lax.rem(lax.div(replica, 2), 4), lax.rem(replica, 2)


def place(x, y, z, core):
    return (lax.div(x, 2) * 8 + z * 2 + core, lax.rem(x, 2) * 4 + y)


def wrap(value):
    return lax.rem(value + 16, 4)


def part_of(index, size, unit):
    return pl.ds(pl.multiple_of(index * size, unit), size)


def remote(src, dst, send, recv, device):
    return pltpu.make_async_remote_copy(
        src_ref=src, dst_ref=dst, send_sem=send, recv_sem=recv, device_id=device, device_id_type=MESH
    )


class Net:
    def __init__(self, ssem, rsem, peer):
        self.ssem, self.rsem, self.peer = ssem, rsem, peer
        self.ns = self.nr = 0
        self.open = []

    def sends(self, count):
        base = self.ns
        self.ns += count
        assert self.ns <= self.ssem.shape[0]
        return lambda index: self.ssem.at[base + index]

    def recvs(self, count):
        base = self.nr
        self.nr += count
        assert self.nr <= self.rsem.shape[0]
        return lambda index: self.rsem.at[base + index]

    def pair(self, count):
        return self.sends(count), self.recvs(count)

    def go(self, src, dst, send, recv, device, when=None):
        copy = remote(src, dst, send, recv, device)
        if when is None:
            copy.start()
        else:
            pl.when(when)(copy.start)
        self.open.append((copy, when))

    def landed(self, ref, recv, when=None):
        copy = remote(ref, ref, self.ssem.at[0], recv, self.peer)
        if when is None:
            copy.wait_recv()
        else:
            pl.when(when)(copy.wait_recv)

    def drain(self):
        done, self.open = self.open, []
        for copy, when in done:
            if when is None:
                copy.wait_send()
            else:
                pl.when(when)(copy.wait_send)


def signal(barrier, device):
    pl.semaphore_signal(barrier, inc=1, device_id=device, device_id_type=MESH)


def dot(left, right):
    return jnp.dot(left, right, preferred_element_type=F32)


def dot_nt(left, right):
    return lax.dot_general(left, right, (((1,), (1,)), ((), ())), preferred_element_type=F32)


SENDS = 272
RECVS = 272
LOCALS = 16


def layer_kernel(
    tokens, seg, gain_one, gain_two, freq,
    cot, wq, wk, wv, wo, wg, wu, wd,
    gain_o,
    vout, vtok, attn_o, wide, d_o,
    misc, wqk, wvo, wkv, st, wgu, wdv, acts, da, kv, kc, vc, kt, vt, qs, mask, mixt, mid, gains, trig, lse,
    gua, own, pa, fr, via, dgate, dup, dwd,
    gmt, own_cot, dkv, rkv, gqk,
    rz, sz, rx, ru, su, ruz, sgu, agu, rzd, sdz, rxd, agd, fin,
    xa, sa, rya, ryl, ta, rza, tile, rh, aout,
    gvec, gpack, gx, gsum, gy, gz, gh,
    ssem, rsem, lsem,
):
    x, y, z, c = coords()
    xl, xh = lax.rem(x, 2), lax.div(x, 2)
    s = xl * 4 + y
    t = 2 * y + c
    core_peer = place(x, y, z, 1 - c)
    net = Net(ssem, rsem, core_peer)

    def of_sequence(k):
        other = lax.rem(s + k, 8)
        return other, place(xh * 2 + lax.div(other, 4), lax.rem(other, 4), z, c)

    def along_z(k):
        return place(x, y, wrap(z + k), c)

    def along_x(k):
        return place(wrap(x + k), y, z, c)

    rows = part_of(s, WR, 16)
    own_rows = part_of(s, ROWS, 16)
    own_tokens = part_of(t, ROWS, 16)
    core_half = part_of(c, 512, 128)

    barrier = pltpu.get_barrier_semaphore()
    for k in range(1, 4):
        signal(barrier, place(x, wrap(y + k), z, c))
        signal(barrier, along_z(k))
    for d in (1, 3):
        for k in range(4):
            signal(barrier, place(wrap(x + d), wrap(y + k), z, c))
        signal(barrier, place(wrap(x + d), y, z, 1 - c))
    for k in range(4):
        signal(barrier, place(wrap(x + 2), wrap(y + k), z, c))
    signal(barrier, core_peer)
    local = [
        pltpu.make_async_copy(wq.at[:, pl.ds(0, 384)], wqk.at[rows, pl.ds(0, 384)], lsem.at[2]),
        pltpu.make_async_copy(wk, wqk.at[rows, pl.ds(384, 128)], lsem.at[3]),
        pltpu.make_async_copy(wq.at[:, pl.ds(384, 512)], wqk.at[rows, pl.ds(512, 512)], lsem.at[4]),
        pltpu.make_async_copy(cot, acts.at[1, own_tokens], lsem.at[5]),
        pltpu.make_async_copy(wk, wkv.at[0, rows], lsem.at[12]),
        pltpu.make_async_copy(wv, wkv.at[1, rows], lsem.at[13]),
    ]
    own_index = 4 * c + z
    own_lanes = part_of(own_index, 128, 128)
    own_v = pltpu.make_async_copy(wv, wvo.at[rows, own_lanes], lsem.at[0])
    own_o = pltpu.make_async_copy(
        wo.at[:, part_of(own_index - jnp.where(own_index > 3, 1, 0), 128, 128)], wvo.at[rows, own_lanes], lsem.at[0]
    )
    pl.when(own_index == 3)(own_v.start)
    pl.when(own_index != 3)(own_o.start)
    for copy in local:
        copy.start()
    sender = xl == lax.div(z, 2)
    own_gate = pltpu.make_async_copy(wg, wide.at[0], lsem.at[6])
    own_up = pltpu.make_async_copy(wu, wide.at[0], lsem.at[6])
    pl.when(sender & (lax.rem(z, 2) == 0))(own_gate.start)
    pl.when(sender & (lax.rem(z, 2) == 1))(own_up.start)
    own_down = pltpu.make_async_copy(wd, wdv, lsem.at[7])
    pl.when(c == xl)(own_down.start)

    misc[s] = jnp.zeros((8, 128), F32)
    misc[s, 0:1, 0:WR] = gain_one[...].astype(F32)
    misc[s, 1:2, 0:WR] = gain_two[...].astype(F32)
    misc[s, 2:3, :] = seg[...].astype(F32)

    pl.semaphore_wait(barrier, 21)

    ms, mr = net.pair(7)
    for k in range(1, 8):
        net.go(misc.at[s], misc.at[s], ms(k - 1), mr(k - 1), of_sequence(k)[1])

    for copy in local[4:6]:
        copy.wait()
    es, er = net.pair(7)
    for k in range(1, 8):
        net.go(wkv.at[c, rows], wkv.at[c, rows], es(k - 1), er(k - 1), of_sequence(k)[1])

    pl.when(own_index == 3)(own_v.wait)
    pl.when(own_index != 3)(own_o.wait)
    os_, or_ = net.pair(7)
    for k in range(1, 8):
        part = wvo.at[rows, own_lanes]
        net.go(part, part, os_(k - 1), or_(k - 1), of_sequence(k)[1])

    pl.when(sender & (lax.rem(z, 2) == 0))(own_gate.wait)
    pl.when(sender & (lax.rem(z, 2) == 1))(own_up.wait)

    for core in range(2):

        @pl.when(sender & (c == core))
        def _():
            for k in range(4):
                st[k] = wide[0, :, FC * (4 * core + k) : FC * (4 * core + k + 1)]

    matrix = lax.rem(z, 2)
    gs, gr = net.pair(8)
    for d in range(2):
        for k in range(4):
            if d == 0 and k == 0:
                continue
            target = place(xh * 2 + lax.rem(xl + d, 2), wrap(y + k), z, c)
            block = st.at[wrap(y + k)]
            net.go(block, wgu.at[matrix, rows], gs(4 * d + k), gr(4 * d + k), target, when=sender)

    @pl.when(sender)
    def _():
        wgu[matrix, rows] = st[y]

    for copy in local[0:3]:
        copy.wait()
    qs_s, qs_r = net.pair(11)
    for k in range(1, 4):
        part = wqk.at[rows, core_half]
        net.go(part, part, qs_s(k - 1), qs_r(k - 1), place(x, wrap(y + k), z, c))
    for k in range(4):
        for d in range(2):
            part = wqk.at[rows, part_of(2 * c + d, 256, 128)]
            i = 3 + 2 * k + d
            net.go(part, part, qs_s(i), qs_r(i), place(wrap(x + 1 - 2 * d), wrap(y + k), z, c))

    for k in range(1, 8):

        @pl.when(s + k < 8)
        def _():
            kv[part_of(s + k, ROWS, 16)] = jnp.zeros((ROWS, 256), BF16)

        @pl.when(k <= s)
        def _():
            rkv[k - 1] = jnp.zeros((ROWS, 256), BF16)

    def block_rows(k):
        return part_of(4 * lax.div(z, 2) + wrap(y - k), WR, 16)

    gz_s, gz_r = net.pair(12)

    def block_along_z(k):
        part = wgu.at[matrix, block_rows(k)]
        for to in range(1, 4):
            net.go(part, part, gz_s(4 * to + k - 4), gz_r(4 * to + k - 4), along_z(to))

    net.landed(wgu.at[0, rows], gr(4), when=jnp.logical_not(sender))
    block_along_z(0)

    for k in range(1, 8):
        net.landed(wvo.at[rows, own_lanes], or_(k - 1))
    oz_s, oz_r = net.pair(3)
    for k in range(1, 4):
        part = wvo.at[:, own_lanes]
        net.go(part, part, oz_s(k - 1), oz_r(k - 1), along_z(k))

    tok = tokens[...].astype(F32)
    unit = tok * lax.rsqrt(jnp.mean(tok * tok, axis=-1, keepdims=True) + EPS)

    for k in range(1, 8):
        net.landed(misc.at[0], mr(k - 1))
    for k in range(8):
        gains[0:8, WR * k : WR * (k + 1)] = misc[k, 0:8, 0:WR]
    numbers = misc[:, 2, :]
    zeros = jnp.sum(jnp.where(numbers < 0.5, 1.0, 0.0), keepdims=True)
    ones = jnp.sum(jnp.where((numbers > 0.5) & (numbers < 1.5), 1.0, 0.0), keepdims=True)
    own_numbers = misc[s, 2:3, :]
    begin = jnp.where(own_numbers < 0.5, 0.0, jnp.where(own_numbers < 1.5, zeros, zeros + ones))
    lane = lax.broadcasted_iota(jnp.int32, (1, ROWS), 1) + s * ROWS
    angle = freq[...] * (lane.astype(F32) - begin)
    trig[0] = jnp.cos(angle)
    trig[1] = jnp.sin(angle)
    key_place = lax.broadcasted_iota(jnp.int32, (LENGTH, ROWS), 0)
    allowed = (key_place >= begin.astype(jnp.int32)) & (key_place <= lane)
    mask[...] = jnp.where(allowed, 0.0, -1e30)
    normed = (unit * gains[0:1, :]).astype(BF16)
    normed_t = jnp.transpose(normed)

    ef_s, ef_r = net.pair(7)
    for k in range(1, 8):
        part = wkv.at[c, part_of(lax.rem(s + 8 - k, 8), WR, 16)]
        net.landed(part, er(k - 1))
        net.go(part, part, ef_s(k - 1), ef_r(k - 1), core_peer)
    for k in range(1, 8):
        net.landed(wkv.at[c, rows], ef_r(k - 1))
    cosine, sine = trig[0], trig[1]

    def rotated(raw, at):
        first = raw[at : at + 32]
        second = raw[at + 32 : at + 64]
        return first * cosine - second * sine, second * cosine + first * sine

    raw_keys = jnp.transpose(dot(normed, wkv[0]))
    keys = jnp.concatenate([*rotated(raw_keys, 0), *rotated(raw_keys, HD)], axis=0)
    kv[own_rows, 0:128] = jnp.transpose(keys).astype(BF16)
    kv[own_rows, 128:256] = dot(normed, wkv[1]).astype(BF16)

    ks, kr = net.pair(7)
    for k in range(1, 8):
        net.go(kv.at[own_rows], kv.at[own_rows], ks(k - 1), kr(k - 1), of_sequence(k)[1], when=s + k < 8)

    is_far = jnp.where(sender, 0, 1)
    for k in range(1, 4):
        net.landed(wgu.at[0, rows], gr(4 * is_far + k))
        block_along_z(k)

    ds_, dr = net.sends(1), net.recvs(2)
    half = part_of(c, FH, 16)
    net.go(wd.at[half], wdv.at[half], ds_(0), dr(c), place(wrap(x + 1 - 2 * c), y, z, xl))

    def gather_tokens(which):
        ts, tr = net.pair(3)
        part = acts.at[which, own_tokens]
        for k in (1, 3, 2):
            net.go(part, part, ts(k - 1), tr(k - 1), place(x, wrap(y + k), z, c))
        return tr

    local[3].wait()
    cot_r = gather_tokens(1)

    qf_s, qf_r = net.pair(11)
    for i in range(11):
        if i < 3:
            part = wqk.at[part_of(xl * 4 + wrap(y - (i + 1)), WR, 16), core_half]
        else:
            k, d = divmod(i - 3, 2)
            part = wqk.at[part_of((1 - xl) * 4 + wrap(y - k), WR, 16), part_of(2 * c + d, 256, 128)]
        net.landed(part, qs_r(i))
        net.go(part, part, qf_s(i), qf_r(i), core_peer)

    for i in range(11):
        net.landed(wqk.at[rows, pl.ds(0, 512 if i < 3 else 256)], qf_r(i))
    raw = jnp.transpose(dot(normed, wqk[...]))
    for head in range(H):
        kv_head, j = divmod(head, GROUP)
        first, second = rotated(raw, HD * head + (128 if head > 5 else 0))
        qs[kv_head, 0:32, ROWS * j : ROWS * (j + 1)] = (first * SCALE).astype(BF16)
        qs[kv_head, 32:64, ROWS * j : ROWS * (j + 1)] = (second * SCALE).astype(BF16)

    for k in range(1, 8):
        net.landed(kv.at[own_rows], kr(k - 1), when=s - k >= 0)
    for head in range(KVH):
        keys = kv[:, HD * head : HD * (head + 1)]
        values = kv[:, 128 + HD * head : 128 + HD * (head + 1)]
        kc[head] = keys
        vc[head] = values
        kt[head] = jnp.transpose(keys)
        vt[head] = jnp.transpose(values)

    def attend(head, j, width):
        lanes = part_of(j, ROWS, 128) if width == 1 else pl.ds(pl.multiple_of(ROWS * j, 256), 2 * ROWS)
        raw_scores = dot(kc[head], qs[head, :, lanes])
        parts = []
        for i in range(width):
            scores = raw_scores[:, ROWS * i : ROWS * (i + 1)] + mask[...]
            highest = jnp.max(scores, axis=0, keepdims=True)
            weights = jnp.exp(scores - highest)
            total = jnp.sum(weights, axis=0, keepdims=True)
            parts.append((weights * (1.0 / total)).astype(BF16))
            lse[GROUP * head + j + i] = jnp.broadcast_to(highest + jnp.log(total), (8, ROWS))
        heads = dot(vt[head], jnp.concatenate(parts, axis=1) if width == 2 else parts[0])
        for i in range(width):
            mixt[part_of(GROUP * head + j + i, HD, HD)] = heads[:, ROWS * i : ROWS * (i + 1)]

    for p in range(GROUP // 2):
        for head in range(KVH):
            attend(head, 2 * p, 2)
    for head in range(KVH):
        attend(head, GROUP - 1, 1)

    of_s, of_r = net.pair(4)
    for k in range(4):
        part = wvo.at[:, part_of(4 * c + wrap(z - k), 128, 128)]
        if k:
            net.landed(part, oz_r(k - 1))
        net.go(part, part, of_s(k), of_r(k), core_peer)
    for k in range(4):
        net.landed(wvo.at[:, own_lanes], of_r(k))
    attended_t = mixt[...].astype(BF16)
    attended = jnp.transpose(mixt[...]).astype(BF16)
    middle = tokens[...].astype(F32) + jnp.concatenate(
        [dot(attended, wvo[:, 0:384]), dot(attended, wvo[:, 512:1024])], axis=1
    )
    mid[...] = middle
    factor = lax.rsqrt(jnp.mean(middle * middle, axis=-1, keepdims=True) + EPS)
    acts[0, own_tokens] = (middle * factor * gains[1:2, :]).astype(BF16)

    n2_r = gather_tokens(0)

    def forward(which, off, send, recv):
        part = acts.at[which, part_of(2 * wrap(y - off) + c, ROWS, 16)]
        return remote(part, part, send(off), recv(off), core_peer)

    nf_s, nf_r = net.pair(4)
    cf_s, cf_r = net.pair(4)
    forward(0, 0, nf_s, nf_r).start()
    for off in (0, 1, 3, 2):
        if off:
            net.landed(acts.at[1, own_tokens], cot_r(off - 1))
        forward(1, off, cf_s, cf_r).start()
    pl.when(c == xl)(own_down.wait)
    for i in range(2):
        net.landed(wdv.at[pl.ds(FH * i, FH)], dr(i), when=c != xl)
    for i in range(12):
        net.landed(wgu.at[0, rows], gz_r(i))

    xsend, xrecv = net.pair(4)
    psend, precv = net.sends(8), net.recvs(6)
    vsend, vrecv = net.pair(2)

    def offset(k):
        return k

    def exchange(off):
        block = part_of(off, 256, 256)
        return remote(pa.at[0, block], pa.at[1, block], xsend(off), xrecv(off), core_peer)

    def part_copy(slot, core):
        off = (0, 1, 3)[slot]
        return remote(
            pa.at[0, pl.ds(256 * off + ROWS * core, ROWS)], fr.at[c, slot], psend(2 * slot + core),
            precv(3 * c + slot), place(x, wrap(y - off), z, core),
        )

    def through(side):
        rows_of = pl.ds(512 + ROWS * side, ROWS)
        return remote(pa.at[0, rows_of], via.at[side], vsend(side), vrecv(side), place(x, wrap(y - 1 + 2 * side), z, c))

    def add_cores(off):
        exchange(off).wait()
        block = pl.ds(256 * off, 256)
        total = own[(0, 1, 0, 2)[off]] + pa[1, block].astype(F32)
        if off % 2:
            side = off // 2
            through(side).wait_recv()
            half_of = slice(ROWS * side, ROWS * (side + 1))
            other = slice(ROWS * (1 - side), ROWS * (2 - side))
            pa[0, pl.ds(256 * off + ROWS * (1 - side), ROWS)] = total[other].astype(BF16)
            pa[0, pl.ds(256 * off + ROWS * side, ROWS)] = (total[half_of] + via[side].astype(F32)).astype(BF16)
        else:
            pa[0, block] = total.astype(BF16)

    def to_owners(off):
        add_cores(off)
        for core in range(2):
            if off == 2:
                through(core).start()
            elif off:
                part_copy(off - off // 3, core).start()
            else:

                @pl.when(c == core)
                def _():
                    fr[core, 0] = pa[0, ROWS * core : ROWS * (core + 1)]

                pl.when(c != core)(part_copy(0, core).start)

    @pl.loop(0, 4)
    def _(k):
        net.landed(acts.at[0, own_tokens], nf_r(offset(k)))
        net.landed(acts.at[1, own_tokens], cf_r(offset(k)))
        off = offset(k)
        block = part_of(wrap(y - off), 256, 256)
        normed_two = acts[0, block]
        cotangent = acts[1, block]
        gate = dot(normed_two, wgu[0])
        up = dot(normed_two, wgu[1])
        grad_hidden = dot_nt(cotangent, wdv[...])
        opening = 1.0 / (1.0 + jnp.exp(-gate))
        act = gate * opening
        hidden = (act * up).astype(BF16)
        grad_gate = (grad_hidden * up * opening * (1.0 + gate * (1.0 - opening))).astype(BF16)
        grad_up = (grad_hidden * act).astype(BF16)
        gua[0, block] = grad_gate
        gua[1, block] = grad_up
        da[1, 0:FC, block] = jnp.transpose(hidden)
        da[0, :, block] = jnp.transpose(normed_two)

        @pl.when(k < 3)
        def _():
            after = offset(k + 1)
            net.landed(acts.at[0, own_tokens], n2_r(after - 1))
            forward(0, after, nf_s, nf_r).start()

        pl.when(k == 1)(lambda: to_owners(0))
        pl.when((k == 3) & (c == 1))(lambda: to_owners(2))

        out_part = dot(hidden, wdv[...])
        grad_part = dot_nt(grad_gate, wgu[0]) + dot_nt(grad_up, wgu[1])
        own[off - 2 * lax.div(off, 2) + lax.div(off, 3)] = jnp.where(c == 0, out_part, grad_part)
        pa[0, part_of(off, 256, 256)] = jnp.where(c == 0, grad_part, out_part).astype(BF16)
        exchange(off).start()

    for off in range(4):
        forward(0, off, nf_s, nf_r).wait_send()
        forward(1, off, cf_s, cf_r).wait_send()
    net.drain()
    pl.when(c == 0)(lambda: to_owners(2))

    def gradient(matrix_, store):
        shift = y + 2 * matrix_
        for h in range(2):
            tall = dot(da[0, 448 * h : 448 * (h + 1)], gua[matrix_]).astype(BF16)
            for k in range(4):
                store[h, wrap(k - shift)] = tall[WR * k : WR * (k + 1)]

    gradient(0, dgate)
    zs, zr = net.pair(3)
    for k in range(1, 4):
        net.go(dgate.at[:, wrap(z + k)], rz.at[k - 1], zs(k - 1), zr(k - 1), along_z(k))
    gradient(1, dup)
    us, ur = net.pair(3)
    for k in range(1, 4):
        part = dup.at[lax.rem(xl + k, 2), pl.ds(2 * lax.div(wrap(x + k), 2), 2)]
        net.go(part, ru.at[k - 1], us(k - 1), ur(k - 1), along_x(k))

    @pl.when(c == 1)
    def _():
        to_owners(1)
        to_owners(3)

    for h in range(2):
        tall = dot(da[1, FH * h : FH * (h + 1)], acts[1]).astype(BF16)
        for i in range(7):
            q = 7 * h + i
            dwd[q // 4, q % 4] = tall[:, 128 * i : 128 * (i + 1)]
    for q in (14, 15):
        dwd[q // 4, q % 4] = jnp.zeros((FH, 128), BF16)

    zds, zdr = net.pair(3)
    for k in range(1, 4):
        net.go(dwd.at[:, wrap(z + k)], rzd.at[k - 1], zds(k - 1), zdr(k - 1), along_z(k))

    own_cot[...] = acts[1, own_tokens]

    @pl.loop(0, GROUP)
    def _(j):
        lanes = part_of(j, ROWS, 128)
        for head in range(KVH):
            scores = dot(kc[head], qs[head, :, lanes]) + mask[...]
            acts[head, :, lanes] = jnp.exp(scores - lse[GROUP * head + j, 0:1, :]).astype(BF16)

    def landed_parts(kind):
        for slot in range(3):
            net.landed(fr.at[kind, slot], precv(3 * kind + slot), when=None if slot else c != kind)
        return fr[kind, 0].astype(F32) + fr[kind, 1].astype(F32) + fr[kind, 2].astype(F32)

    @pl.when(c == 0)
    def _():
        to_owners(1)
        to_owners(3)

    grad_normed = landed_parts(1)
    middle = mid[...]
    own[0, 0:ROWS] = middle
    factor = lax.rsqrt(jnp.mean(middle * middle, axis=-1, keepdims=True) + EPS)
    unit_two = middle * factor
    scaled = grad_normed * gains[1:2, :]
    gvec[...] = jnp.broadcast_to(jnp.sum(grad_normed * unit_two, axis=0, keepdims=True), (8, D))
    grad_middle = own_cot[...].astype(F32) + factor * (
        scaled - unit_two * jnp.mean(scaled * unit_two, axis=-1, keepdims=True)
    )
    mid[...] = grad_middle

    branch = grad_middle.astype(BF16)
    grad_mixed = jnp.transpose(
        dot_nt(branch[:, 0:384], wvo[:, 0:384]) + dot_nt(branch[:, 384:D], wvo[:, 512:1024])
    )
    for head in range(H):
        kv_head, j = divmod(head, GROUP)
        gmt[kv_head, :, ROWS * j : ROWS * (j + 1)] = grad_mixed[HD * head : HD * (head + 1)].astype(BF16)
    grad_out = dot(attended_t, branch).astype(BF16)
    da[1, :, 0:384] = grad_out[:, 0:384]
    da[1, :, 512:1024] = grad_out[:, 384:D]
    first_of_peer = pl.ds(pl.multiple_of(512 * (1 - c), 128), 384)
    last_of_peer = pl.ds(pl.multiple_of(512 * (1 - c) + 384, 128), 128)
    first_own = pl.ds(pl.multiple_of(512 * c, 128), 384)
    last_own = pl.ds(pl.multiple_of(512 * c + 384, 128), 128)
    firsts, lasts_ = pl.ds(0, 384), pl.ds(384, 128)
    xas, xar = net.pair(5)
    net.go(da.at[1, :, first_of_peer], xa.at[1, :, firsts], xas(1), xar(1), core_peer)
    net.go(da.at[1, :, last_of_peer], xa.at[1, :, lasts_], xas(3), xar(3), core_peer, when=c == 0)

    for slot in range(3):
        for core in range(2):
            if slot:
                part_copy(slot, core).wait_send()
            else:
                pl.when(c != core)(part_copy(slot, core).wait_send)
    for side in range(2):
        through(side).wait_send()

    def to_rows_owners(i, lanes, sems):
        for k in range(1, 4):
            other = part_of(xl * 4 + wrap(y + k), WR, 16)
            net.go(
                sa.at[i, other, lanes], rya.at[i, 0, k - 1, :, lanes], sems[0](k - 1), sems[1](k - 1),
                place(x, wrap(y + k), z, c),
            )

    def to_rows_owners_across(i, half_size, sems):
        for k in range(4):
            other = part_of((1 - xl) * 4 + wrap(y + k), WR, 16)
            for d, cut in enumerate(half_size):
                net.go(
                    sa.at[i, other, cut], rya.at[i, 1, k, :, cut], sems[0](3 + 2 * k + d), sems[1](3 + 2 * k + d),
                    place(wrap(x + 1 - 2 * d), wrap(y + k), z, c),
                )

    def from_rows_owners(i, lanes, half_size, sems):
        for k in range(1, 4):
            net.landed(rya.at[i, 0, k - 1, :, lanes], sems[1](k - 1))
        for k in range(4):
            for d, cut in enumerate(half_size):
                net.landed(rya.at[i, 1, k, :, cut], sems[1](3 + 2 * k + d))

    def last_tile(i, when):
        net.landed(xa.at[i, :, lasts_], xar(2 + i), when=when)

        @pl.when(when)
        def _():
            sa[i, :, 384:512] = (da[i, :, last_own].astype(F32) + xa[i, :, 384:512].astype(F32)).astype(BF16)

        for k in range(1, 8):
            far = k > 3
            other = (1 - xl if far else xl) * 4 + wrap(y + k)
            target = place(wrap(x + (1 - 2 * i if far else 0)), wrap(y + k), z, c)
            part = sa.at[i, part_of(other, WR, 16), lasts_]
            net.go(part, ryl.at[i, k - 1], yl[i][0](k - 1), yl[i][1](k - 1), target, when=when)

    first_cuts = ((pl.ds(0, 256), pl.ds(256, 128)), (pl.ds(0, 128), pl.ds(128, 256)))
    yf = [net.pair(11), net.pair(11)]
    yl = [net.pair(7), net.pair(7)]
    net.landed(xa.at[1, :, firsts], xar(1))
    sa[1, :, 0:384] = (da[1, :, first_own].astype(F32) + xa[1, :, 0:384].astype(F32)).astype(BF16)
    to_rows_owners(1, firsts, yf[1])


    for k in range(1, 4):
        net.landed(ru.at[k - 1], ur(k - 1))
    for i in range(2):
        su[i] = (
            dup[xl, 2 * xh + i].astype(F32) + ru[0, i].astype(F32) + ru[1, i].astype(F32) + ru[2, i].astype(F32)
        ).astype(BF16)
    vs, vr = net.sends(2), net.recvs(4)
    for i in range(2):
        target = 2 * xh + i
        net.go(su.at[i], ruz.at[z], vs(i), vr(z), place(x, y, target, c), when=z != target)
    for k in range(1, 4):
        net.landed(rz.at[k - 1], zr(k - 1))
    for i in range(2):
        sz[i] = (
            dgate[i, z].astype(F32) + rz[0, i].astype(F32) + rz[1, i].astype(F32) + rz[2, i].astype(F32)
        ).astype(BF16)
    xs_s, xs_r = net.pair(3)
    for k in range(1, 4):
        net.go(sz.at[lax.rem(xl + k, 2)], rx.at[k - 1], xs_s(k - 1), xs_r(k - 1), along_x(k))

    def attend_back(head, j, width):
        lanes = part_of(j, ROWS, 128) if width == 1 else pl.ds(pl.multiple_of(ROWS * j, 256), 2 * ROWS)
        probs = acts[head, :, lanes].astype(F32)
        grad_probs = dot(vc[head], gmt[head, :, lanes])
        delta = jnp.sum(grad_probs * probs, axis=0, keepdims=True)
        grad_scores = (probs * (grad_probs - delta)).astype(BF16)
        pa[head, :, lanes] = grad_scores
        both = dot(kt[head], grad_scores) * SCALE
        cosine, sine = trig[0], trig[1]
        for i in range(width):
            rot = both[:, ROWS * i : ROWS * (i + 1)]
            at = HD * (GROUP * head + j + i)
            mixt[pl.ds(pl.multiple_of(at, 32), 32)] = rot[0:32] * cosine + rot[32:64] * sine
            mixt[pl.ds(pl.multiple_of(at + 32, 32), 32)] = rot[32:64] * cosine - rot[0:32] * sine

    kvs, kvr = net.pair(14)
    for head in range(KVH):
        for p in range(GROUP // 2):
            attend_back(head, 2 * p, 2)
        attend_back(head, GROUP - 1, 1)
        dkv[:, 128 * head : 128 * head + HD] = dot_nt(pa[head], qs[head]).astype(BF16)
        dkv[:, 128 * head + HD : 128 * (head + 1)] = dot_nt(acts[head], gmt[head]).astype(BF16)
        for k in range(1, 8):
            other, target = of_sequence(k)
            lanes = pl.ds(128 * head, 128)
            i = 7 * head + k - 1
            net.go(
                dkv.at[part_of(other, ROWS, 16), lanes], rkv.at[k - 1, :, lanes], kvs(i), kvr(i), target, when=s + k >= 8
            )

    vout[...] = (own[0, 0:ROWS] + landed_parts(0)).astype(BF16)

    grad_query = jnp.transpose(mixt[...]).astype(BF16)
    gqk[:, 0:384] = grad_query[:, 0:384]
    gqk[:, 512:1024] = grad_query[:, 384:D]
    part = dot(normed_t, grad_query).astype(BF16)
    da[0, :, 0:384] = part[:, 0:384]
    da[0, :, 512:1024] = part[:, 384:D]
    net.go(da.at[0, :, first_of_peer], xa.at[0, :, firsts], xas(0), xar(0), core_peer)
    net.go(da.at[0, :, last_of_peer], xa.at[0, :, lasts_], xas(2), xar(2), core_peer, when=c == 0)

    for k in range(1, 4):
        net.landed(rx.at[k - 1], xs_r(k - 1))
    sgu[0] = (
        sz[xl].astype(F32) + rx[0].astype(F32) + rx[1].astype(F32) + rx[2].astype(F32)
    ).astype(BF16)
    own_block = 4 * c + y
    held = [4 * c + wrap(y - z), 4 * c + wrap(y - z - 2)]
    ags, agr = net.pair(4)
    net.go(sgu.at[0], agu.at[0, own_block], ags(0), agr(0), place(x, wrap(y + z), z, c), when=z != 0)

    @pl.when(z == 0)
    def _():
        agu[0, own_block] = sgu[0]

    cosine, sine = trig[0], trig[1]
    back, grad_values = [], []
    for head in range(KVH):
        lanes = slice(128 * head, 128 * (head + 1))
        total = dkv[own_rows, lanes].astype(F32)
        for k in range(1, 8):
            net.landed(rkv.at[k - 1, :, pl.ds(0, 128)], kvr(7 * head + k - 1), when=k > s)
            total = total + rkv[k - 1, :, lanes].astype(F32)
        keys = jnp.transpose(total)
        first, second = keys[0:32], keys[32:64]
        back += [first * cosine + second * sine, second * cosine - first * sine]
        grad_values.append(total[:, HD:128])
    grad_key = jnp.transpose(jnp.concatenate(back, axis=0)).astype(BF16)
    gqk[:, 384:512] = grad_key
    grad_value = jnp.concatenate(grad_values, axis=1).astype(BF16)
    da[0, :, 384:512] = dot(normed_t, grad_key).astype(BF16)
    da[1, :, 384:512] = dot(normed_t, grad_value).astype(BF16)
    for i in range(2):
        net.go(da.at[i, :, last_of_peer], xa.at[i, :, lasts_], xas(2 + i), xar(2 + i), core_peer, when=c == 1)

    net.landed(xa.at[0, :, firsts], xar(0))
    sa[0, :, 0:384] = (da[0, :, first_own].astype(F32) + xa[0, :, 0:384].astype(F32)).astype(BF16)
    to_rows_owners_across(1, first_cuts[1], yf[1])
    to_rows_owners(0, firsts, yf[0])
    to_rows_owners_across(0, first_cuts[0], yf[0])
    last_tile(1, c == 1)
    last_tile(0, c == 1)

    grad_normed = dot_nt(gqk[...], wqk[...]) + dot_nt(grad_value, wvo[:, 384:512])
    tok = tokens[...].astype(F32)
    factor = lax.rsqrt(jnp.mean(tok * tok, axis=-1, keepdims=True) + EPS)
    unit = tok * factor
    scaled = grad_normed * gains[0:1, :]
    vtok[...] = mid[...] + factor * (scaled - unit * jnp.mean(scaled * unit, axis=-1, keepdims=True))
    gvec[0:1, :] = jnp.sum(grad_normed * unit, axis=0, keepdims=True)
    for row in range(2):
        for i in range(7):
            gpack[7 * row + i : 7 * row + i + 1, :] = gvec[row : row + 1, 128 * i : 128 * (i + 1)]
    net.go(gpack, gx, xas(4), xar(4), core_peer)

    for i in range(2):
        last_tile(i, c == 0)
    net.landed(gx, xar(4))
    gsum[...] = gpack[...] + gx[...]
    gys, gyr = net.pair(7)
    for k in range(1, 8):
        net.go(gsum, gy.at[k - 1], gys(k - 1), gyr(k - 1), of_sequence(k)[1])

    owner = xh == lax.div(z, 2)
    for k in range(4):
        net.landed(su.at[0], vr(k), when=owner & (z != k))
    ucs, ucr = net.pair(1)
    uhs = net.sends(1)

    @pl.when(owner)
    def _():
        ruz[z] = su[lax.rem(z, 2)]
        sgu[1] = (
            ruz[0].astype(F32) + ruz[1].astype(F32) + ruz[2].astype(F32) + ruz[3].astype(F32)
        ).astype(BF16)

    net.go(sgu.at[1], agu.at[1, own_block], ucs(0), ucr(0), place(x, wrap(y + z + 2), z, c), when=owner & (z != 2))
    net.go(sgu.at[1], agu.at[1, own_block], uhs(0), ucr(0), place(wrap(x + 2), wrap(y + z + 2), z, c), when=owner)

    @pl.when(owner & (z == 2))
    def _():
        agu[1, own_block] = sgu[1]

    for k in range(1, 4):
        net.landed(rzd.at[k - 1], zdr(k - 1))
    for i in range(4):
        sdz[i] = (
            dwd[i, z].astype(F32) + rzd[0, i].astype(F32) + rzd[1, i].astype(F32) + rzd[2, i].astype(F32)
        ).astype(BF16)
    xds, xdr = net.pair(3)
    for k in range(1, 4):
        net.go(sdz, rxd.at[k - 1], xds(k - 1), xdr(k - 1), along_x(k), when=lax.rem(xl + k, 2) == c)


    afs, afr = net.pair(8)

    def spread(matrix_, sends, recvs):
        for k in range(1, 4):
            net.go(agu.at[matrix_, held[matrix_]], agu.at[matrix_, held[matrix_]], sends(k), recvs(k), along_z(k))
        part = agu.at[matrix_, held[matrix_]]
        net.go(part, part, afs(4 * matrix_), afr(4 * matrix_), core_peer)

    net.landed(agu.at[0, held[0]], agr(0), when=z != 0)
    spread(0, ags, agr)

    zas2, zar2 = net.pair(6)
    for i in range(2):
        from_rows_owners(i, firsts, first_cuts[i], yf[i])
        total = sa[i, rows, 0:384].astype(F32)
        for k in range(3):
            total = total + rya[i, 0, k, :, 0:384].astype(F32)
        for k in range(4):
            total = total + rya[i, 1, k, :, 0:384].astype(F32)
        ta[i, :, 0:384] = total.astype(BF16)
        total = sa[i, rows, 384:512].astype(F32)
        for k in range(1, 8):
            net.landed(ryl.at[i, k - 1], yl[i][1](k - 1))
            total = total + ryl[i, k - 1].astype(F32)
        ta[i, :, 384:512] = total.astype(BF16)
    for k in range(1, 4):
        net.go(ta.at[:, :, part_of(wrap(z + k), 128, 128)], rza.at[k - 1], zas2(k - 1), zar2(k - 1), along_z(k))
    total = gsum[...]
    for k in range(1, 8):
        net.landed(gy.at[k - 1], gyr(k - 1))
        total = total + gy[k - 1]
    gz[3] = total
    for k in range(1, 4):
        net.go(gz.at[3], gz.at[k - 1], zas2(k + 2), zar2(k + 2), along_z(k))

    for k in range(1, 4):
        net.landed(rxd.at[k - 1], xdr(k - 1), when=xl == c)
    zas, zar = net.pair(3)

    @pl.when(xl == c)
    def _():
        for i in range(4):
            agd[i, z] = (
                sdz[i].astype(F32) + rxd[0, i].astype(F32) + rxd[1, i].astype(F32) + rxd[2, i].astype(F32)
            ).astype(BF16)

    for k in range(1, 4):
        net.go(agd.at[:, z], agd.at[:, z], zas(k - 1), zar(k - 1), along_z(k), when=xl == c)

    uas, uar = net.pair(4)
    net.landed(agu.at[1, held[1]], ucr(0), when=jnp.logical_not(owner) | (z != 2))
    spread(1, uas, uar)

    for k in range(1, 4):
        net.landed(rza.at[k - 1], zar2(k - 1))
    tile[...] = (
        ta[:, :, part_of(z, 128, 128)].astype(F32)
        + rza[0].astype(F32) + rza[1].astype(F32) + rza[2].astype(F32)
    ).astype(BF16)
    total = gz[3]
    for k in range(1, 4):
        net.landed(gz.at[k - 1], zar2(k + 2))
        total = total + gz[k - 1]
    gh[1] = total
    hs, hr = net.pair(2)
    net.go(tile, rh, hs(0), hr(0), along_x(2))
    net.go(gh.at[1], gh.at[0], hs(1), hr(1), along_x(2))

    net.landed(rh, hr(0))
    own_tile = aout.at[:, :, own_lanes]
    aout[:, :, own_lanes] = (tile[...].astype(F32) + rh[...].astype(F32)).astype(BF16)
    lasts, lastr = net.pair(3)
    for k in range(1, 4):
        net.go(own_tile, own_tile, lasts(k - 1), lastr(k - 1), along_z(k))
    net.landed(gh.at[0], hr(1))
    gpack_sum = gh[0] + gh[1]
    gain_o[...] = jnp.zeros_like(gain_o)
    for row in range(2):
        for i in range(7):
            gain_o[row : row + 1, 128 * i : 128 * (i + 1)] = gpack_sum[7 * row + i : 7 * row + i + 1]

    net.drain()

    outs = [
        pltpu.make_async_copy(aout, attn_o, lsem.at[9]),
    ]

    def to_other_core(matrix_, recvs):
        for k in (1, 3, 2):
            part = agu.at[matrix_, 4 * c + wrap(y - wrap(z - k) - 2 * matrix_)]
            net.landed(part, recvs(k))
            net.go(part, part, afs(4 * matrix_ + k), afr(4 * matrix_ + k), core_peer)

    def assemble(matrix_):
        for k in range(4):
            net.landed(agu.at[matrix_, 0], afr(4 * matrix_ + k))
        for k in range(8):
            wide[matrix_, :, FC * k : FC * (k + 1)] = agu[matrix_, k]

    to_other_core(0, agr)
    assemble(0)
    for k in range(1, 4):
        net.landed(agd.at[:, z], zar(k - 1), when=xl == c)
    dfs, dfr = net.pair(1)
    net.go(agd, fin, dfs(0), dfr(0), core_peer, when=xl == c)
    own_sums = pltpu.make_async_copy(agd, d_o, lsem.at[8])
    pl.when(xl == c)(own_sums.start)
    for k in range(1, 4):
        net.landed(own_tile, lastr(k - 1))
    fs, fr_ = net.pair(1)
    part = aout.at[:, :, core_half]
    net.go(part, part, fs(0), fr_(0), core_peer)
    to_other_core(1, uar)
    net.landed(fin, dfr(0), when=xl != c)
    peer_sums = pltpu.make_async_copy(fin, d_o, lsem.at[8])
    pl.when(xl != c)(peer_sums.start)
    net.landed(aout.at[:, :, pl.ds(0, 512)], fr_(0))
    outs[0].start()
    assemble(1)

    net.drain()
    for copy in outs:
        copy.wait()
    pl.when(xl == c)(own_sums.wait)
    pl.when(xl != c)(peer_sums.wait)


def finish_kernel(
    gain, vout, vtok, attn, wide, down,
    one, two, out, tok, gq, gk, gv, go, gate, up, gdown,
    fq, fk, fv, fo, fgate, fup, fdown, osem,
):
    outs = []

    def store(source, target):
        copy = pltpu.make_async_copy(source, target, osem.at[len(outs)])
        copy.start()
        outs.append(copy)

    store(vtok, tok)
    store(vout, out)
    fgate[...] = wide[0].astype(F32)
    store(fgate, gate)
    fup[...] = wide[1].astype(F32)
    store(fup, up)
    for q in range(14):
        h, i = divmod(q, 7)
        fdown[FH * h : FH * (h + 1), 128 * i : 128 * (i + 1)] = down[q // 4, q % 4].astype(F32)
    store(fdown, gdown)
    fq[:, 0:384] = attn[0, :, 0:384].astype(F32)
    fq[:, 384:D] = attn[0, :, 512:1024].astype(F32)
    store(fq, gq)
    fo[:, 0:384] = attn[1, :, 0:384].astype(F32)
    fo[:, 384:D] = attn[1, :, 512:1024].astype(F32)
    store(fo, go)
    fk[...] = attn[0, :, 384:512].astype(F32)
    store(fk, gk)
    fv[...] = attn[1, :, 384:512].astype(F32)
    store(fv, gv)
    shard = lax.axis_index("shard")
    for k in range(8):

        @pl.when(shard == k)
        def _():
            one[...] = gain[0:1, WR * k : WR * (k + 1)]
            two[...] = gain[1:2, WR * k : WR * (k + 1)]

    for copy in outs:
        copy.wait()


def vmem():
    return pl.BlockSpec(memory_space=pltpu.VMEM)


def anywhere():
    return pl.BlockSpec(memory_space=pl.ANY)


def shape(dims, dtype):
    return jax.ShapeDtypeStruct(dims, dtype)


def body(
    tokens, segments, attn_gain, w_query, w_key, w_value, w_out, ffn_gain, w_gate, w_up, w_down, cotangent
):
    half = HD // 2
    frequency = THETA ** (-(np.arange(half) * 2.0 / HD))
    freq = np.broadcast_to(frequency[:, None], (half, ROWS)).astype(np.float32)
    layer = pl.pallas_call(
        layer_kernel,
        name="layer",
        out_shape=[
            pltpu.VMEM((8, D), F32),
            pltpu.VMEM((ROWS, D), BF16),
            pltpu.VMEM((ROWS, D), F32),
            pltpu.VMEM((2, WR, 1024), BF16),
            pltpu.VMEM((2, WR, FF), BF16),
            pltpu.VMEM((4, 4, FH, 128), BF16),
        ],
        in_specs=[vmem()] * 5 + [anywhere()] * 8,
        out_specs=[vmem()] * 3 + [anywhere(), vmem(), anywhere()],
        scratch_shapes=[
            pltpu.VMEM((8, 8, 128), F32),
            pltpu.VMEM((D, 1024), BF16),
            pltpu.VMEM((D, 1024), BF16),
            pltpu.VMEM((2, D, 128), BF16),
            pltpu.VMEM((4, WR, FC), BF16),
            pltpu.VMEM((2, D, FC), BF16),
            pltpu.VMEM((FC, D), BF16),
            pltpu.VMEM((2, LENGTH, D), BF16),
            pltpu.VMEM((2, D, LENGTH), BF16),
            pltpu.VMEM((LENGTH, 256), BF16),
            pltpu.VMEM((KVH, LENGTH, HD), BF16),
            pltpu.VMEM((KVH, LENGTH, HD), BF16),
            pltpu.VMEM((KVH, HD, LENGTH), BF16),
            pltpu.VMEM((KVH, HD, LENGTH), BF16),
            pltpu.VMEM((KVH, HD, D), BF16),
            pltpu.VMEM((LENGTH, ROWS), F32),
            pltpu.VMEM((D, ROWS), F32),
            pltpu.VMEM((ROWS, D), F32),
            pltpu.VMEM((8, D), F32),
            pltpu.VMEM((2, half, ROWS), F32),
            pltpu.VMEM((H, 8, ROWS), F32),
            pltpu.VMEM((2, LENGTH, FC), BF16),
            pltpu.VMEM((3, 256, D), F32),
            pltpu.VMEM((2, LENGTH, D), BF16),
            pltpu.VMEM((2, 3, ROWS, D), BF16),
            pltpu.VMEM((2, ROWS, D), BF16),
            pltpu.VMEM((2, 4, WR, FC), BF16),
            pltpu.VMEM((2, 4, WR, FC), BF16),
            pltpu.VMEM((4, 4, FH, 128), BF16),
            pltpu.VMEM((KVH, HD, D), BF16),
            pltpu.VMEM((ROWS, D), BF16),
            pltpu.VMEM((LENGTH, 256), BF16),
            pltpu.VMEM((7, ROWS, 256), BF16),
            pltpu.VMEM((ROWS, 1024), BF16),
            pltpu.VMEM((3, 2, WR, FC), BF16),
            pltpu.VMEM((2, WR, FC), BF16),
            pltpu.VMEM((3, WR, FC), BF16),
            pltpu.VMEM((3, 2, WR, FC), BF16),
            pltpu.VMEM((2, WR, FC), BF16),
            pltpu.VMEM((4, WR, FC), BF16),
            pltpu.VMEM((2, WR, FC), BF16),
            pltpu.VMEM((2, 8, WR, FC), BF16),
            pltpu.VMEM((3, 4, FH, 128), BF16),
            pltpu.VMEM((4, FH, 128), BF16),
            pltpu.VMEM((3, 4, FH, 128), BF16),
            pltpu.VMEM((4, 4, FH, 128), BF16),
            pltpu.VMEM((4, 4, FH, 128), BF16),
            pltpu.VMEM((2, D, 512), BF16),
            pltpu.VMEM((2, D, 512), BF16),
            pltpu.VMEM((2, 2, 4, WR, 384), BF16),
            pltpu.VMEM((2, 7, WR, 128), BF16),
            pltpu.VMEM((2, WR, 512), BF16),
            pltpu.VMEM((3, 2, WR, 128), BF16),
            pltpu.VMEM((2, WR, 128), BF16),
            pltpu.VMEM((2, WR, 128), BF16),
            pltpu.VMEM((2, WR, 1024), BF16),
            pltpu.VMEM((8, D), F32),
            pltpu.VMEM((16, 128), F32),
            pltpu.VMEM((16, 128), F32),
            pltpu.VMEM((16, 128), F32),
            pltpu.VMEM((7, 16, 128), F32),
            pltpu.VMEM((4, 16, 128), F32),
            pltpu.VMEM((2, 16, 128), F32),
            pltpu.SemaphoreType.DMA((SENDS,)),
            pltpu.SemaphoreType.DMA((RECVS,)),
            pltpu.SemaphoreType.DMA((LOCALS,)),
        ],
        compiler_params=pltpu.CompilerParams(
            collective_id=0, has_side_effects=True, vmem_limit_bytes=58 << 20
        ),
    )
    results = layer(
        tokens,
        segments.reshape(1, ROWS),
        attn_gain.reshape(1, WR),
        ffn_gain.reshape(1, WR),
        freq,
        cotangent,
        w_query,
        w_key,
        w_value,
        w_out,
        w_gate,
        w_up,
        w_down,
    )
    finish = pl.pallas_call(
        finish_kernel,
        name="finish",
        out_shape=[
            shape((1, WR), F32),
            shape((1, WR), F32),
            shape((ROWS, D), BF16),
            shape((ROWS, D), F32),
            shape((WR, D), F32),
            shape((WR, 128), F32),
            shape((WR, 128), F32),
            shape((WR, D), F32),
            shape((WR, FF), F32),
            shape((WR, FF), F32),
            shape((FC, D), F32),
        ],
        in_specs=[vmem()] * 6,
        out_specs=[vmem()] * 2 + [anywhere()] * 9,
        scratch_shapes=[
            pltpu.VMEM((WR, D), F32),
            pltpu.VMEM((WR, 128), F32),
            pltpu.VMEM((WR, 128), F32),
            pltpu.VMEM((WR, D), F32),
            pltpu.VMEM((WR, FF), F32),
            pltpu.VMEM((WR, FF), F32),
            pltpu.VMEM((FC, D), F32),
            pltpu.SemaphoreType.DMA((9,)),
        ],
        compiler_params=pltpu.CompilerParams(vmem_limit_bytes=28 << 20),
    )
    one, two, out, tok, gq, gk, gv, go, gate, up, down = finish(*results)
    return out, tok, one.reshape(WR), gq, gk, gv, go, two.reshape(WR), gate, up, down


def solution(mesh):
    tokens = P(("replica", "shard"), None)
    weight = P("shard", None)
    return jax.shard_map(
        body,
        mesh=mesh,
        in_specs=(
            tokens, P(("replica", "shard")), P("shard"), weight, weight, weight, weight,
            P("shard"), weight, weight, weight, tokens,
        ),
        out_specs=(
            tokens, tokens, P("shard"), weight, weight, weight, weight, P("shard"), weight, weight, weight,
        ),
        check_vma=False,
    )
```
